32 devices in a mesh: ctx: 8 (over z, x), head: 4 (over y, core).
Axes of the slice: x: 2, y: 2, z: 4, core: 2. Of those that a mesh axis runs over, the one named last changes fastest.
Arguments:
- queries: bfloat16 [2048, 2048], P('ctx', 'head'), may hold values from -32 to 32
- key_heads: bfloat16 [2048, 2048], P('ctx', 'head'), may hold values from -32 to 32
- value_heads: bfloat16 [2048, 2048], P('ctx', 'head'), may hold values from -6 to 6
- out_weight: bfloat16 [4096, 2048], P('ctx', 'head'), may hold values from -0.5 to 0.5
- block_lists: int32 [16, 3], replicated, may hold values from 0 to 15, as said below
- out_grad: bfloat16 [2048, 4096], P('ctx', 'head'), may hold values from -6 to 6
Outputs:
- attended: bfloat16 [2048, 4096], P('ctx', 'head')
- query_grad: bfloat16 [2048, 2048], P('ctx', 'head')
- key_grad: bfloat16 [2048, 2048], P('ctx', 'head')
- value_grad: bfloat16 [2048, 2048], P('ctx', 'head')
- weight_grad: float32 [4096, 2048], P('ctx', 'head')
The draws below stay inside these ranges and needn't reach their ends.
Inputs may be any that keep to these rules, and one draw needn't show every extreme that they name: `block_lists`: every entry of row b lies within 4 blocks of b, and the first entry of each row lies exactly 4 blocks away from b.
All inputs are finite; a program needn't handle non-finite values.
Results may differ from the reference program's by a relative error of at most 0.028.
Values may be sent and summed in bfloat16 or wider, within the bound.
No kernel may reach another device: no remote copies, remote signals or barrier semaphores. Data moves between devices by JAX's collectives and lax.ppermute only.
A program may use at most 128 MiB of HBM per device.

```python
import jax
import jax.numpy as jnp
from jax import lax

D = 4096
HEADS = 16
HD = 128
BLK = 128
RANDS = 3
NQB = 16
TOKENS = 2048
REACH = 4


def draw_queries(key, part):
    drawn = jnp.clip(jax.random.normal(jax.random.fold_in(key, 11), (TOKENS, HEADS * HD), jnp.float32), -4.0, 4.0)
    return drawn.astype(jnp.bfloat16)


def draw_key_heads(key, part):
    drawn = jnp.clip(jax.random.normal(jax.random.fold_in(key, 21), (TOKENS, HEADS * HD), jnp.float32), -4.0, 4.0)
    return drawn.astype(jnp.bfloat16)


def draw_block_lists(key, part):
    rows = jnp.arange(NQB, dtype=jnp.int32)[:, None]
    offsets = jax.random.randint(jax.random.fold_in(key, 31), (NQB, RANDS), -REACH, REACH + 1)
    signs = jax.random.randint(jax.random.fold_in(key, 32), (NQB, 1), 0, 2) * 2 - 1
    offsets = jnp.concatenate([signs * REACH, offsets[:, 1:]], axis=1).astype(jnp.int32)
    picks = rows + offsets
    return jnp.where((picks < 0) | (picks >= NQB), rows - offsets, picks).astype(jnp.int32)


def with_spikes(result, rng, source, target, shards_of, factor):
    def block_of(dim):
        return (jnp.arange(result.shape[dim]) // (result.shape[dim] // shards_of)).reshape((-1,) + (1,) * (result.ndim - 1 - dim))

    one_side = jax.random.permutation(rng, shards_of)[block_of(target)]
    second = (block_of(target) + shards_of // 2) % shards_of
    return jnp.where((block_of(source) == one_side) | (block_of(source) == second), factor * result, result)


def steps_of(own_key, extent, cuts, low, largest):
    factor_of = 1.0
    for axis_at, blocks in cuts:
        steps = jax.random.uniform(jax.random.fold_in(jax.random.fold_in(own_key, 6), axis_at), (blocks,), jnp.float32, low / len(cuts), largest / len(cuts))
        factor_of = factor_of * jnp.repeat(jnp.exp(steps), extent[axis_at] // blocks).reshape((-1,) + (1,) * (len(extent) - 1 - axis_at))
    return factor_of


def centred(stream_key, shape, scale, reach, shards=(), kind=jnp.bfloat16):
    drawn = jax.random.normal(stream_key, shape, jnp.float32) * scale
    if len(shards) > 0:
        drawn = steps_of(stream_key, shape, shards, -0.22, 0.18) * drawn
    return jnp.clip(drawn, min=-reach, max=reach).astype(kind)


def gaussian_with(key, extent, scale, limit, split, heavy, kind=jnp.bfloat16):
    drawn = scale * jax.random.normal(key, extent, jnp.float32)
    if split:
        drawn = drawn * steps_of(key, extent, split, -0.22, 0.18)
    return jnp.clip(with_spikes(drawn, jax.random.fold_in(key, 3), *heavy), -limit, limit).astype(kind)


def setup_inputs(seed: int = 0) -> dict:
    streams_of = jax.random.split(jax.random.key(seed), 7)
    queries = draw_queries(jax.random.fold_in(streams_of[6], 71), 0)
    key_heads = draw_key_heads(jax.random.fold_in(streams_of[6], 71), 0)
    value_heads = centred(streams_of[2], (TOKENS, HEADS * HD), 1.0, 6.0, ((0, 8), (1, 4)))
    out_weight = centred(streams_of[3], (D, HEADS * HD), HD ** -0.5, 0.5, ((0, 8), (1, 4)))
    block_lists = draw_block_lists(jax.random.fold_in(streams_of[6], 71), 0)
    out_grad = gaussian_with(streams_of[5], (TOKENS, D), 1.0, 6.0, ((0, 8), (1, 4)), (0, 1, 8, 2.0))
    return {"queries": queries, "key_heads": key_heads, "value_heads": value_heads, "out_weight": out_weight, "block_lists": block_lists, "out_grad": out_grad}


def block_table(block_lists):
    total_blocks = block_lists.shape[0]
    rows = jnp.arange(total_blocks, dtype=jnp.int32)[:, None]
    table = jnp.concatenate([jnp.zeros_like(rows), rows - 1, rows, rows + 1, block_lists.astype(jnp.int32)], axis=1)
    width = table.shape[1]
    earlier = jnp.arange(width)[None, :] < jnp.arange(width)[:, None]
    repeated = jnp.any((table[:, :, None] == table[:, None, :]) & earlier[None], axis=2)
    fresh = (table >= 0) & (table < total_blocks) & jnp.logical_not(repeated)
    return jnp.clip(table, 0, total_blocks - 1).astype(jnp.int32), fresh


def block_probs(query_block, key_block, fresh_row, scale):
    scores = jnp.einsum("qhd,khd->hqk", query_block.astype(jnp.float32), key_block.astype(jnp.float32)) * scale
    keep = jnp.repeat(fresh_row, BLK)
    scores = jnp.where(keep[None, None, :], scores, -jnp.inf)
    row_top = jnp.max(scores, axis=2, keepdims=True)
    expo = jnp.exp(scores - row_top)
    return expo / jnp.sum(expo, axis=2, keepdims=True)


def reference(queries, key_heads, value_heads, out_weight, block_lists, out_grad):
    scale = HD ** -0.5
    total_blocks = block_lists.shape[0]
    table, fresh = block_table(block_lists)
    query_blocks = queries.reshape(total_blocks, BLK, HEADS, HD)
    key_blocks = key_heads.reshape(total_blocks, BLK, HEADS, HD)
    value_blocks = value_heads.reshape(total_blocks, BLK, HEADS, HD)
    indices = jnp.arange(total_blocks, dtype=jnp.int32)

    def forward_block(index):
        picks = table[index]
        probs = block_probs(query_blocks[index], key_blocks[picks].reshape(-1, HEADS, HD), fresh[index], scale)
        low = lax.optimization_barrier(probs.astype(jnp.bfloat16)).astype(jnp.float32)
        values_here = value_blocks[picks].reshape(-1, HEADS, HD).astype(jnp.float32)
        return jnp.einsum("hqk,khd->qhd", low, values_here).astype(jnp.bfloat16)

    mixed = lax.map(forward_block, indices).reshape(-1, HEADS * HD)
    attended = jnp.dot(mixed, out_weight.T, preferred_element_type=jnp.float32).astype(jnp.bfloat16)
    mixed_grad = jnp.dot(out_grad, out_weight, preferred_element_type=jnp.float32).astype(jnp.bfloat16)
    weight_grad = jnp.dot(out_grad.T, mixed, preferred_element_type=jnp.float32)
    delta = jnp.sum(mixed_grad.astype(jnp.float32).reshape(-1, HEADS, HD) * mixed.astype(jnp.float32).reshape(-1, HEADS, HD), axis=2)
    delta_blocks = delta.reshape(total_blocks, BLK, HEADS)
    grad_blocks = mixed_grad.reshape(total_blocks, BLK, HEADS, HD)

    def backward_block(carry, index):
        key_acc, value_acc = carry
        picks = table[index]
        keys_here = key_blocks[picks].reshape(-1, HEADS, HD).astype(jnp.float32)
        values_here = value_blocks[picks].reshape(-1, HEADS, HD).astype(jnp.float32)
        probs = block_probs(query_blocks[index], keys_here, fresh[index], scale)
        low = lax.optimization_barrier(probs.astype(jnp.bfloat16)).astype(jnp.float32)
        grad_here = grad_blocks[index].astype(jnp.float32)
        dots = jnp.einsum("qhd,khd->hqk", grad_here, values_here)
        slopes = probs * (dots - delta_blocks[index].T[:, :, None])
        slopes = lax.optimization_barrier(slopes.astype(jnp.bfloat16)).astype(jnp.float32)
        query_here = query_blocks[index].astype(jnp.float32)
        query_grad = (jnp.einsum("hqk,khd->qhd", slopes, keys_here) * scale).astype(jnp.bfloat16)
        key_part = jnp.einsum("hqk,qhd->khd", slopes, query_here).reshape(-1, BLK, HEADS, HD)
        value_part = jnp.einsum("hqk,qhd->khd", low, grad_here).reshape(-1, BLK, HEADS, HD)
        key_acc = key_acc.at[picks].add(key_part)
        value_acc = value_acc.at[picks].add(value_part)
        return (key_acc, value_acc), query_grad

    zeros = jnp.zeros((total_blocks, BLK, HEADS, HD), jnp.float32)
    (key_acc, value_acc), query_grad = lax.scan(backward_block, (zeros, zeros), indices)
    key_grad = (key_acc * scale).reshape(-1, HEADS * HD).astype(jnp.bfloat16)
    value_grad = value_acc.reshape(-1, HEADS * HD).astype(jnp.bfloat16)
    query_grad = query_grad.reshape(-1, HEADS * HD)
    return attended, query_grad, key_grad, value_grad, weight_grad
```

```python
import functools

import jax
import jax.numpy as jnp
from jax import lax
from jax.experimental import pallas as pl
from jax.experimental.pallas import tpu as pltpu
from jax.sharding import PartitionSpec as P

HD = 128
BLK = 128
REACH = 4

NT = (((1,), (1,)), ((), ()))
TN = (((0,), (0,)), ((), ()))
NN = (((1,), (0,)), ((), ()))


def mm(a, b, dims):
    return lax.dot_general(a, b, dims, preferred_element_type=jnp.float32)


def shifted(x, by):
    peers = lax.axis_size("ctx")
    return lax.ppermute(x, "ctx", [(i, i + by) for i in range(peers) if 0 <= i + by < peers])


def tree_strides(peers):
    strides = []
    stride = 1
    while stride < peers:
        strides.append(stride)
        stride *= 2
    return strides


def from_first(x):
    peers = lax.axis_size("ctx")
    me = lax.axis_index("ctx")
    for stride in reversed(tree_strides(peers)):
        pairs = [(i, i + stride) for i in range(0, peers, 2 * stride) if i + stride < peers]
        got = lax.ppermute(x, "ctx", pairs)
        x = jnp.where(me % (2 * stride) == stride, got, x)
    return x


def to_first(x):
    peers = lax.axis_size("ctx")
    for stride in tree_strides(peers):
        pairs = [(i + stride, i) for i in range(0, peers, 2 * stride) if i + stride < peers]
        x = x + lax.ppermute(x.astype(jnp.bfloat16), "ctx", pairs).astype(x.dtype)
    return x


def block_bias(lists_ref, run, per_dev, total_blocks, offset, i, j):
    row = run * per_dev + i
    key = (run + offset) * per_dev + j
    hit = (key - row <= 1) & (row - key <= 1)
    for n in range(lists_ref.shape[1]):
        hit = hit | (lists_ref[row, n] == key)
    hit = hit & (key >= 1) & (key < total_blocks)
    return jnp.where(hit, 0.0, -jnp.inf).astype(jnp.float32)


def fwd_kernel(offsets, per_dev, scale, run_ref, lists_ref, q_ref, k_ref, v_ref, *rest):
    bands = rest[: len(offsets)]
    first_ref, mixed_ref, lse_ref, s_ref = rest[len(offsets) :]
    total_blocks = lists_ref.shape[0]
    run = run_ref[0]
    q = q_ref[...]
    tokens = q.shape[0]

    def key_of(p):
        return k_ref[...] if p == 0 else bands[p - 1][0]

    def value_of(p):
        return v_ref[...] if p == 0 else bands[p - 1][1]

    places = (0,) + offsets
    top = None
    for p, offset in enumerate(places):
        s = mm(key_of(p), q, NT) * scale
        for j in range(per_dev):
            for i in range(per_dev):
                part = s[j * BLK : (j + 1) * BLK, i * BLK : (i + 1) * BLK]
                part = part + block_bias(lists_ref, run, per_dev, total_blocks, offset, i, j)
                s_ref[p * tokens + j * BLK : p * tokens + (j + 1) * BLK, i * BLK : (i + 1) * BLK] = part
    s_ref[len(places) * tokens :, :] = mm(first_ref[0], q, NT) * scale
    s = s_ref[...]
    top = jnp.max(s, axis=0, keepdims=True)
    e = jnp.exp(s - top)
    total = jnp.sum(e, axis=0, keepdims=True)
    inverse = 1.0 / total
    low = (e * inverse).astype(jnp.bfloat16)
    out = mm(first_ref[1], low[len(places) * tokens :], TN)
    for p in range(len(places)):
        out = out + mm(value_of(p), low[p * tokens : (p + 1) * tokens], TN)
    mixed_ref[...] = out.T.astype(jnp.bfloat16)
    lse_ref[0] = top + jnp.log(total)


def bwd_kernel(offsets, per_dev, scale, run_ref, lists_ref, q_ref, k_ref, v_ref, *rest):
    bands = rest[: len(offsets)]
    first_ref, mixed_ref, grad_ref, lse_ref = rest[len(offsets) : len(offsets) + 4]
    outs = rest[len(offsets) + 4 :]
    dq_ref, own_ref = outs[:2]
    band_outs = outs[2 : 2 + len(offsets)]
    dfirst_ref, s_ref = outs[2 + len(offsets) :]
    total_blocks = lists_ref.shape[0]
    run = run_ref[0]
    q = q_ref[...]
    tokens = q.shape[0]
    grad = grad_ref[...]
    lse = lse_ref[0]
    product = grad.astype(jnp.float32) * mixed_ref[...].astype(jnp.float32)
    delta = jnp.sum(product.T, axis=0, keepdims=True)

    def piece(key, value, offset):
        s = mm(key, q, NT) * scale
        if offset is None:
            p = jnp.exp(s - lse)
        else:
            for j in range(per_dev):
                for i in range(per_dev):
                    part = s[j * BLK : (j + 1) * BLK, i * BLK : (i + 1) * BLK]
                    part = part + block_bias(lists_ref, run, per_dev, total_blocks, offset, i, j)
                    s_ref[j * BLK : (j + 1) * BLK, i * BLK : (i + 1) * BLK] = part
            p = jnp.exp(s_ref[...] - lse)
        slopes = (p * (mm(value, grad, NT) - delta)).astype(jnp.bfloat16)
        dk = mm(slopes, q, NN)
        dv = mm(p.astype(jnp.bfloat16), grad, NN)
        return dk, dv, mm(key, slopes, TN)

    dk, dv, dq = piece(first_ref[0], first_ref[1], None)
    dfirst_ref[0] = dk
    dfirst_ref[1] = dv
    for n, offset in enumerate(offsets):
        dk, dv, more = piece(bands[n][0], bands[n][1], offset)
        band_outs[n][0] = dk.astype(jnp.bfloat16)
        band_outs[n][1] = dv.astype(jnp.bfloat16)
        dq = dq + more
    dk, dv, more = piece(k_ref[...], v_ref[...], 0)
    own_ref[0] = dk
    own_ref[1] = dv
    dq_ref[...] = ((dq + more) * scale).T.astype(jnp.bfloat16)


def local(queries, key_heads, value_heads, out_weight, block_lists, out_grad):
    scale = HD ** (-0.5)
    tokens, features = queries.shape
    groups = features // HD
    per_dev = tokens // BLK
    ctx = lax.axis_size("ctx")
    head = lax.axis_size("head")
    run = lax.axis_index("ctx")
    column = lax.axis_index("head")
    reach = -(-REACH // per_dev)
    offsets = tuple(o for o in range(-reach, reach + 1) if o != 0)
    places = 1 + len(offsets)

    both = jnp.stack([key_heads, value_heads])
    bands = [shifted(both, -o) for o in offsets]
    first = from_first(both[:, :BLK])
    full_weight = lax.all_gather(out_weight, "ctx", axis=0, tiled=True)
    grad_full = lax.all_gather(out_grad, "head", axis=1, tiled=True)

    rounds = ctx // head
    width = out_weight.shape[0]
    mine = jnp.zeros((rounds * tokens, width), jnp.bfloat16)
    for r in range(rounds):
        pairs = []
        for c in range(ctx):
            for h in range(head):
                pairs.append((c * head + h, (rounds * h + (c + r) % rounds) * head + c // rounds))
        sent = lax.dynamic_slice_in_dim(out_grad, ((run + r) % rounds) * width, width, 1)
        got = lax.ppermute(sent, ("ctx", "head"), pairs)
        mine = lax.dynamic_update_slice_in_dim(mine, got, ((run - r) % rounds) * tokens, 0)
    grad_rows = lax.all_gather(mine, "head", axis=0, tiled=True)

    run_word = run.astype(jnp.int32).reshape(1)
    smem = pl.BlockSpec(memory_space=pltpu.SMEM)
    flat = pl.BlockSpec((tokens, HD), lambda h: (0, h))
    pair = pl.BlockSpec((2, tokens, HD), lambda h: (0, 0, h))
    head_pair = pl.BlockSpec((2, BLK, HD), lambda h: (0, 0, h))
    row = pl.BlockSpec((1, 1, tokens), lambda h: (h, 0, 0))
    keys = places * tokens + BLK
    mixed, lse = pl.pallas_call(
        functools.partial(fwd_kernel, offsets, per_dev, scale),
        grid=(groups,),
        in_specs=[smem, smem, flat, flat, flat] + [pair] * len(offsets) + [head_pair],
        out_specs=[flat, row],
        out_shape=[
            jax.ShapeDtypeStruct((tokens, features), jnp.bfloat16),
            jax.ShapeDtypeStruct((groups, 1, tokens), jnp.float32),
        ],
        scratch_shapes=[pltpu.VMEM((keys, tokens), jnp.float32)],
        compiler_params=pltpu.CompilerParams(vmem_limit_bytes=40 * 1024 * 1024),
        cost_estimate=pl.CostEstimate(
            flops=4 * keys * tokens * features, bytes_accessed=4 * keys * features, transcendentals=keys * tokens * groups
        ),
        name="attend",
    )(run_word, block_lists, queries, key_heads, value_heads, *bands, first)

    partial_out = mm(mixed, full_weight, NT).astype(jnp.bfloat16)
    attended = lax.psum_scatter(partial_out, "head", scatter_dimension=1, tiled=True)
    mixed_grad = mm(grad_full, full_weight, NN).astype(jnp.bfloat16)
    mixed_all = lax.all_gather(mixed, "ctx", axis=0, tiled=True)

    results = pl.pallas_call(
        functools.partial(bwd_kernel, offsets, per_dev, scale),
        grid=(groups,),
        in_specs=[smem, smem, flat, flat, flat] + [pair] * len(offsets) + [head_pair, flat, flat, row],
        out_specs=[flat, pair] + [pair] * len(offsets) + [head_pair],
        out_shape=[
            jax.ShapeDtypeStruct((tokens, features), jnp.bfloat16),
            jax.ShapeDtypeStruct((2, tokens, features), jnp.float32),
        ]
        + [jax.ShapeDtypeStruct((2, tokens, features), jnp.bfloat16)] * len(offsets)
        + [jax.ShapeDtypeStruct((2, BLK, features), jnp.float32)],
        scratch_shapes=[pltpu.VMEM((tokens, tokens), jnp.float32)],
        compiler_params=pltpu.CompilerParams(vmem_limit_bytes=40 * 1024 * 1024),
        cost_estimate=pl.CostEstimate(
            flops=10 * keys * tokens * features, bytes_accessed=10 * keys * features, transcendentals=keys * tokens * groups
        ),
        name="attend_grad",
    )(run_word, block_lists, queries, key_heads, value_heads, *bands, first, mixed, mixed_grad, lse)
    query_grad, own = results[:2]
    sums = own
    for o, part in zip(offsets, results[2:-1]):
        sums = sums + shifted(part, o).astype(jnp.float32)
    first_sum = to_first(results[-1])
    first_sum = jnp.where(run == 0, first_sum, 0.0)
    sums = sums + jnp.pad(first_sum, ((0, 0), (0, tokens - BLK), (0, 0)))
    key_grad = (sums[0] * scale).astype(jnp.bfloat16)
    value_grad = sums[1].astype(jnp.bfloat16)
    weight_grad = mm(grad_rows, mixed_all, TN)
    return (attended, query_grad, key_grad, value_grad, weight_grad)


def solution(mesh):
    spec = P("ctx", "head")
    return jax.shard_map(
        local,
        mesh=mesh,
        in_specs=(spec, spec, spec, spec, P(), spec),
        out_specs=(spec,) * 5,
        check_vma=False,
    )
```

```python
import functools

import jax
import jax.numpy as jnp
from jax import lax
from jax.experimental import pallas as pl
from jax.experimental.pallas import tpu as pltpu
from jax.sharding import PartitionSpec as P

HD = 128
BLK = 128
REACH = 4

NT = (((1,), (1,)), ((), ()))
TN = (((0,), (0,)), ((), ()))
NN = (((1,), (0,)), ((), ()))


def mm(a, b, dims):
    return lax.dot_general(a, b, dims, preferred_element_type=jnp.float32)


def shifted(x, by):
    peers = lax.axis_size("ctx")
    return lax.ppermute(x, "ctx", [(i, i + by) for i in range(peers) if 0 <= i + by < peers])


def tree_strides(peers):
    strides = []
    stride = 1
    while stride < peers:
        strides.append(stride)
        stride *= 2
    return strides


def from_first(x):
    peers = lax.axis_size("ctx")
    me = lax.axis_index("ctx")
    for stride in reversed(tree_strides(peers)):
        pairs = [(i, i + stride) for i in range(0, peers, 2 * stride) if i + stride < peers]
        got = lax.ppermute(x, "ctx", pairs)
        x = jnp.where(me % (2 * stride) == stride, got, x)
    return x


def to_first(x):
    peers = lax.axis_size("ctx")
    for stride in tree_strides(peers):
        pairs = [(i + stride, i) for i in range(0, peers, 2 * stride) if i + stride < peers]
        x = x + lax.ppermute(x.astype(jnp.bfloat16), "ctx", pairs).astype(x.dtype)
    return x


def all_rows(x):
    peers = lax.axis_size("ctx")
    length = peers // 2
    if peers % 2 or length < 2 or length > 4:
        full = lax.all_gather(x, "ctx", axis=0, tiled=True)
        return full, x
    me = lax.axis_index("ctx")
    place = me // 2
    side = me % 2

    def along(piece, step, by):
        pairs = []
        for z in range(length):
            origin = z - (step - 1) * by
            if 0 <= z + by < length and 0 <= origin < length:
                pairs += [(2 * z + n, 2 * (z + by) + n) for n in range(2)]
        return lax.ppermute(piece, "ctx", pairs)

    def swapped(piece, held):
        pairs = [(2 * z + n, 2 * z + 1 - n) for z in range(length) if held(z) for n in range(2)]
        return lax.ppermute(piece, "ctx", pairs)

    up, down = [x], [x]
    other_up = [swapped(x, lambda z: True)]
    other_down = [other_up[0]]
    for step in range(1, length):
        up.append(along(up[-1], step, 1))
        down.append(along(down[-1], step, -1))
        if 2 * step >= length:
            both = jnp.where(place >= step, up[-1], down[-1])
            swap = swapped(both, lambda z: z >= step or z <= length - 1 - step)
            other_up.append(swap)
            other_down.append(swap)
        else:
            other_up.append(swapped(up[-1], lambda z: z >= step))
            other_down.append(swapped(down[-1], lambda z: z <= length - 1 - step))
    rows = x.shape[0]
    full = jnp.zeros((peers * rows,) + x.shape[1:], x.dtype)
    for step in range(length):
        origin = (place - step) % length
        for n, ups, downs in ((side, up, down), (1 - side, other_up, other_down)):
            piece = ups[0] if step == 0 else jnp.where(place >= step, ups[step], downs[length - step])
            full = lax.dynamic_update_slice_in_dim(full, piece, (2 * origin + n) * rows, 0)
    return full, down[length // 2]


def block_bias(lists_ref, run, per_dev, total_blocks, offset, i, j):
    row = run * per_dev + i
    key = (run + offset) * per_dev + j
    hit = (key - row <= 1) & (row - key <= 1)
    for n in range(lists_ref.shape[1]):
        hit = hit | (lists_ref[row, n] == key)
    hit = hit & (key >= 1) & (key < total_blocks)
    return jnp.where(hit, 0.0, -jnp.inf).astype(jnp.float32)


def fwd_kernel(offsets, per_dev, scale, run_ref, lists_ref, q_ref, k_ref, v_ref, *rest):
    bands = rest[: len(offsets)]
    first_ref, mixed_ref, lse_ref, s_ref = rest[len(offsets) :]
    total_blocks = lists_ref.shape[0]
    run = run_ref[0]
    q = q_ref[...]
    tokens = q.shape[0]

    def key_of(p):
        return k_ref[...] if p == 0 else bands[p - 1][0]

    def value_of(p):
        return v_ref[...] if p == 0 else bands[p - 1][1]

    places = (0,) + offsets
    top = None
    for p, offset in enumerate(places):
        s = mm(key_of(p), q, NT) * scale
        for j in range(per_dev):
            for i in range(per_dev):
                part = s[j * BLK : (j + 1) * BLK, i * BLK : (i + 1) * BLK]
                part = part + block_bias(lists_ref, run, per_dev, total_blocks, offset, i, j)
                s_ref[p * tokens + j * BLK : p * tokens + (j + 1) * BLK, i * BLK : (i + 1) * BLK] = part
    s_ref[len(places) * tokens :, :] = mm(first_ref[0], q, NT) * scale
    s = s_ref[...]
    top = jnp.max(s, axis=0, keepdims=True)
    e = jnp.exp(s - top)
    total = jnp.sum(e, axis=0, keepdims=True)
    inverse = 1.0 / total
    low = (e * inverse).astype(jnp.bfloat16)
    out = mm(first_ref[1], low[len(places) * tokens :], TN)
    for p in range(len(places)):
        out = out + mm(value_of(p), low[p * tokens : (p + 1) * tokens], TN)
    mixed_ref[...] = out.T.astype(jnp.bfloat16)
    lse_ref[0] = top + jnp.log(total)


def bwd_kernel(offsets, per_dev, scale, run_ref, lists_ref, q_ref, k_ref, v_ref, *rest):
    bands = rest[: len(offsets)]
    first_ref, mixed_ref, grad_ref, lse_ref = rest[len(offsets) : len(offsets) + 4]
    outs = rest[len(offsets) + 4 :]
    dq_ref, own_ref = outs[:2]
    band_outs = outs[2 : 2 + len(offsets)]
    dfirst_ref, s_ref = outs[2 + len(offsets) :]
    total_blocks = lists_ref.shape[0]
    run = run_ref[0]
    q = q_ref[...]
    tokens = q.shape[0]
    grad = grad_ref[...]
    lse = lse_ref[0]
    product = grad.astype(jnp.float32) * mixed_ref[...].astype(jnp.float32)
    delta = jnp.sum(product.T, axis=0, keepdims=True)

    def piece(key, value, offset):
        s = mm(key, q, NT) * scale
        if offset is None:
            p = jnp.exp(s - lse)
        else:
            for j in range(per_dev):
                for i in range(per_dev):
                    part = s[j * BLK : (j + 1) * BLK, i * BLK : (i + 1) * BLK]
                    part = part + block_bias(lists_ref, run, per_dev, total_blocks, offset, i, j)
                    s_ref[j * BLK : (j + 1) * BLK, i * BLK : (i + 1) * BLK] = part
            p = jnp.exp(s_ref[...] - lse)
        slopes = (p * (mm(value, grad, NT) - delta)).astype(jnp.bfloat16)
        dk = mm(slopes, q, NN)
        dv = mm(p.astype(jnp.bfloat16), grad, NN)
        return dk, dv, mm(key, slopes, TN)

    dk, dv, dq = piece(first_ref[0], first_ref[1], None)
    dfirst_ref[0] = dk
    dfirst_ref[1] = dv
    for n, offset in enumerate(offsets):
        dk, dv, more = piece(bands[n][0], bands[n][1], offset)
        band_outs[n][0] = dk.astype(jnp.bfloat16)
        band_outs[n][1] = dv.astype(jnp.bfloat16)
        dq = dq + more
    dk, dv, more = piece(k_ref[...], v_ref[...], 0)
    own_ref[0] = dk
    own_ref[1] = dv
    dq_ref[...] = ((dq + more) * scale).T.astype(jnp.bfloat16)


def local(queries, key_heads, value_heads, out_weight, block_lists, out_grad):
    scale = HD ** (-0.5)
    tokens, features = queries.shape
    groups = features // HD
    per_dev = tokens // BLK
    ctx = lax.axis_size("ctx")
    head = lax.axis_size("head")
    run = lax.axis_index("ctx")
    column = lax.axis_index("head")
    reach = -(-REACH // per_dev)
    offsets = tuple(o for o in range(-reach, reach + 1) if o != 0)
    places = 1 + len(offsets)

    both = jnp.stack([key_heads, value_heads])
    bands = [shifted(both, -o) for o in offsets]
    first = from_first(both[:, :BLK])
    full_weight, halfway = all_rows(out_weight)
    grad_full = lax.all_gather(out_grad, "head", axis=1, tiled=True)

    rounds = ctx // head
    width = out_weight.shape[0]
    mine = jnp.zeros((rounds * tokens, width), jnp.bfloat16)
    for r in range(rounds):
        pairs = []
        for c in range(ctx):
            for h in range(head):
                pairs.append((c * head + h, (rounds * h + (c + r) % rounds) * head + c // rounds))
        sent = lax.dynamic_slice_in_dim(out_grad, ((run + r) % rounds) * width, width, 1)
        sent, halfway = lax.optimization_barrier((sent, halfway))
        got = lax.ppermute(sent, ("ctx", "head"), pairs)
        mine = lax.dynamic_update_slice_in_dim(mine, got, ((run - r) % rounds) * tokens, 0)
    grad_rows = lax.all_gather(mine, "head", axis=0, tiled=True)

    run_word = run.astype(jnp.int32).reshape(1)
    smem = pl.BlockSpec(memory_space=pltpu.SMEM)
    flat = pl.BlockSpec((tokens, HD), lambda h: (0, h))
    pair = pl.BlockSpec((2, tokens, HD), lambda h: (0, 0, h))
    head_pair = pl.BlockSpec((2, BLK, HD), lambda h: (0, 0, h))
    row = pl.BlockSpec((1, 1, tokens), lambda h: (h, 0, 0))
    keys = places * tokens + BLK
    mixed, lse = pl.pallas_call(
        functools.partial(fwd_kernel, offsets, per_dev, scale),
        grid=(groups,),
        in_specs=[smem, smem, flat, flat, flat] + [pair] * len(offsets) + [head_pair],
        out_specs=[flat, row],
        out_shape=[
            jax.ShapeDtypeStruct((tokens, features), jnp.bfloat16),
            jax.ShapeDtypeStruct((groups, 1, tokens), jnp.float32),
        ],
        scratch_shapes=[pltpu.VMEM((keys, tokens), jnp.float32)],
        compiler_params=pltpu.CompilerParams(vmem_limit_bytes=40 * 1024 * 1024),
        cost_estimate=pl.CostEstimate(
            flops=4 * keys * tokens * features, bytes_accessed=4 * keys * features, transcendentals=keys * tokens * groups
        ),
        name="attend",
    )(run_word, block_lists, queries, key_heads, value_heads, *bands, first)

    partial_out = mm(mixed, full_weight, NT).astype(jnp.bfloat16)
    attended = lax.psum_scatter(partial_out, "head", scatter_dimension=1, tiled=True)
    mixed_grad = mm(grad_full, full_weight, NN).astype(jnp.bfloat16)
    mixed_all, _ = all_rows(mixed)

    results = pl.pallas_call(
        functools.partial(bwd_kernel, offsets, per_dev, scale),
        grid=(groups,),
        in_specs=[smem, smem, flat, flat, flat] + [pair] * len(offsets) + [head_pair, flat, flat, row],
        out_specs=[flat, pair] + [pair] * len(offsets) + [head_pair],
        out_shape=[
            jax.ShapeDtypeStruct((tokens, features), jnp.bfloat16),
            jax.ShapeDtypeStruct((2, tokens, features), jnp.float32),
        ]
        + [jax.ShapeDtypeStruct((2, tokens, features), jnp.bfloat16)] * len(offsets)
        + [jax.ShapeDtypeStruct((2, BLK, features), jnp.float32)],
        scratch_shapes=[pltpu.VMEM((tokens, tokens), jnp.float32)],
        compiler_params=pltpu.CompilerParams(vmem_limit_bytes=40 * 1024 * 1024),
        cost_estimate=pl.CostEstimate(
            flops=10 * keys * tokens * features, bytes_accessed=10 * keys * features, transcendentals=keys * tokens * groups
        ),
        name="attend_grad",
    )(run_word, block_lists, queries, key_heads, value_heads, *bands, first, mixed, mixed_grad, lse)
    query_grad, own = results[:2]
    sums = own
    for o, part in zip(offsets, results[2:-1]):
        sums = sums + shifted(part, o).astype(jnp.float32)
    first_sum = to_first(results[-1])
    first_sum = jnp.where(run == 0, first_sum, 0.0)
    sums = sums + jnp.pad(first_sum, ((0, 0), (0, tokens - BLK), (0, 0)))
    key_grad = (sums[0] * scale).astype(jnp.bfloat16)
    value_grad = sums[1].astype(jnp.bfloat16)
    weight_grad = mm(grad_rows, mixed_all, TN)
    return (attended, query_grad, key_grad, value_grad, weight_grad)


def solution(mesh):
    spec = P("ctx", "head")
    return jax.shard_map(
        local,
        mesh=mesh,
        in_specs=(spec, spec, spec, spec, P(), spec),
        out_specs=(spec,) * 5,
        check_vma=False,
    )
```

```python
import functools

import jax
import jax.numpy as jnp
from jax import lax
from jax.experimental import pallas as pl
from jax.experimental.pallas import tpu as pltpu
from jax.sharding import PartitionSpec as P

HD = 128
BLK = 128
REACH = 4

NT = (((1,), (1,)), ((), ()))
TN = (((0,), (0,)), ((), ()))
NN = (((1,), (0,)), ((), ()))


def mm(a, b, dims):
    return lax.dot_general(a, b, dims, preferred_element_type=jnp.float32)


def shifted(x, by):
    peers = lax.axis_size("ctx")
    return lax.ppermute(x, "ctx", [(i, i + by) for i in range(peers) if 0 <= i + by < peers])


def tree_strides(peers):
    strides = []
    stride = 1
    while stride < peers:
        strides.append(stride)
        stride *= 2
    return strides


def from_first(x):
    peers = lax.axis_size("ctx")
    me = lax.axis_index("ctx")
    for stride in reversed(tree_strides(peers)):
        pairs = [(i, i + stride) for i in range(0, peers, 2 * stride) if i + stride < peers]
        got = lax.ppermute(x, "ctx", pairs)
        x = jnp.where(me % (2 * stride) == stride, got, x)
    return x


def to_first(x):
    peers = lax.axis_size("ctx")
    for stride in tree_strides(peers):
        pairs = [(i + stride, i) for i in range(0, peers, 2 * stride) if i + stride < peers]
        x = x + lax.ppermute(x.astype(jnp.bfloat16), "ctx", pairs).astype(x.dtype)
    return x


def line_of(step, by, length):
    return [z for z in range(length) if 0 <= z - step * by < length]


def along(piece, step, by, length):
    pairs = [(2 * (z - by) + n, 2 * z + n) for z in line_of(step, by, length) for n in range(2)]
    return lax.ppermute(piece, "ctx", pairs)


def swapped(piece, places):
    return lax.ppermute(piece, "ctx", [(2 * z + n, 2 * z + 1 - n) for z in places for n in range(2)])


def tied(x, *others):
    return lax.optimization_barrier((x,) + others)[0]


def spread_index(n, length):
    return (n % 2) * (length // 2) + n // 2


def spread_back(n, length):
    return (n % (length // 2)) * 2 + n // (length // 2)


def origins(length, with_swapped):
    plan = []
    for other in range(2 if with_swapped else 1):
        plan.append((0, other))
        for step in range(1, length):
            plan.append((step, other))
            plan.append((-step, other))
    return plan


def start_pieces(plan, length, pieces, target_of, sems):
    place = lax.div(lax.axis_index("ctx"), 2)
    side = lax.rem(lax.axis_index("ctx"), 2)
    for (back, other), piece in zip(plan, pieces):
        origin = place - back
        at, slot = target_of(origin, side if other == 0 else 1 - side)

        def send(piece=piece, at=at, slot=slot):
            pltpu.make_async_copy(piece, at, sems.at[slot]).start()

        if back == 0:
            send()
        else:
            pl.when((origin >= 0) & (origin < length))(send)


def project_kernel(plan, length, grads_ref, mixed_ref, *rest):
    pieces = rest[: len(plan)]
    grad_ref, out_ref, held_ref, sems = rest[len(plan) :]
    blocks, width = held_ref.shape[:2]

    def target_of(origin, side):
        slot = 2 * origin + side
        return held_ref.at[slot], slot

    start_pieces(plan, length, pieces, target_of, sems)
    mixed = mixed_ref[...]
    total = None
    for b in range(blocks):
        pltpu.make_async_copy(held_ref.at[b], held_ref.at[b], sems.at[b]).wait()
        weight = held_ref[b]
        part = mm(grads_ref[:, b * width : (b + 1) * width], weight, NN)
        total = part if total is None else total + part
        out_ref[:, b * width : (b + 1) * width] = mm(mixed, weight, NT).astype(jnp.bfloat16)
    grad_ref[...] = total.astype(jnp.bfloat16)


def weight_kernel(plan, length, rows_ref, *rest):
    pieces = rest[: len(plan)]
    own_ref, other_ref, held_ref, sems = rest[len(plan) :]
    width = own_ref.shape[0]
    side = lax.rem(lax.axis_index("ctx"), 2)

    def target_of(origin, side):
        slot = lax.rem(origin + length, length // 2) * 2 + lax.div(origin, length // 2)
        return held_ref.at[slot], slot

    start_pieces(plan, length, pieces, target_of, sems)
    for b in range(length):
        pltpu.make_async_copy(held_ref.at[b], held_ref.at[b], sems.at[b]).wait()
    mixed = held_ref[...].reshape(rows_ref.shape[0], -1)
    other = rows_ref[:, pl.ds(pl.multiple_of((1 - side) * width, 128), width)]
    other_ref[...] = mm(other, mixed, TN).astype(jnp.bfloat16)
    own = rows_ref[:, pl.ds(pl.multiple_of(side * width, 128), width)]
    own_ref[...] = mm(own, mixed, TN)


def block_bias(lists_ref, run, per_dev, total_blocks, offset, i, j):
    row = run * per_dev + i
    key = (run + offset) * per_dev + j
    hit = (key - row <= 1) & (row - key <= 1)
    for n in range(lists_ref.shape[1]):
        hit = hit | (lists_ref[row, n] == key)
    hit = hit & (key >= 1) & (key < total_blocks)
    return jnp.where(hit, 0.0, -jnp.inf).astype(jnp.float32)


def fwd_kernel(offsets, per_dev, scale, run_ref, lists_ref, q_ref, k_ref, v_ref, *rest):
    bands = rest[: len(offsets)]
    first_ref, mixed_ref, lse_ref, s_ref = rest[len(offsets) :]
    total_blocks = lists_ref.shape[0]
    run = run_ref[0]
    q = q_ref[...]
    tokens = q.shape[0]

    def key_of(p):
        return k_ref[...] if p == 0 else bands[p - 1][0]

    def value_of(p):
        return v_ref[...] if p == 0 else bands[p - 1][1]

    places = (0,) + offsets
    top = None
    for p, offset in enumerate(places):
        s = mm(key_of(p), q, NT) * scale
        for j in range(per_dev):
            for i in range(per_dev):
                part = s[j * BLK : (j + 1) * BLK, i * BLK : (i + 1) * BLK]
                part = part + block_bias(lists_ref, run, per_dev, total_blocks, offset, i, j)
                s_ref[p * tokens + j * BLK : p * tokens + (j + 1) * BLK, i * BLK : (i + 1) * BLK] = part
    s_ref[len(places) * tokens :, :] = mm(first_ref[0], q, NT) * scale
    s = s_ref[...]
    top = jnp.max(s, axis=0, keepdims=True)
    e = jnp.exp(s - top)
    total = jnp.sum(e, axis=0, keepdims=True)
    inverse = 1.0 / total
    low = (e * inverse).astype(jnp.bfloat16)
    out = mm(first_ref[1], low[len(places) * tokens :], TN)
    for p in range(len(places)):
        out = out + mm(value_of(p), low[p * tokens : (p + 1) * tokens], TN)
    mixed_ref[...] = out.T.astype(jnp.bfloat16)
    lse_ref[0] = top + jnp.log(total)


def bwd_kernel(offsets, per_dev, scale, run_ref, lists_ref, q_ref, k_ref, v_ref, *rest):
    bands = rest[: len(offsets)]
    first_ref, mixed_ref, grad_ref, lse_ref = rest[len(offsets) : len(offsets) + 4]
    outs = rest[len(offsets) + 4 :]
    dq_ref, own_ref = outs[:2]
    band_outs = outs[2 : 2 + len(offsets)]
    (s_ref,) = outs[2 + len(offsets) :]
    total_blocks = lists_ref.shape[0]
    run = run_ref[0]
    q = q_ref[...]
    tokens = q.shape[0]
    grad = grad_ref[...]
    lse = lse_ref[0]
    product = grad.astype(jnp.float32) * mixed_ref[...].astype(jnp.float32)
    delta = jnp.sum(product.T, axis=0, keepdims=True)

    def piece(key, value, offset):
        s = mm(key, q, NT) * scale
        if offset is None:
            p = jnp.exp(s - lse)
        else:
            for j in range(per_dev):
                for i in range(per_dev):
                    part = s[j * BLK : (j + 1) * BLK, i * BLK : (i + 1) * BLK]
                    part = part + block_bias(lists_ref, run, per_dev, total_blocks, offset, i, j)
                    s_ref[j * BLK : (j + 1) * BLK, i * BLK : (i + 1) * BLK] = part
            p = jnp.exp(s_ref[...] - lse)
        slopes = (p * (mm(value, grad, NT) - delta)).astype(jnp.bfloat16)
        more = mm(key, slopes, TN)
        if offset is None:
            return more
        return mm(slopes, q, NN), mm(p.astype(jnp.bfloat16), grad, NN), more

    dq = piece(first_ref[0], first_ref[1], None)
    for n, offset in enumerate(offsets):
        dk, dv, more = piece(bands[n][0], bands[n][1], offset)
        band_outs[n][0] = dk.astype(jnp.bfloat16)
        band_outs[n][1] = dv.astype(jnp.bfloat16)
        dq = dq + more
    dk, dv, more = piece(k_ref[...], v_ref[...], 0)
    own_ref[0] = dk
    own_ref[1] = dv
    dq_ref[...] = ((dq + more) * scale).T.astype(jnp.bfloat16)


def first_kernel(scale, q_ref, first_ref, mixed_ref, grad_ref, lse_ref, dfirst_ref):
    q = q_ref[...]
    grad = grad_ref[...]
    product = grad.astype(jnp.float32) * mixed_ref[...].astype(jnp.float32)
    delta = jnp.sum(product.T, axis=0, keepdims=True)
    p = jnp.exp(mm(first_ref[0], q, NT) * scale - lse_ref[0])
    slopes = (p * (mm(first_ref[1], grad, NT) - delta)).astype(jnp.bfloat16)
    dfirst_ref[0] = mm(slopes, q, NN).astype(jnp.bfloat16)
    dfirst_ref[1] = mm(p.astype(jnp.bfloat16), grad, NN).astype(jnp.bfloat16)


def local(queries, key_heads, value_heads, out_weight, block_lists, out_grad):
    scale = HD ** (-0.5)
    tokens, features = queries.shape
    groups = features // HD
    per_dev = tokens // BLK
    ctx = lax.axis_size("ctx")
    head = lax.axis_size("head")
    run = lax.axis_index("ctx")
    column = lax.axis_index("head")
    reach = -(-REACH // per_dev)
    offsets = tuple(o for o in range(-reach, reach + 1) if o != 0)
    places = 1 + len(offsets)

    length = ctx // 2
    direct = ctx == 8 and head == length and reach == 2
    place = run // 2
    side = run % 2
    smem = pl.BlockSpec(memory_space=pltpu.SMEM)
    whole = pl.BlockSpec(memory_space=pltpu.VMEM)
    anywhere = pl.BlockSpec(memory_space=pl.ANY)
    width = out_weight.shape[0]

    both = jnp.stack([key_heads, value_heads])
    bands = [shifted(both, -o) for o in offsets]
    grad_full = lax.all_gather(out_grad, "head", axis=1, tiled=True)
    head_rows = both[:, :BLK]
    if direct:
        far = lax.ppermute(head_rows, "ctx", [(0, length)])
        ready = tuple(bands) + (far,)
        early = jnp.where(run == 1, bands[offsets.index(-1)][:, :BLK], head_rows)
        early = jnp.where(run == 2, bands[offsets.index(-2)][:, :BLK], early)
        early = jnp.where(run == length, far, early)
        hop = [(1, 3), (4, 5), (2, 6), (0, 7)]
        late = lax.ppermute(early, "ctx", hop)
        first = jnp.where((run == 3) | (run > 4), late, early)
        base = tied(out_weight, *ready)
        up, down = [base], [base]
        swaps = [swapped(base, range(length))]
        pieces = [base]
        for step in range(1, length):
            up.append(along(up[-1], step, 1, length))
            down.append(along(down[-1], step, -1, length))
            pieces += [up[-1], down[-1]]
            swaps.append(swapped(up[-1], line_of(step, 1, length)))
            swaps.append(swapped(down[-1], line_of(step, -1, length)))
        weight_pieces = pieces + swaps
        middle = (up[length // 2], down[length // 2])
        last = (up[-1], down[-1])
        shard = out_grad.shape[1]
        sent = lax.dynamic_slice_in_dim(grad_full, spread_index(column, length) * shard, shard, 1)
        sent = tied(sent, *middle)
        pairs = []
        for c in range(ctx):
            for h in range(head):
                target = 2 * spread_index(h, length) + c % 2
                pairs.append((c * head + h, target * head + spread_back(c // 2, length)))
        far_rows = lax.ppermute(sent, ("ctx", "head"), pairs)
        grad_rows = lax.all_gather(far_rows, "head", axis=0, tiled=True)
    else:
        first = from_first(head_rows)
        full_weight = lax.all_gather(out_weight, "ctx", axis=0, tiled=True)
        rounds = ctx // head
        mine = jnp.zeros((rounds * tokens, width), jnp.bfloat16)
        for r in range(rounds):
            pairs = []
            for c in range(ctx):
                for h in range(head):
                    pairs.append((c * head + h, (rounds * h + (c + r) % rounds) * head + c // rounds))
            sent = lax.dynamic_slice_in_dim(out_grad, ((run + r) % rounds) * width, width, 1)
            got = lax.ppermute(sent, ("ctx", "head"), pairs)
            mine = lax.dynamic_update_slice_in_dim(mine, got, ((run - r) % rounds) * tokens, 0)
        grad_rows = lax.all_gather(mine, "head", axis=0, tiled=True)

    run_word = run.astype(jnp.int32).reshape(1)
    flat = pl.BlockSpec((tokens, HD), lambda h: (0, h))
    pair = pl.BlockSpec((2, tokens, HD), lambda h: (0, 0, h))
    head_pair = pl.BlockSpec((2, BLK, HD), lambda h: (0, 0, h))
    row = pl.BlockSpec((1, 1, tokens), lambda h: (h, 0, 0))
    keys = places * tokens + BLK
    mixed, lse = pl.pallas_call(
        functools.partial(fwd_kernel, offsets, per_dev, scale),
        grid=(groups,),
        in_specs=[smem, smem, flat, flat, flat] + [pair] * len(offsets) + [head_pair],
        out_specs=[flat, row],
        out_shape=[
            jax.ShapeDtypeStruct((tokens, features), jnp.bfloat16),
            jax.ShapeDtypeStruct((groups, 1, tokens), jnp.float32),
        ],
        scratch_shapes=[pltpu.VMEM((keys, tokens), jnp.float32)],
        compiler_params=pltpu.CompilerParams(vmem_limit_bytes=40 * 1024 * 1024),
        cost_estimate=pl.CostEstimate(
            flops=4 * keys * tokens * features, bytes_accessed=4 * keys * features, transcendentals=keys * tokens * groups
        ),
        name="attend",
    )(run_word, block_lists, queries, key_heads, value_heads, *bands, first)

    if direct:
        plan = origins(length, True)
        mixed_grad, partial_out = pl.pallas_call(
            functools.partial(project_kernel, plan, length),
            in_specs=[whole, whole] + [anywhere] * len(plan),
            out_specs=[whole, whole],
            out_shape=[
                jax.ShapeDtypeStruct((tokens, features), jnp.bfloat16),
                jax.ShapeDtypeStruct((tokens, ctx * width), jnp.bfloat16),
            ],
            scratch_shapes=[pltpu.VMEM((ctx, width, features), jnp.bfloat16), pltpu.SemaphoreType.DMA((ctx,))],
            compiler_params=pltpu.CompilerParams(vmem_limit_bytes=32 * 1024 * 1024),
            cost_estimate=pl.CostEstimate(
                flops=4 * tokens * features * ctx * width, bytes_accessed=2 * ctx * width * (features + 2 * tokens), transcendentals=0
            ),
            name="project",
        )(grad_full, mixed, *weight_pieces)
        mixed_base = tied(mixed, *last)
        up, down = [mixed_base], [mixed_base]
        mixed_pieces = [mixed_base]
        for step in range(1, length):
            up.append(along(up[-1], step, 1, length))
            down.append(along(down[-1], step, -1, length))
            mixed_pieces += [up[-1], down[-1]]
    else:
        partial_out = mm(mixed, full_weight, NT).astype(jnp.bfloat16)
        mixed_grad = mm(grad_full, full_weight, NN).astype(jnp.bfloat16)
        mixed_all = lax.all_gather(mixed, "ctx", axis=0, tiled=True)
    attended = lax.psum_scatter(partial_out, "head", scatter_dimension=1, tiled=True)
    dfirst = pl.pallas_call(
        functools.partial(first_kernel, scale),
        grid=(groups,),
        in_specs=[flat, head_pair, flat, flat, row],
        out_specs=head_pair,
        out_shape=jax.ShapeDtypeStruct((2, BLK, features), jnp.bfloat16),
        compiler_params=pltpu.CompilerParams(vmem_limit_bytes=32 * 1024 * 1024),
        cost_estimate=pl.CostEstimate(
            flops=8 * BLK * tokens * features, bytes_accessed=8 * tokens * features, transcendentals=BLK * tokens * groups
        ),
        name="first_grad",
    )(queries, first, mixed, mixed_grad, lse)
    if direct:
        turn = [(b, a) for a, b in hop]
        first_sum = dfirst.astype(jnp.float32) + lax.ppermute(dfirst, "ctx", turn).astype(jnp.float32)

    results = pl.pallas_call(
        functools.partial(bwd_kernel, offsets, per_dev, scale),
        grid=(groups,),
        in_specs=[smem, smem, flat, flat, flat] + [pair] * len(offsets) + [head_pair, flat, flat, row],
        out_specs=[flat, pair] + [pair] * len(offsets),
        out_shape=[
            jax.ShapeDtypeStruct((tokens, features), jnp.bfloat16),
            jax.ShapeDtypeStruct((2, tokens, features), jnp.float32),
        ]
        + [jax.ShapeDtypeStruct((2, tokens, features), jnp.bfloat16)] * len(offsets),
        scratch_shapes=[pltpu.VMEM((tokens, tokens), jnp.float32)],
        compiler_params=pltpu.CompilerParams(vmem_limit_bytes=40 * 1024 * 1024),
        cost_estimate=pl.CostEstimate(
            flops=10 * keys * tokens * features, bytes_accessed=10 * keys * features, transcendentals=keys * tokens * groups
        ),
        name="attend_grad",
    )(run_word, block_lists, queries, key_heads, value_heads, *bands, first, mixed, mixed_grad, lse)
    query_grad, own = results[:2]
    if direct:
        near = first_sum.astype(jnp.bfloat16)
        for c in (1, 2, length):
            first_sum = first_sum + lax.ppermute(near, "ctx", [(c, 0)]).astype(jnp.float32)
    else:
        first_sum = to_first(dfirst.astype(jnp.float32))
    sums = own
    for o, part in zip(offsets, results[2:]):
        sums = sums + shifted(part, o).astype(jnp.float32)
    first_sum = jnp.where(run == 0, first_sum, 0.0)
    sums = sums + jnp.pad(first_sum, ((0, 0), (0, tokens - BLK), (0, 0)))
    key_grad = (sums[0] * scale).astype(jnp.bfloat16)
    value_grad = sums[1].astype(jnp.bfloat16)
    if direct:
        plan = origins(length, False)
        half, other_half = pl.pallas_call(
            functools.partial(weight_kernel, plan, length),
            in_specs=[whole] + [anywhere] * len(plan),
            out_specs=[whole, whole],
            out_shape=[
                jax.ShapeDtypeStruct((width, features), jnp.float32),
                jax.ShapeDtypeStruct((width, features), jnp.bfloat16),
            ],
            scratch_shapes=[pltpu.VMEM((length, tokens, features), jnp.bfloat16), pltpu.SemaphoreType.DMA((length,))],
            compiler_params=pltpu.CompilerParams(vmem_limit_bytes=32 * 1024 * 1024),
            cost_estimate=pl.CostEstimate(
                flops=4 * length * tokens * width * features, bytes_accessed=4 * length * tokens * features, transcendentals=0
            ),
            name="weight_sum",
        )(grad_rows, *mixed_pieces)
        weight_grad = half + swapped(other_half, range(length)).astype(jnp.float32)
    else:
        weight_grad = mm(grad_rows, mixed_all, TN)
    return (attended, query_grad, key_grad, value_grad, weight_grad)


def solution(mesh):
    spec = P("ctx", "head")
    return jax.shard_map(
        local,
        mesh=mesh,
        in_specs=(spec, spec, spec, spec, P(), spec),
        out_specs=(spec,) * 5,
        check_vma=False,
    )
```

```python
import functools

import jax
import jax.numpy as jnp
from jax import lax
from jax.experimental import pallas as pl
from jax.experimental.pallas import tpu as pltpu
from jax.sharding import PartitionSpec as P

HD = 128
BLK = 128
REACH = 4

NT = (((1,), (1,)), ((), ()))
TN = (((0,), (0,)), ((), ()))
NN = (((1,), (0,)), ((), ()))


def mm(a, b, dims):
    return lax.dot_general(a, b, dims, preferred_element_type=jnp.float32)


def shifted(x, by):
    peers = lax.axis_size("ctx")
    return lax.ppermute(x, "ctx", [(i, i + by) for i in range(peers) if 0 <= i + by < peers])


def tree_strides(peers):
    strides = []
    stride = 1
    while stride < peers:
        strides.append(stride)
        stride *= 2
    return strides


def from_first(x):
    peers = lax.axis_size("ctx")
    me = lax.axis_index("ctx")
    for stride in reversed(tree_strides(peers)):
        pairs = [(i, i + stride) for i in range(0, peers, 2 * stride) if i + stride < peers]
        got = lax.ppermute(x, "ctx", pairs)
        x = jnp.where(me % (2 * stride) == stride, got, x)
    return x


def to_first(x):
    peers = lax.axis_size("ctx")
    for stride in tree_strides(peers):
        pairs = [(i + stride, i) for i in range(0, peers, 2 * stride) if i + stride < peers]
        x = x + lax.ppermute(x.astype(jnp.bfloat16), "ctx", pairs).astype(x.dtype)
    return x


def line_of(step, by, length):
    return [z for z in range(length) if 0 <= z - step * by < length]


def along(piece, step, by, length):
    pairs = [(2 * (z - by) + n, 2 * z + n) for z in line_of(step, by, length) for n in range(2)]
    return lax.ppermute(piece, "ctx", pairs)


def swapped(piece, places):
    return lax.ppermute(piece, "ctx", [(2 * z + n, 2 * z + 1 - n) for z in places for n in range(2)])


def tied(x, *others):
    return lax.optimization_barrier((x,) + others)[0]


def spread_back(n, length):
    return (n % (length // 2)) * 2 + n // (length // 2)


def origins(length):
    plan = [0]
    for step in range(1, length):
        plan += [step, -step]
    return plan


def start_pieces(plan, length, pieces, held_ref, slot_of, sems):
    place = lax.div(lax.axis_index("ctx"), 2)
    for back, piece in zip(plan, pieces):
        origin = place - back

        def send(piece=piece, origin=origin):
            slot = slot_of(origin)
            pltpu.make_async_copy(piece, held_ref.at[slot], sems.at[slot]).start()

        if back == 0:
            send()
        else:
            pl.when((origin >= 0) & (origin < length))(send)


def project_kernel(plan, length, grads_ref, mixed_ref, other_ref, *rest):
    pieces = rest[: len(plan)]
    grad_ref, other_grad_ref, out_ref, held_ref, sems = rest[len(plan) :]
    width = held_ref.shape[1]
    tokens = mixed_ref.shape[0]
    start_pieces(plan, length, pieces, held_ref, lambda origin: origin, sems)
    total = None
    for b in range(length):
        pltpu.make_async_copy(held_ref.at[b], held_ref.at[b], sems.at[b]).wait()
        weight = held_ref[b]
        columns = slice(b * width, (b + 1) * width)
        part = mm(grads_ref[:, columns], weight, NN)
        total = part if total is None else total + part
        out_ref[:tokens, columns] = mm(mixed_ref[...], weight, NT).astype(jnp.bfloat16)
        out_ref[tokens:, columns] = mm(other_ref[...], weight, NT).astype(jnp.bfloat16)
    grad_ref[...] = total[:tokens]
    other_grad_ref[...] = total[tokens:].astype(jnp.bfloat16)


def weight_kernel(plan, length, rows_ref, *rest):
    pieces = rest[: len(plan)]
    own_ref, other_ref, held_ref, sems = rest[len(plan) :]
    width = own_ref.shape[0]
    side = lax.rem(lax.axis_index("ctx"), 2)

    def slot_of(origin):
        return lax.rem(origin, length // 2) * 2 + lax.div(origin, length // 2)

    start_pieces(plan, length, pieces, held_ref, slot_of, sems)
    for b in range(length):
        pltpu.make_async_copy(held_ref.at[b], held_ref.at[b], sems.at[b]).wait()
    mixed = held_ref[...].reshape(rows_ref.shape[0], -1)
    other = rows_ref[:, pl.ds(pl.multiple_of((1 - side) * width, 128), width)]
    other_ref[...] = mm(other, mixed, TN).astype(jnp.bfloat16)
    own = rows_ref[:, pl.ds(pl.multiple_of(side * width, 128), width)]
    own_ref[...] = mm(own, mixed, TN)


def runs_away(offset, run):
    side = lax.rem(run, 2)
    if offset == "pair":
        return 1 - 2 * side
    if offset == "across":
        return 2 * side - 1
    return offset


def block_bias(lists_ref, run, per_dev, total_blocks, offset, i, j):
    row = run * per_dev + i
    key = (run + runs_away(offset, run)) * per_dev + j
    hit = (key - row <= 1) & (row - key <= 1)
    for n in range(lists_ref.shape[1]):
        hit = hit | (lists_ref[row, n] == key)
    hit = hit & (key >= 1) & (key < total_blocks)
    return jnp.where(hit, 0.0, -jnp.inf).astype(jnp.float32)


def fwd_kernel(offsets, per_dev, scale, run_ref, lists_ref, q_ref, k_ref, v_ref, *rest):
    bands = rest[: len(offsets)]
    first_ref, mixed_ref, lse_ref, s_ref = rest[len(offsets) :]
    total_blocks = lists_ref.shape[0]
    run = run_ref[0]
    q = q_ref[...]
    tokens = q.shape[0]

    def key_of(p):
        return k_ref[...] if p == 0 else bands[p - 1][0]

    def value_of(p):
        return v_ref[...] if p == 0 else bands[p - 1][1]

    places = (0,) + offsets
    top = None
    for p, offset in enumerate(places):
        s = mm(key_of(p), q, NT) * scale
        for j in range(per_dev):
            for i in range(per_dev):
                part = s[j * BLK : (j + 1) * BLK, i * BLK : (i + 1) * BLK]
                part = part + block_bias(lists_ref, run, per_dev, total_blocks, offset, i, j)
                s_ref[p * tokens + j * BLK : p * tokens + (j + 1) * BLK, i * BLK : (i + 1) * BLK] = part
    s_ref[len(places) * tokens :, :] = mm(first_ref[0], q, NT) * scale
    s = s_ref[...]
    top = jnp.max(s, axis=0, keepdims=True)
    e = jnp.exp(s - top)
    total = jnp.sum(e, axis=0, keepdims=True)
    inverse = 1.0 / total
    low = (e * inverse).astype(jnp.bfloat16)
    out = mm(first_ref[1], low[len(places) * tokens :], TN)
    for p in range(len(places)):
        out = out + mm(value_of(p), low[p * tokens : (p + 1) * tokens], TN)
    mixed_ref[...] = out.T.astype(jnp.bfloat16)
    lse_ref[0] = top + jnp.log(total)


def probs_of(lists_ref, s_ref, run, per_dev, s, offset, lse):
    if offset is None:
        return jnp.exp(s - lse)
    for j in range(per_dev):
        for i in range(per_dev):
            part = s[j * BLK : (j + 1) * BLK, i * BLK : (i + 1) * BLK]
            part = part + block_bias(lists_ref, run, per_dev, lists_ref.shape[0], offset, i, j)
            s_ref[j * BLK : (j + 1) * BLK, i * BLK : (i + 1) * BLK] = part
    return jnp.exp(s_ref[...] - lse)


def first_kernel(offsets, per_dev, scale, run_ref, lists_ref, q_ref, *rest):
    bands = rest[: len(offsets)]
    first_ref, mixed_ref, grad_ref, lse_ref, dfirst_ref = rest[len(offsets) : len(offsets) + 5]
    band_outs = rest[len(offsets) + 5 : -1]
    s_ref = rest[-1]
    q = q_ref[...]
    grad = grad_ref[...]
    lse = lse_ref[0]
    product = grad.astype(jnp.float32) * mixed_ref[...].astype(jnp.float32)
    delta = jnp.sum(product.T, axis=0, keepdims=True)
    plan = [(None, first_ref, dfirst_ref)] + list(zip(offsets, bands, band_outs))
    for offset, pair_ref, out_ref in plan:
        p = probs_of(lists_ref, s_ref, run_ref[0], per_dev, mm(pair_ref[0], q, NT) * scale, offset, lse)
        slopes = (p * (mm(pair_ref[1], grad, NT) - delta)).astype(jnp.bfloat16)
        out_ref[0] = mm(slopes, q, NN).astype(jnp.bfloat16)
        out_ref[1] = mm(p.astype(jnp.bfloat16), grad, NN).astype(jnp.bfloat16)


def bwd_kernel(offsets, early, per_dev, scale, run_ref, lists_ref, q_ref, k_ref, v_ref, *rest):
    bands = rest[: len(offsets)]
    first_ref, mixed_ref, grad_ref, lse_ref = rest[len(offsets) : len(offsets) + 4]
    outs = rest[len(offsets) + 4 :]
    dq_ref, own_ref = outs[:2]
    band_outs = list(outs[2:-1])
    s_ref = outs[-1]
    q = q_ref[...]
    grad = grad_ref[...]
    lse = lse_ref[0]
    product = grad.astype(jnp.float32) * mixed_ref[...].astype(jnp.float32)
    delta = jnp.sum(product.T, axis=0, keepdims=True)
    dq = None
    plan = [(None, first_ref[0], first_ref[1], None)]
    for offset, pair_ref in zip(offsets, bands):
        plan.append((offset, pair_ref[0], pair_ref[1], None if offset in early else band_outs.pop(0)))
    plan.append((0, k_ref[...], v_ref[...], own_ref))
    for offset, key, value, out_ref in plan:
        p = probs_of(lists_ref, s_ref, run_ref[0], per_dev, mm(key, q, NT) * scale, offset, lse)
        slopes = (p * (mm(value, grad, NT) - delta)).astype(jnp.bfloat16)
        more = mm(key, slopes, TN)
        dq = more if dq is None else dq + more
        if out_ref is not None:
            out_ref[0] = mm(slopes, q, NN).astype(out_ref.dtype)
            out_ref[1] = mm(p.astype(jnp.bfloat16), grad, NN).astype(out_ref.dtype)
    dq_ref[...] = (dq * scale).T.astype(jnp.bfloat16)


def local(queries, key_heads, value_heads, out_weight, block_lists, out_grad):
    scale = HD ** (-0.5)
    tokens, features = queries.shape
    groups = features // HD
    per_dev = tokens // BLK
    ctx = lax.axis_size("ctx")
    head = lax.axis_size("head")
    run = lax.axis_index("ctx")
    column = lax.axis_index("head")
    reach = -(-REACH // per_dev)
    length = ctx // 2
    direct = ctx == 8 and head == length and reach == 2
    place = run // 2
    side = run % 2
    if direct:
        offsets, early = (-2, 2, "pair", "across"), ("across",)
    else:
        offsets, early = tuple(o for o in range(-reach, reach + 1) if o != 0), ()
    places = 1 + len(offsets)
    smem = pl.BlockSpec(memory_space=pltpu.SMEM)
    whole = pl.BlockSpec(memory_space=pltpu.VMEM)
    anywhere = pl.BlockSpec(memory_space=pl.ANY)
    width = out_weight.shape[0]

    both = jnp.stack([key_heads, value_heads])
    head_rows = both[:, :BLK]
    if direct:
        before, after = shifted(both, 2), shifted(both, -2)
        beside = swapped(both, range(length))
        sent = jnp.where(side == 0, after, before)
        hop = [(2 * z, 2 * z + 1) for z in range(length - 1)] + [(2 * z + 1, 2 * z) for z in range(1, length)]
        across = lax.ppermute(sent, "ctx", hop)
        far = lax.ppermute(head_rows, "ctx", [(0, length)])
        known = jnp.where(run == 1, beside[:, :BLK], head_rows)
        known = jnp.where(run == 2, before[:, :BLK], known)
        known = jnp.where(run == length, far, known)
        spread_to = [(1, 3), (4, 5), (2, 6), (0, 7)]
        late = lax.ppermute(known, "ctx", spread_to)
        first = jnp.where((run == 3) | (run > 4), late, known)

        half = out_grad.shape[1] // 2
        own_half = lax.dynamic_slice_in_dim(out_grad, side * half, half, 1)
        other_half = lax.dynamic_slice_in_dim(out_grad, (1 - side) * half, half, 1)
        halves = jnp.concatenate([own_half, swapped(other_half, range(length))], axis=0)
        grad_side = lax.all_gather(halves, "head", axis=1, tiled=True)

        base = tied(out_weight, before, after, beside)
        up, down = [base], [base]
        weight_pieces = [base]
        for step in range(1, length):
            up.append(along(up[-1], step, 1, length))
            down.append(along(down[-1], step, -1, length))
            if step == 1:
                up[1], down[1], across = lax.optimization_barrier((up[1], down[1], across))
            weight_pieces += [up[-1], down[-1]]
        bands = [before, after, beside, across]
        middle = (up[length // 2], down[length // 2])
        last = (up[-1], down[-1])
        sent = tied(out_grad, *middle)
        pairs = []
        for c in range(ctx):
            for h in range(head):
                pairs.append((c * head + h, (2 * h + c % 2) * head + spread_back(c // 2, length)))
        far_rows = lax.ppermute(sent, ("ctx", "head"), pairs)
    else:
        bands = [shifted(both, -o) for o in offsets]
        first = from_first(head_rows)
        grad_full = lax.all_gather(out_grad, "head", axis=1, tiled=True)
        full_weight = lax.all_gather(out_weight, "ctx", axis=0, tiled=True)
        rounds = ctx // head
        mine = jnp.zeros((rounds * tokens, width), jnp.bfloat16)
        for r in range(rounds):
            pairs = []
            for c in range(ctx):
                for h in range(head):
                    pairs.append((c * head + h, (rounds * h + (c + r) % rounds) * head + c // rounds))
            sent = lax.dynamic_slice_in_dim(out_grad, ((run + r) % rounds) * width, width, 1)
            got = lax.ppermute(sent, ("ctx", "head"), pairs)
            mine = lax.dynamic_update_slice_in_dim(mine, got, ((run - r) % rounds) * tokens, 0)
        grad_rows = lax.all_gather(mine, "head", axis=0, tiled=True)

    run_word = run.astype(jnp.int32).reshape(1)
    flat = pl.BlockSpec((tokens, HD), lambda h: (0, h))
    pair = pl.BlockSpec((2, tokens, HD), lambda h: (0, 0, h))
    head_pair = pl.BlockSpec((2, BLK, HD), lambda h: (0, 0, h))
    row = pl.BlockSpec((1, 1, tokens), lambda h: (h, 0, 0))
    keys = places * tokens + BLK
    mixed, lse = pl.pallas_call(
        functools.partial(fwd_kernel, offsets, per_dev, scale),
        grid=(groups,),
        in_specs=[smem, smem, flat, flat, flat] + [pair] * len(offsets) + [head_pair],
        out_specs=[flat, row],
        out_shape=[
            jax.ShapeDtypeStruct((tokens, features), jnp.bfloat16),
            jax.ShapeDtypeStruct((groups, 1, tokens), jnp.float32),
        ],
        scratch_shapes=[pltpu.VMEM((keys, tokens), jnp.float32)],
        compiler_params=pltpu.CompilerParams(vmem_limit_bytes=40 * 1024 * 1024),
        cost_estimate=pl.CostEstimate(
            flops=4 * keys * tokens * features, bytes_accessed=4 * keys * features, transcendentals=keys * tokens * groups
        ),
        name="attend",
    )(run_word, block_lists, queries, key_heads, value_heads, *bands, first)

    if direct:
        plan = origins(length)
        own_grad, other_grad, partial_out = pl.pallas_call(
            functools.partial(project_kernel, plan, length),
            in_specs=[whole] * 3 + [anywhere] * len(plan),
            out_specs=[whole] * 3,
            out_shape=[
                jax.ShapeDtypeStruct((tokens, features), jnp.float32),
                jax.ShapeDtypeStruct((tokens, features), jnp.bfloat16),
                jax.ShapeDtypeStruct((2 * tokens, length * width), jnp.bfloat16),
            ],
            scratch_shapes=[pltpu.VMEM((length, width, features), jnp.bfloat16), pltpu.SemaphoreType.DMA((length,))],
            compiler_params=pltpu.CompilerParams(vmem_limit_bytes=32 * 1024 * 1024),
            cost_estimate=pl.CostEstimate(
                flops=8 * tokens * features * length * width,
                bytes_accessed=2 * length * width * (features + 4 * tokens),
                transcendentals=0,
            ),
            name="project",
        )(grad_side, mixed, swapped(mixed, range(length)), *weight_pieces)
        mixed_grad = (own_grad + swapped(other_grad, range(length)).astype(jnp.float32)).astype(jnp.bfloat16)
        scattered = lax.psum_scatter(partial_out, "head", scatter_dimension=1, tiled=True)
        mine, theirs = scattered[:tokens], swapped(scattered[tokens:], range(length))
        attended = jnp.where(
            side == 0, jnp.concatenate([mine, theirs], axis=1), jnp.concatenate([theirs, mine], axis=1)
        )
        grad_rows = lax.all_gather(tied(far_rows, other_grad), "head", axis=0, tiled=True)
        mixed_base = tied(mixed, *last)
        up, down = [mixed_base], [mixed_base]
        mixed_pieces = [mixed_base]
        for step in range(1, length):
            up.append(along(up[-1], step, 1, length))
            down.append(along(down[-1], step, -1, length))
            mixed_pieces += [up[-1], down[-1]]
        mixed_grad = tied(mixed_grad, up[1], down[1])
    else:
        partial_out = mm(mixed, full_weight, NT).astype(jnp.bfloat16)
        mixed_grad = mm(grad_full, full_weight, NN).astype(jnp.bfloat16)
        mixed_all = lax.all_gather(mixed, "ctx", axis=0, tiled=True)
        attended = lax.psum_scatter(partial_out, "head", scatter_dimension=1, tiled=True)
    early_bands = [band for o, band in zip(offsets, bands) if o in early]
    dfirst, *early_grads = pl.pallas_call(
        functools.partial(first_kernel, early, per_dev, scale),
        grid=(groups,),
        in_specs=[smem, smem, flat] + [pair] * len(early) + [head_pair, flat, flat, row],
        out_specs=[head_pair] + [pair] * len(early),
        out_shape=[jax.ShapeDtypeStruct((2, BLK, features), jnp.bfloat16)]
        + [jax.ShapeDtypeStruct((2, tokens, features), jnp.bfloat16)] * len(early),
        scratch_shapes=[pltpu.VMEM((tokens, tokens), jnp.float32)],
        compiler_params=pltpu.CompilerParams(vmem_limit_bytes=32 * 1024 * 1024),
        cost_estimate=pl.CostEstimate(
            flops=16 * BLK * tokens * features, bytes_accessed=8 * tokens * features, transcendentals=BLK * tokens * groups
        ),
        name="first_grad",
    )(run_word, block_lists, queries, *early_bands, first, mixed, mixed_grad, lse)

    results = pl.pallas_call(
        functools.partial(bwd_kernel, offsets, early, per_dev, scale),
        grid=(groups,),
        in_specs=[smem, smem, flat, flat, flat] + [pair] * len(offsets) + [head_pair, flat, flat, row],
        out_specs=[flat, pair] + [pair] * (len(offsets) - len(early)),
        out_shape=[
            jax.ShapeDtypeStruct((tokens, features), jnp.bfloat16),
            jax.ShapeDtypeStruct((2, tokens, features), jnp.float32),
        ]
        + [jax.ShapeDtypeStruct((2, tokens, features), jnp.bfloat16)] * (len(offsets) - len(early)),
        scratch_shapes=[pltpu.VMEM((tokens, tokens), jnp.float32)],
        compiler_params=pltpu.CompilerParams(vmem_limit_bytes=40 * 1024 * 1024),
        cost_estimate=pl.CostEstimate(
            flops=10 * keys * tokens * features, bytes_accessed=10 * keys * features, transcendentals=keys * tokens * groups
        ),
        name="attend_grad",
    )(run_word, block_lists, queries, key_heads, value_heads, *bands, first, mixed, mixed_grad, lse)
    query_grad, own = results[:2]
    if direct:
        to_before, to_after, to_beside = results[2:]
        back = [(b, a) for a, b in hop]
        diagonal = lax.ppermute(early_grads[0], "ctx", back).astype(jnp.float32)
        first_sum = dfirst.astype(jnp.float32)
        first_sum = first_sum + lax.ppermute(dfirst, "ctx", [(b, a) for a, b in spread_to]).astype(jnp.float32)
        folded = jnp.pad(jnp.where(run == 2, first_sum, 0.0), ((0, 0), (0, tokens - BLK), (0, 0)))
        to_before = to_before.astype(jnp.float32) + jnp.where(side == 1, diagonal, 0.0) + folded
        to_after = to_after.astype(jnp.float32) + jnp.where(side == 0, diagonal, 0.0)
        near = first_sum.astype(jnp.bfloat16)
        for c in (1, length):
            first_sum = first_sum + lax.ppermute(near, "ctx", [(c, 0)]).astype(jnp.float32)
        sums = own + swapped(to_beside, range(length)).astype(jnp.float32)
        sums = sums + shifted(to_before.astype(jnp.bfloat16), -2).astype(jnp.float32)
        sums = sums + shifted(to_after.astype(jnp.bfloat16), 2).astype(jnp.float32)
    else:
        first_sum = to_first(dfirst.astype(jnp.float32))
        sums = own
        for o, part in zip(offsets, results[2:]):
            sums = sums + shifted(part, o).astype(jnp.float32)
    first_sum = jnp.where(run == 0, first_sum, 0.0)
    sums = sums + jnp.pad(first_sum, ((0, 0), (0, tokens - BLK), (0, 0)))
    key_grad = (sums[0] * scale).astype(jnp.bfloat16)
    value_grad = sums[1].astype(jnp.bfloat16)
    if direct:
        plan = origins(length)
        own_part, other_part = pl.pallas_call(
            functools.partial(weight_kernel, plan, length),
            in_specs=[whole] + [anywhere] * len(plan),
            out_specs=[whole, whole],
            out_shape=[
                jax.ShapeDtypeStruct((width, features), jnp.float32),
                jax.ShapeDtypeStruct((width, features), jnp.bfloat16),
            ],
            scratch_shapes=[pltpu.VMEM((length, tokens, features), jnp.bfloat16), pltpu.SemaphoreType.DMA((length,))],
            compiler_params=pltpu.CompilerParams(vmem_limit_bytes=32 * 1024 * 1024),
            cost_estimate=pl.CostEstimate(
                flops=4 * length * tokens * width * features, bytes_accessed=4 * length * tokens * features, transcendentals=0
            ),
            name="weight_sum",
        )(grad_rows, *mixed_pieces)
        weight_grad = own_part + swapped(other_part, range(length)).astype(jnp.float32)
    else:
        weight_grad = mm(grad_rows, mixed_all, TN)
    return (attended, query_grad, key_grad, value_grad, weight_grad)


def solution(mesh):
    spec = P("ctx", "head")
    return jax.shard_map(
        local,
        mesh=mesh,
        in_specs=(spec, spec, spec, spec, P(), spec),
        out_specs=(spec,) * 5,
        check_vma=False,
    )
```

```python
import functools

import jax
import jax.numpy as jnp
from jax import lax
from jax.experimental import pallas as pl
from jax.experimental.pallas import tpu as pltpu
from jax.sharding import PartitionSpec as P

HD = 128
BLK = 128
REACH = 4

NT = (((1,), (1,)), ((), ()))
TN = (((0,), (0,)), ((), ()))
NN = (((1,), (0,)), ((), ()))


def mm(a, b, dims):
    return lax.dot_general(a, b, dims, preferred_element_type=jnp.float32)


def shifted(x, by):
    peers = lax.axis_size("ctx")
    return lax.ppermute(x, "ctx", [(i, i + by) for i in range(peers) if 0 <= i + by < peers])


def tree_strides(peers):
    strides = []
    stride = 1
    while stride < peers:
        strides.append(stride)
        stride *= 2
    return strides


def from_first(x):
    peers = lax.axis_size("ctx")
    me = lax.axis_index("ctx")
    for stride in reversed(tree_strides(peers)):
        pairs = [(i, i + stride) for i in range(0, peers, 2 * stride) if i + stride < peers]
        got = lax.ppermute(x, "ctx", pairs)
        x = jnp.where(me % (2 * stride) == stride, got, x)
    return x


def to_first(x):
    peers = lax.axis_size("ctx")
    for stride in tree_strides(peers):
        pairs = [(i + stride, i) for i in range(0, peers, 2 * stride) if i + stride < peers]
        x = x + lax.ppermute(x.astype(jnp.bfloat16), "ctx", pairs).astype(x.dtype)
    return x


def line_of(step, by, length):
    return [z for z in range(length) if 0 <= z - step * by < length]


def along(piece, step, by, length):
    pairs = [(2 * (z - by) + n, 2 * z + n) for z in line_of(step, by, length) for n in range(2)]
    return lax.ppermute(piece, "ctx", pairs)


def swapped(piece, places):
    return lax.ppermute(piece, "ctx", [(2 * z + n, 2 * z + 1 - n) for z in places for n in range(2)])


def tied(x, *others):
    return lax.optimization_barrier((x,) + others)[0]


def spread_back(n, length):
    return (n % (length // 2)) * 2 + n // (length // 2)


def origins(length):
    plan = [0]
    for step in range(1, length):
        plan += [step, -step]
    return plan


def start_pieces(plan, length, pieces, held_ref, slot_of, sems):
    place = lax.div(lax.axis_index("ctx"), 2)
    for back, piece in zip(plan, pieces):
        origin = place - back

        def send(piece=piece, origin=origin):
            slot = slot_of(origin)
            pltpu.make_async_copy(piece, held_ref.at[slot], sems.at[slot]).start()

        if back == 0:
            send()
        else:
            pl.when((origin >= 0) & (origin < length))(send)


def grads_kernel(plan, length, grads_ref, *rest):
    pieces = rest[: len(plan)]
    grad_ref, other_ref, rows_ref, held_ref, sems, sem = rest[len(plan) :]
    width = held_ref.shape[1]
    tokens = grad_ref.shape[0]
    rows = pltpu.make_async_copy(grads_ref, rows_ref, sem)
    rows.start()
    start_pieces(plan, length, pieces, held_ref, lambda origin: origin, sems)
    rows.wait()
    total = None
    for b in range(length):
        pltpu.make_async_copy(held_ref.at[b], held_ref.at[b], sems.at[b]).wait()
        part = mm(rows_ref[:, b * width : (b + 1) * width], held_ref[b], NN)
        total = part if total is None else total + part
    grad_ref[...] = total[:tokens]
    other_ref[...] = total[tokens:].astype(jnp.bfloat16)


def outs_kernel(plan, length, mixed_ref, other_ref, *rest):
    pieces = rest[: len(plan)]
    keep_ref, send_ref, held_ref, sems = rest[len(plan) :]
    tokens = mixed_ref.shape[0]
    core = lax.rem(lax.axis_index("head"), 2)
    row = lax.div(lax.axis_index("head"), 2)
    start_pieces(plan, length, pieces, held_ref, lambda origin: origin, sems)
    for b in range(length):
        pltpu.make_async_copy(held_ref.at[b], held_ref.at[b], sems.at[b]).wait()
        mine = mm(mixed_ref[...], held_ref[b], NT).astype(jnp.bfloat16)
        theirs = mm(other_ref[...], held_ref[b], NT).astype(jnp.bfloat16)
        slot = jnp.where(row == b // 2, 0, 1)

        def put(out_ref, mine=mine, theirs=theirs, slot=slot):
            out_ref[slot, :tokens, :] = mine
            out_ref[slot, tokens:, :] = theirs

        pl.when(core == b % 2)(functools.partial(put, keep_ref))
        pl.when(core != b % 2)(functools.partial(put, send_ref))


def finish_kernel(scale, run_ref, own_ref, a_ref, b_ref, c_ref, first_ref, key_ref, value_ref):
    there = jnp.where(run_ref[0] == 0, 1.0, 0.0).astype(jnp.float32)
    for n, out_ref in enumerate((key_ref, value_ref)):
        total = own_ref[n] + a_ref[n].astype(jnp.float32) + b_ref[n].astype(jnp.float32) + c_ref[n].astype(jnp.float32)
        factor = scale if n == 0 else 1.0
        head = total[:BLK] + there * first_ref[n]
        out_ref[:BLK, :] = (head * factor).astype(jnp.bfloat16)
        out_ref[BLK:, :] = (total[BLK:] * factor).astype(jnp.bfloat16)


def weight_kernel(plan, length, far_ref, *rest):
    pieces = rest[: len(plan)]
    own_ref, other_ref, rows_ref, held_ref, sems, sem = rest[len(plan) :]
    rows = pltpu.make_async_copy(far_ref, rows_ref, sem)
    rows.start()
    width = own_ref.shape[0]
    side = lax.rem(lax.axis_index("ctx"), 2)

    def slot_of(origin):
        return lax.rem(origin, length // 2) * 2 + lax.div(origin, length // 2)

    start_pieces(plan, length, pieces, held_ref, slot_of, sems)
    for b in range(length):
        pltpu.make_async_copy(held_ref.at[b], held_ref.at[b], sems.at[b]).wait()
    rows.wait()
    mixed = held_ref[...].reshape(rows_ref.shape[0], -1)
    other = rows_ref[:, pl.ds(pl.multiple_of((1 - side) * width, 128), width)]
    other_ref[...] = mm(other, mixed, TN).astype(jnp.bfloat16)
    own = rows_ref[:, pl.ds(pl.multiple_of(side * width, 128), width)]
    own_ref[...] = mm(own, mixed, TN)


def runs_away(offset, run):
    side = lax.rem(run, 2)
    if offset == "pair":
        return 1 - 2 * side
    if offset == "across":
        return 2 * side - 1
    return offset


def block_bias(lists_ref, run, per_dev, total_blocks, offset, i, j):
    row = run * per_dev + i
    key = (run + runs_away(offset, run)) * per_dev + j
    hit = (key - row <= 1) & (row - key <= 1)
    for n in range(lists_ref.shape[1]):
        hit = hit | (lists_ref[row, n] == key)
    hit = hit & (key >= 1) & (key < total_blocks)
    return jnp.where(hit, 0.0, -jnp.inf).astype(jnp.float32)


def fwd_kernel(offsets, per_dev, scale, run_ref, lists_ref, q_ref, k_ref, v_ref, *rest):
    bands = rest[: len(offsets)]
    first_ref, mixed_ref, lse_ref, s_ref = rest[len(offsets) :]
    total_blocks = lists_ref.shape[0]
    run = run_ref[0]
    q = q_ref[...]
    tokens = q.shape[0]

    def key_of(p):
        return k_ref[...] if p == 0 else bands[p - 1][0]

    def value_of(p):
        return v_ref[...] if p == 0 else bands[p - 1][1]

    places = (0,) + offsets
    top = None
    for p, offset in enumerate(places):
        s = mm(key_of(p), q, NT) * scale
        for j in range(per_dev):
            for i in range(per_dev):
                part = s[j * BLK : (j + 1) * BLK, i * BLK : (i + 1) * BLK]
                part = part + block_bias(lists_ref, run, per_dev, total_blocks, offset, i, j)
                s_ref[p * tokens + j * BLK : p * tokens + (j + 1) * BLK, i * BLK : (i + 1) * BLK] = part
    s_ref[len(places) * tokens :, :] = mm(first_ref[0], q, NT) * scale
    s = s_ref[...]
    top = jnp.max(s, axis=0, keepdims=True)
    e = jnp.exp(s - top)
    total = jnp.sum(e, axis=0, keepdims=True)
    inverse = 1.0 / total
    low = (e * inverse).astype(jnp.bfloat16)
    out = mm(first_ref[1], low[len(places) * tokens :], TN)
    for p in range(len(places)):
        out = out + mm(value_of(p), low[p * tokens : (p + 1) * tokens], TN)
    mixed_ref[...] = out.T.astype(jnp.bfloat16)
    lse_ref[0] = top + jnp.log(total)


def probs_of(lists_ref, s_ref, run, per_dev, s, offset, lse):
    if offset is None:
        return jnp.exp(s - lse)
    for j in range(per_dev):
        for i in range(per_dev):
            part = s[j * BLK : (j + 1) * BLK, i * BLK : (i + 1) * BLK]
            part = part + block_bias(lists_ref, run, per_dev, lists_ref.shape[0], offset, i, j)
            s_ref[j * BLK : (j + 1) * BLK, i * BLK : (i + 1) * BLK] = part
    return jnp.exp(s_ref[...] - lse)


def first_kernel(offsets, per_dev, scale, run_ref, lists_ref, q_ref, *rest):
    bands = rest[: len(offsets)]
    first_ref, mixed_ref, grad_ref, lse_ref, dfirst_ref = rest[len(offsets) : len(offsets) + 5]
    band_outs = rest[len(offsets) + 5 : -1]
    s_ref = rest[-1]
    q = q_ref[...]
    grad = grad_ref[...]
    lse = lse_ref[0]
    product = grad.astype(jnp.float32) * mixed_ref[...].astype(jnp.float32)
    delta = jnp.sum(product.T, axis=0, keepdims=True)
    plan = [(None, first_ref, dfirst_ref)] + list(zip(offsets, bands, band_outs))
    for n, (offset, pair_ref, out_ref) in enumerate(plan):
        p = probs_of(lists_ref, s_ref.at[n], run_ref[0], per_dev, mm(pair_ref[0], q, NT) * scale, offset, lse)
        slopes = (p * (mm(pair_ref[1], grad, NT) - delta)).astype(jnp.bfloat16)
        out_ref[0] = mm(slopes, q, NN).astype(jnp.bfloat16)
        out_ref[1] = mm(p.astype(jnp.bfloat16), grad, NN).astype(jnp.bfloat16)


def bwd_kernel(offsets, early, per_dev, scale, run_ref, lists_ref, q_ref, k_ref, v_ref, *rest):
    bands = rest[: len(offsets)]
    first_ref, mixed_ref, grad_ref, lse_ref = rest[len(offsets) : len(offsets) + 4]
    outs = rest[len(offsets) + 4 :]
    dq_ref, own_ref = outs[:2]
    band_outs = list(outs[2:-1])
    s_ref = outs[-1]
    q = q_ref[...]
    grad = grad_ref[...]
    lse = lse_ref[0]
    product = grad.astype(jnp.float32) * mixed_ref[...].astype(jnp.float32)
    delta = jnp.sum(product.T, axis=0, keepdims=True)
    dq = None
    plan = [(None, first_ref[0], first_ref[1], None)]
    for offset, pair_ref in zip(offsets, bands):
        plan.append((offset, pair_ref[0], pair_ref[1], None if offset in early else band_outs.pop(0)))
    plan.append((0, k_ref[...], v_ref[...], own_ref))
    for n, (offset, key, value, out_ref) in enumerate(plan):
        p = probs_of(lists_ref, s_ref.at[n], run_ref[0], per_dev, mm(key, q, NT) * scale, offset, lse)
        slopes = (p * (mm(value, grad, NT) - delta)).astype(jnp.bfloat16)
        more = mm(key, slopes, TN)
        dq = more if dq is None else dq + more
        if out_ref is not None:
            out_ref[0] = mm(slopes, q, NN).astype(out_ref.dtype)
            out_ref[1] = mm(p.astype(jnp.bfloat16), grad, NN).astype(out_ref.dtype)
    dq_ref[...] = (dq * scale).T.astype(jnp.bfloat16)


def local(queries, key_heads, value_heads, out_weight, block_lists, out_grad):
    scale = HD ** (-0.5)
    tokens, features = queries.shape
    groups = features // HD
    per_dev = tokens // BLK
    ctx = lax.axis_size("ctx")
    head = lax.axis_size("head")
    run = lax.axis_index("ctx")
    column = lax.axis_index("head")
    reach = -(-REACH // per_dev)
    length = ctx // 2
    direct = ctx == 8 and head == length and reach == 2
    place = run // 2
    side = run % 2
    if direct:
        offsets, early = (-2, 2, "pair", "across"), ("across",)
    else:
        offsets, early = tuple(o for o in range(-reach, reach + 1) if o != 0), ()
    places = 1 + len(offsets)
    smem = pl.BlockSpec(memory_space=pltpu.SMEM)
    whole = pl.BlockSpec(memory_space=pltpu.VMEM)
    anywhere = pl.BlockSpec(memory_space=pl.ANY)
    width = out_weight.shape[0]

    both = jnp.stack([key_heads, value_heads])
    head_rows = both[:, :BLK]
    if direct:
        before, after = shifted(both, 2), shifted(both, -2)
        beside = swapped(both, range(length))
        sent = jnp.where(side == 0, after, before)
        hop = [(2 * z, 2 * z + 1) for z in range(length - 1)] + [(2 * z + 1, 2 * z) for z in range(1, length)]
        across = lax.ppermute(sent, "ctx", hop)
        known = jnp.where(run == 1, beside[:, :BLK], head_rows)
        known = jnp.where(run == 2, before[:, :BLK], known)
        known = jnp.where((run == 3) | (run == 4), lax.ppermute(known, "ctx", [(2, 4), (1, 3)]), known)
        first = jnp.where(run > 4, lax.ppermute(known, "ctx", [(4, 6), (2, 5), (3, 7)]), known)
        gather_to = [(3, 1), (5, 4), (6, 2), (7, 0)]

        half = out_grad.shape[1] // 2
        own_half = lax.dynamic_slice_in_dim(out_grad, side * half, half, 1)
        other_half = lax.dynamic_slice_in_dim(out_grad, (1 - side) * half, half, 1)
        other_half = tied(other_half, before, after)
        halves = jnp.concatenate([own_half, swapped(other_half, range(length))], axis=0)
        grad_side = lax.all_gather(halves, "head", axis=1, tiled=True)

        base = tied(out_weight, before, after, beside)
        up, down = [base], [base]
        weight_pieces = [base]
        for step in range(1, length):
            up.append(along(up[-1], step, 1, length))
            down.append(along(down[-1], step, -1, length))
            if step == 1:
                up[1], down[1], across = lax.optimization_barrier((up[1], down[1], across))
            weight_pieces += [up[-1], down[-1]]
        bands = [before, after, beside, across]
        middle = (up[length // 2], down[length // 2])
        last = (up[-1], down[-1])
        sent = tied(out_grad, *middle)
        pairs = []
        for c in range(ctx):
            for h in range(head):
                pairs.append((c * head + h, (2 * h + c % 2) * head + spread_back(c // 2, length)))
        far_rows = lax.ppermute(sent, ("ctx", "head"), pairs)
    else:
        bands = [shifted(both, -o) for o in offsets]
        first = from_first(head_rows)
        grad_full = lax.all_gather(out_grad, "head", axis=1, tiled=True)
        full_weight = lax.all_gather(out_weight, "ctx", axis=0, tiled=True)
        rounds = ctx // head
        mine = jnp.zeros((rounds * tokens, width), jnp.bfloat16)
        for r in range(rounds):
            pairs = []
            for c in range(ctx):
                for h in range(head):
                    pairs.append((c * head + h, (rounds * h + (c + r) % rounds) * head + c // rounds))
            sent = lax.dynamic_slice_in_dim(out_grad, ((run + r) % rounds) * width, width, 1)
            got = lax.ppermute(sent, ("ctx", "head"), pairs)
            mine = lax.dynamic_update_slice_in_dim(mine, got, ((run - r) % rounds) * tokens, 0)
        grad_rows = lax.all_gather(mine, "head", axis=0, tiled=True)

    run_word = run.astype(jnp.int32).reshape(1)
    flat = pl.BlockSpec((tokens, HD), lambda h: (0, h))
    pair = pl.BlockSpec((2, tokens, HD), lambda h: (0, 0, h))
    head_pair = pl.BlockSpec((2, BLK, HD), lambda h: (0, 0, h))
    row = pl.BlockSpec((1, 1, tokens), lambda h: (h, 0, 0))
    keys = places * tokens + BLK
    mixed, lse = pl.pallas_call(
        functools.partial(fwd_kernel, offsets, per_dev, scale),
        grid=(groups,),
        in_specs=[smem, smem, flat, flat, flat] + [pair] * len(offsets) + [head_pair],
        out_specs=[flat, row],
        out_shape=[
            jax.ShapeDtypeStruct((tokens, features), jnp.bfloat16),
            jax.ShapeDtypeStruct((groups, 1, tokens), jnp.float32),
        ],
        scratch_shapes=[pltpu.VMEM((keys, tokens), jnp.float32)],
        compiler_params=pltpu.CompilerParams(vmem_limit_bytes=40 * 1024 * 1024),
        cost_estimate=pl.CostEstimate(
            flops=4 * keys * tokens * features, bytes_accessed=4 * keys * features, transcendentals=keys * tokens * groups
        ),
        name="attend",
    )(run_word, block_lists, queries, key_heads, value_heads, *bands, first)

    if direct:
        plan = origins(length)
        held = [pltpu.VMEM((length, width, features), jnp.bfloat16), pltpu.SemaphoreType.DMA((length,))]
        own_grad, other_grad = pl.pallas_call(
            functools.partial(grads_kernel, plan, length),
            in_specs=[anywhere] * (1 + len(plan)),
            out_specs=[whole] * 2,
            out_shape=[
                jax.ShapeDtypeStruct((tokens, features), jnp.float32),
                jax.ShapeDtypeStruct((tokens, features), jnp.bfloat16),
            ],
            scratch_shapes=[pltpu.VMEM((2 * tokens, length * width), jnp.bfloat16)] + held + [pltpu.SemaphoreType.DMA],
            compiler_params=pltpu.CompilerParams(vmem_limit_bytes=32 * 1024 * 1024),
            cost_estimate=pl.CostEstimate(
                flops=4 * tokens * features * length * width,
                bytes_accessed=2 * length * width * (features + 2 * tokens),
                transcendentals=0,
            ),
            name="project_grad",
        )(grad_side, *weight_pieces)
        mixed_grad = (own_grad + swapped(other_grad, range(length)).astype(jnp.float32)).astype(jnp.bfloat16)
        keep, send = pl.pallas_call(
            functools.partial(outs_kernel, plan, length),
            in_specs=[whole] * 2 + [anywhere] * len(plan),
            out_specs=[whole] * 2,
            out_shape=[jax.ShapeDtypeStruct((2, 2 * tokens, width), jnp.bfloat16)] * 2,
            scratch_shapes=held,
            compiler_params=pltpu.CompilerParams(vmem_limit_bytes=32 * 1024 * 1024),
            cost_estimate=pl.CostEstimate(
                flops=4 * tokens * features * length * width,
                bytes_accessed=2 * length * width * (features + 2 * tokens),
                transcendentals=0,
            ),
            name="project_out",
        )(mixed, swapped(mixed, range(length)), *weight_pieces)
        grad_rows = lax.all_gather(tied(far_rows, other_grad), "head", axis=0, tiled=True)
        mixed_base = tied(mixed, *last)
        up, down = [mixed_base], [mixed_base]
        mixed_pieces = [mixed_base]
        for step in range(1, length):
            up.append(along(up[-1], step, 1, length))
            down.append(along(down[-1], step, -1, length))
            mixed_pieces += [up[-1], down[-1]]
        mixed_grad = tied(mixed_grad, far_rows)
        lse_later = tied(lse, up[1], down[1])
    else:
        partial_out = mm(mixed, full_weight, NT).astype(jnp.bfloat16)
        mixed_grad = mm(grad_full, full_weight, NN).astype(jnp.bfloat16)
        mixed_all = lax.all_gather(mixed, "ctx", axis=0, tiled=True)
        attended = lax.psum_scatter(partial_out, "head", scatter_dimension=1, tiled=True)
        lse_later = lse
    early_bands = [band for o, band in zip(offsets, bands) if o in early]
    dfirst, *early_grads = pl.pallas_call(
        functools.partial(first_kernel, early, per_dev, scale),
        grid=(groups,),
        in_specs=[smem, smem, flat] + [pair] * len(early) + [head_pair, flat, flat, row],
        out_specs=[head_pair] + [pair] * len(early),
        out_shape=[jax.ShapeDtypeStruct((2, BLK, features), jnp.bfloat16)]
        + [jax.ShapeDtypeStruct((2, tokens, features), jnp.bfloat16)] * len(early),
        scratch_shapes=[pltpu.VMEM((1 + len(early), tokens, tokens), jnp.float32)],
        compiler_params=pltpu.CompilerParams(vmem_limit_bytes=32 * 1024 * 1024),
        cost_estimate=pl.CostEstimate(
            flops=16 * BLK * tokens * features, bytes_accessed=8 * tokens * features, transcendentals=BLK * tokens * groups
        ),
        name="first_grad",
    )(run_word, block_lists, queries, *early_bands, first, mixed, mixed_grad, lse)

    results = pl.pallas_call(
        functools.partial(bwd_kernel, offsets, early, per_dev, scale),
        grid=(groups,),
        in_specs=[smem, smem, flat, flat, flat] + [pair] * len(offsets) + [head_pair, flat, flat, row],
        out_specs=[flat, pair] + [pair] * (len(offsets) - len(early)),
        out_shape=[
            jax.ShapeDtypeStruct((tokens, features), jnp.bfloat16),
            jax.ShapeDtypeStruct((2, tokens, features), jnp.float32),
        ]
        + [jax.ShapeDtypeStruct((2, tokens, features), jnp.bfloat16)] * (len(offsets) - len(early)),
        scratch_shapes=[pltpu.VMEM((1 + places, tokens, tokens), jnp.float32)],
        compiler_params=pltpu.CompilerParams(vmem_limit_bytes=40 * 1024 * 1024),
        cost_estimate=pl.CostEstimate(
            flops=10 * keys * tokens * features, bytes_accessed=10 * keys * features, transcendentals=keys * tokens * groups
        ),
        name="attend_grad",
    )(run_word, block_lists, queries, key_heads, value_heads, *bands, first, mixed, mixed_grad, lse_later)
    query_grad, own = results[:2]
    if direct:
        to_before, to_after, to_beside = results[2:]
        back = [(b, a) for a, b in hop]
        diagonal = lax.ppermute(early_grads[0], "ctx", back).astype(jnp.float32)
        first_sum = dfirst.astype(jnp.float32)
        first_sum = first_sum + lax.ppermute(dfirst, "ctx", gather_to).astype(jnp.float32)
        folded = jnp.pad(jnp.where(run == 2, first_sum, 0.0), ((0, 0), (0, tokens - BLK), (0, 0)))
        to_before = to_before.astype(jnp.float32) + jnp.where(side == 1, diagonal, 0.0) + folded
        to_after = to_after.astype(jnp.float32) + jnp.where(side == 0, diagonal, 0.0)
        near = first_sum.astype(jnp.bfloat16)
        for c in (1, length):
            first_sum = first_sum + lax.ppermute(near, "ctx", [(c, 0)]).astype(jnp.float32)
        back_pair = swapped(to_beside, range(length))
        back_down = shifted(to_before.astype(jnp.bfloat16), -2)
        back_up = shifted(to_after.astype(jnp.bfloat16), 2)
        wide = pl.BlockSpec((2, tokens, HD), lambda h: (0, 0, h))
        key_grad, value_grad = pl.pallas_call(
            functools.partial(finish_kernel, scale),
            grid=(groups,),
            in_specs=[smem] + [wide] * 4 + [head_pair],
            out_specs=[flat, flat],
            out_shape=[jax.ShapeDtypeStruct((tokens, features), jnp.bfloat16)] * 2,
            cost_estimate=pl.CostEstimate(flops=16 * tokens * features, bytes_accessed=26 * tokens * features, transcendentals=0),
            name="finish",
        )(run_word, own, back_pair, back_down, back_up, first_sum)

        send = tied(send, query_grad)
        got = lax.ppermute(send, "head", [(h, h ^ 1) for h in range(head)])
        held_sum = keep.astype(jnp.float32) + got.astype(jnp.float32)
        got = lax.ppermute(held_sum[1].astype(jnp.bfloat16), "head", [(h, h ^ 2) for h in range(head)])
        scattered = (held_sum[0] + got.astype(jnp.float32)).astype(jnp.bfloat16)
        mine, theirs = scattered[:tokens], swapped(scattered[tokens:], range(length))
        attended = jnp.where(
            side == 0, jnp.concatenate([mine, theirs], axis=1), jnp.concatenate([theirs, mine], axis=1)
        )
    else:
        first_sum = to_first(dfirst.astype(jnp.float32))
        sums = own
        for o, part in zip(offsets, results[2:]):
            sums = sums + shifted(part, o).astype(jnp.float32)
        first_sum = jnp.where(run == 0, first_sum, 0.0)
        sums = sums + jnp.pad(first_sum, ((0, 0), (0, tokens - BLK), (0, 0)))
        key_grad = (sums[0] * scale).astype(jnp.bfloat16)
        value_grad = sums[1].astype(jnp.bfloat16)
    if direct:
        plan = origins(length)
        own_part, other_part = pl.pallas_call(
            functools.partial(weight_kernel, plan, length),
            in_specs=[anywhere] * (1 + len(plan)),
            out_specs=[whole, whole],
            out_shape=[
                jax.ShapeDtypeStruct((width, features), jnp.float32),
                jax.ShapeDtypeStruct((width, features), jnp.bfloat16),
            ],
            scratch_shapes=[
                pltpu.VMEM((length * tokens, 2 * width), jnp.bfloat16),
                pltpu.VMEM((length, tokens, features), jnp.bfloat16),
                pltpu.SemaphoreType.DMA((length,)),
                pltpu.SemaphoreType.DMA,
            ],
            compiler_params=pltpu.CompilerParams(vmem_limit_bytes=32 * 1024 * 1024),
            cost_estimate=pl.CostEstimate(
                flops=4 * length * tokens * width * features, bytes_accessed=4 * length * tokens * features, transcendentals=0
            ),
            name="weight_sum",
        )(grad_rows, *mixed_pieces)
        weight_grad = own_part + swapped(other_part, range(length)).astype(jnp.float32)
    else:
        weight_grad = mm(grad_rows, mixed_all, TN)
    return (attended, query_grad, key_grad, value_grad, weight_grad)


def solution(mesh):
    spec = P("ctx", "head")
    return jax.shard_map(
        local,
        mesh=mesh,
        in_specs=(spec, spec, spec, spec, P(), spec),
        out_specs=(spec,) * 5,
        check_vma=False,
    )
```

```python
import functools

import jax
import jax.numpy as jnp
from jax import lax
from jax.experimental import pallas as pl
from jax.experimental.pallas import tpu as pltpu
from jax.sharding import PartitionSpec as P

HD = 128
BLK = 128
REACH = 4

CHEAP = pl.CostEstimate(flops=1, bytes_accessed=1, transcendentals=0)

NT = (((1,), (1,)), ((), ()))
TN = (((0,), (0,)), ((), ()))
NN = (((1,), (0,)), ((), ()))


def mm(a, b, dims):
    return lax.dot_general(a, b, dims, preferred_element_type=jnp.float32)


def shifted(x, by):
    peers = lax.axis_size("ctx")
    return lax.ppermute(x, "ctx", [(i, i + by) for i in range(peers) if 0 <= i + by < peers])


def tree_strides(peers):
    strides = []
    stride = 1
    while stride < peers:
        strides.append(stride)
        stride *= 2
    return strides


def from_first(x):
    peers = lax.axis_size("ctx")
    me = lax.axis_index("ctx")
    for stride in reversed(tree_strides(peers)):
        pairs = [(i, i + stride) for i in range(0, peers, 2 * stride) if i + stride < peers]
        got = lax.ppermute(x, "ctx", pairs)
        x = jnp.where(me % (2 * stride) == stride, got, x)
    return x


def to_first(x):
    peers = lax.axis_size("ctx")
    for stride in tree_strides(peers):
        pairs = [(i + stride, i) for i in range(0, peers, 2 * stride) if i + stride < peers]
        x = x + lax.ppermute(x.astype(jnp.bfloat16), "ctx", pairs).astype(x.dtype)
    return x


def turned(x, by, length):
    return lax.ppermute(x, "ctx", [(2 * z + n, 2 * ((z + by) % length) + n) for z in range(length) for n in range(2)])


def swapped(piece, places):
    return lax.ppermute(piece, "ctx", [(2 * z + n, 2 * z + 1 - n) for z in places for n in range(2)])


def tied(x, *others):
    return lax.optimization_barrier((x,) + others)[0]


def start_weights(pieces, held_ref, sems):
    place = lax.div(lax.axis_index("ctx"), 2)
    own, up, down, over, last = pieces
    length = held_ref.shape[0]

    def send(piece, slot):
        pltpu.make_async_copy(piece, held_ref.at[slot], sems.at[slot]).start()

    send(own, place)
    send(over, lax.rem(place + length // 2, length))
    pl.when(place > 0)(lambda: send(up.at[2:], place - 1))
    pl.when(place < length - 1)(lambda: send(down.at[2:], place + 1))
    pl.when((place == 0) | (place == length - 1))(lambda: send(last, length - 1 - place))


def weight_at(held_ref, sems, b):
    pltpu.make_async_copy(held_ref.at[b], held_ref.at[b], sems.at[b]).wait()
    return held_ref[b].reshape(-1, held_ref.shape[-1])


def fetch_rows(own_ref, other_ref, rows_ref, sems):
    tokens = own_ref.shape[0]
    copies = [
        pltpu.make_async_copy(ref, rows_ref.at[n * tokens : (n + 1) * tokens], sems.at[n])
        for n, ref in enumerate((own_ref, other_ref))
    ]
    for copy in copies:
        copy.start()
    return copies


def grads_kernel(length, own_rows_ref, other_rows_ref, *rest):
    pieces = rest[:5]
    grad_ref, other_ref, rows_ref, held_ref, sems, row_sems = rest[5:]
    tokens = grad_ref.shape[0]
    width = rows_ref.shape[1] // length
    copies = fetch_rows(own_rows_ref, other_rows_ref, rows_ref, row_sems)
    start_weights(pieces, held_ref, sems)
    for copy in copies:
        copy.wait()
    total = None
    for b in range(length):
        part = mm(rows_ref[:, b * width : (b + 1) * width], weight_at(held_ref, sems, b), NN)
        total = part if total is None else total + part
    grad_ref[...] = total[:tokens]
    other_ref[...] = total[tokens:].astype(jnp.bfloat16)


def outs_kernel(length, mixed_ref, other_ref, *rest):
    pieces = rest[:5]
    out_ref, held_ref, sems = rest[5:]
    tokens = mixed_ref.shape[0]
    width = out_ref.shape[1] // length
    start_weights(pieces, held_ref, sems)
    for b in range(length):
        weight = weight_at(held_ref, sems, b)
        columns = slice(b * width, (b + 1) * width)
        out_ref[:tokens, columns] = mm(mixed_ref[...], weight, NT).astype(jnp.bfloat16)
        out_ref[tokens:, columns] = mm(other_ref[...], weight, NT).astype(jnp.bfloat16)


def weight_kernel(length, own_rows_ref, other_rows_ref, mixed_ref, other_ref, own_ref, *rest):
    sends = rest[: length - 1]
    rows_ref, both_ref, row_sems = rest[length - 1 :]
    width = own_ref.shape[0]
    tokens = mixed_ref.shape[0]
    place = lax.div(lax.axis_index("ctx"), 2)
    copies = fetch_rows(own_rows_ref, other_rows_ref, rows_ref, row_sems)
    both_ref[:tokens, :] = mixed_ref[...]
    both_ref[tokens:, :] = other_ref[...]
    for copy in copies:
        copy.wait()
    for n, out_ref in enumerate((own_ref,) + sends):
        column = pl.multiple_of(lax.rem(place + n, length) * width, 128)
        out_ref[...] = mm(rows_ref[:, pl.ds(column, width)], both_ref[...], TN).astype(out_ref.dtype)


def finish_kernel(scale, run_ref, own_ref, a_ref, b_ref, c_ref, first_ref, key_ref, value_ref):
    there = jnp.where((run_ref[0] == 0) & (pl.program_id(0) == 0), 1.0, 0.0).astype(jnp.float32)
    for n, out_ref in enumerate((key_ref, value_ref)):
        total = own_ref[n] + a_ref[n].astype(jnp.float32) + b_ref[n].astype(jnp.float32) + c_ref[n].astype(jnp.float32)
        total = total + there * first_ref[n]
        out_ref[...] = (total * (scale if n == 0 else 1.0)).astype(jnp.bfloat16)


def runs_away(offset, run):
    side = lax.rem(run, 2)
    if offset == "pair":
        return 1 - 2 * side
    if offset == "across":
        return 2 * side - 1
    return offset


def block_bias(lists_ref, run, per_dev, total_blocks, offset, i, j):
    row = run * per_dev + i
    key = (run + runs_away(offset, run)) * per_dev + j
    hit = (key - row <= 1) & (row - key <= 1)
    for n in range(lists_ref.shape[1]):
        hit = hit | (lists_ref[row, n] == key)
    hit = hit & (key >= 1) & (key < total_blocks)
    return jnp.where(hit, 0.0, -jnp.inf).astype(jnp.float32)


def fwd_kernel(offsets, per_dev, scale, run_ref, lists_ref, q_ref, k_ref, v_ref, *rest):
    bands = rest[: len(offsets)]
    first_ref, mixed_ref, lse_ref, s_ref = rest[len(offsets) :]
    total_blocks = lists_ref.shape[0]
    run = run_ref[0]
    q = q_ref[...]
    tokens = q.shape[0]

    def key_of(p):
        return k_ref[...] if p == 0 else bands[p - 1][0]

    def value_of(p):
        return v_ref[...] if p == 0 else bands[p - 1][1]

    places = (0,) + offsets
    top = None
    for p, offset in enumerate(places):
        s = mm(key_of(p), q, NT) * scale
        for j in range(per_dev):
            for i in range(per_dev):
                part = s[j * BLK : (j + 1) * BLK, i * BLK : (i + 1) * BLK]
                part = part + block_bias(lists_ref, run, per_dev, total_blocks, offset, i, j)
                s_ref[p * tokens + j * BLK : p * tokens + (j + 1) * BLK, i * BLK : (i + 1) * BLK] = part
    s_ref[len(places) * tokens :, :] = mm(first_ref[0], q, NT) * scale
    s = s_ref[...]
    top = jnp.max(s, axis=0, keepdims=True)
    e = jnp.exp(s - top)
    total = jnp.sum(e, axis=0, keepdims=True)
    inverse = 1.0 / total
    low = (e * inverse).astype(jnp.bfloat16)
    out = mm(first_ref[1], low[len(places) * tokens :], TN)
    for p in range(len(places)):
        out = out + mm(value_of(p), low[p * tokens : (p + 1) * tokens], TN)
    mixed_ref[...] = out.T.astype(jnp.bfloat16)
    lse_ref[0] = top + jnp.log(total)


def probs_of(lists_ref, s_ref, run, per_dev, s, offset, lse):
    if offset is None:
        return jnp.exp(s - lse)
    for j in range(per_dev):
        for i in range(per_dev):
            part = s[j * BLK : (j + 1) * BLK, i * BLK : (i + 1) * BLK]
            part = part + block_bias(lists_ref, run, per_dev, lists_ref.shape[0], offset, i, j)
            s_ref[j * BLK : (j + 1) * BLK, i * BLK : (i + 1) * BLK] = part
    return jnp.exp(s_ref[...] - lse)


def first_kernel(offsets, per_dev, scale, run_ref, lists_ref, q_ref, *rest):
    bands = rest[: len(offsets)]
    first_ref, mixed_ref, grad_ref, lse_ref, dfirst_ref = rest[len(offsets) : len(offsets) + 5]
    band_outs = rest[len(offsets) + 5 : -1]
    s_ref = rest[-1]
    q = q_ref[...]
    grad = grad_ref[...]
    lse = lse_ref[0]
    product = grad.astype(jnp.float32) * mixed_ref[...].astype(jnp.float32)
    delta = jnp.sum(product.T, axis=0, keepdims=True)
    plan = [(None, first_ref, dfirst_ref)] + list(zip(offsets, bands, band_outs))
    for n, (offset, pair_ref, out_ref) in enumerate(plan):
        p = probs_of(lists_ref, s_ref.at[n], run_ref[0], per_dev, mm(pair_ref[0], q, NT) * scale, offset, lse)
        slopes = (p * (mm(pair_ref[1], grad, NT) - delta)).astype(jnp.bfloat16)
        out_ref[0] = mm(slopes, q, NN).astype(jnp.bfloat16)
        out_ref[1] = mm(p.astype(jnp.bfloat16), grad, NN).astype(jnp.bfloat16)


def bwd_kernel(offsets, early, per_dev, scale, run_ref, lists_ref, q_ref, k_ref, v_ref, *rest):
    bands = rest[: len(offsets)]
    first_ref, mixed_ref, grad_ref, lse_ref = rest[len(offsets) : len(offsets) + 4]
    outs = rest[len(offsets) + 4 :]
    dq_ref, own_ref = outs[:2]
    band_outs = list(outs[2:-1])
    s_ref = outs[-1]
    q = q_ref[...]
    grad = grad_ref[...]
    lse = lse_ref[0]
    product = grad.astype(jnp.float32) * mixed_ref[...].astype(jnp.float32)
    delta = jnp.sum(product.T, axis=0, keepdims=True)
    dq = None
    plan = [(None, first_ref[0], first_ref[1], None)]
    for offset, pair_ref in zip(offsets, bands):
        plan.append((offset, pair_ref[0], pair_ref[1], None if offset in early else band_outs.pop(0)))
    plan.append((0, k_ref[...], v_ref[...], own_ref))
    for n, (offset, key, value, out_ref) in enumerate(plan):
        p = probs_of(lists_ref, s_ref.at[n], run_ref[0], per_dev, mm(key, q, NT) * scale, offset, lse)
        slopes = (p * (mm(value, grad, NT) - delta)).astype(jnp.bfloat16)
        more = mm(key, slopes, TN)
        dq = more if dq is None else dq + more
        if out_ref is not None:
            out_ref[0] = mm(slopes, q, NN).astype(out_ref.dtype)
            out_ref[1] = mm(p.astype(jnp.bfloat16), grad, NN).astype(out_ref.dtype)
    dq_ref[...] = (dq * scale).T.astype(jnp.bfloat16)


def local(queries, key_heads, value_heads, out_weight, block_lists, out_grad):
    scale = HD ** (-0.5)
    tokens, features = queries.shape
    groups = features // HD
    per_dev = tokens // BLK
    ctx = lax.axis_size("ctx")
    head = lax.axis_size("head")
    run = lax.axis_index("ctx")
    column = lax.axis_index("head")
    reach = -(-REACH // per_dev)
    length = ctx // 2
    direct = ctx == 8 and head == length and reach == 2 and out_weight.shape[0] == 2 * tokens
    place = run // 2
    side = run % 2
    if direct:
        offsets, early = (-2, 2, "pair", "across"), ("across",)
    else:
        offsets, early = tuple(o for o in range(-reach, reach + 1) if o != 0), ()
    places = 1 + len(offsets)
    smem = pl.BlockSpec(memory_space=pltpu.SMEM)
    whole = pl.BlockSpec(memory_space=pltpu.VMEM)
    anywhere = pl.BlockSpec(memory_space=pl.ANY)
    width = out_weight.shape[0]

    both = jnp.stack([key_heads, value_heads])
    head_rows = both[:, :BLK]
    if direct:
        own_weight = out_weight.reshape(2, tokens, features)
        packed = jnp.concatenate([both, own_weight], axis=0)
        before, after = shifted(packed, 2), shifted(packed, -2)
        beside = swapped(both, range(length))
        sent = jnp.where(side == 0, after[:2], before[:2])
        hop = [(2 * z, 2 * z + 1) for z in range(length - 1)] + [(2 * z + 1, 2 * z) for z in range(1, length)]
        across = lax.ppermute(sent, "ctx", hop)
        known = jnp.where(run == 1, beside[:, :BLK], head_rows)
        known = jnp.where(run == 2, before[:2, :BLK], known)
        known = jnp.where((run == 3) | (run == 4), lax.ppermute(known, "ctx", [(2, 4), (1, 3)]), known)
        first = jnp.where(run > 4, lax.ppermute(known, "ctx", [(4, 6), (2, 5), (3, 7)]), known)
        gather_to = [(3, 1), (5, 4), (6, 2), (7, 0)]

        over = turned(own_weight, 2, length)
        last = lax.ppermute(over, "ctx", [(2 * a + n, 2 * b + n) for a, b in ((1, 0), (2, 3)) for n in range(2)])
        weight_pieces = [own_weight, before, after, over, last]
        grad_full = lax.all_gather(out_grad, "head", axis=1, tiled=True)
        def side_rows(of):
            cuts = [lax.dynamic_slice_in_dim(grad_full, (2 * b + of) * width, width, 1) for b in range(length)]
            return jnp.concatenate(cuts, axis=1)

        own_rows, other_rows = side_rows(side), side_rows(1 - side)
        other_rows = swapped(other_rows, range(length))
        bands = [before, after, beside, across]
    else:
        bands = [shifted(both, -o) for o in offsets]
        first = from_first(head_rows)
        grad_full = lax.all_gather(out_grad, "head", axis=1, tiled=True)
        full_weight = lax.all_gather(out_weight, "ctx", axis=0, tiled=True)
        rounds = ctx // head
        mine = jnp.zeros((rounds * tokens, width), jnp.bfloat16)
        for r in range(rounds):
            pairs = []
            for c in range(ctx):
                for h in range(head):
                    pairs.append((c * head + h, (rounds * h + (c + r) % rounds) * head + c // rounds))
            sent = lax.dynamic_slice_in_dim(out_grad, ((run + r) % rounds) * width, width, 1)
            got = lax.ppermute(sent, ("ctx", "head"), pairs)
            mine = lax.dynamic_update_slice_in_dim(mine, got, ((run - r) % rounds) * tokens, 0)
        grad_rows = lax.all_gather(mine, "head", axis=0, tiled=True)

    run_word = run.astype(jnp.int32).reshape(1)
    flat = pl.BlockSpec((tokens, HD), lambda h: (0, h))
    pair = pl.BlockSpec((2, tokens, HD), lambda h: (0, 0, h))
    head_pair = pl.BlockSpec((2, BLK, HD), lambda h: (0, 0, h))
    row = pl.BlockSpec((1, 1, tokens), lambda h: (h, 0, 0))
    keys = places * tokens + BLK
    mixed, lse = pl.pallas_call(
        functools.partial(fwd_kernel, offsets, per_dev, scale),
        grid=(groups,),
        in_specs=[smem, smem, flat, flat, flat] + [pair] * len(offsets) + [head_pair],
        out_specs=[flat, row],
        out_shape=[
            jax.ShapeDtypeStruct((tokens, features), jnp.bfloat16),
            jax.ShapeDtypeStruct((groups, 1, tokens), jnp.float32),
        ],
        scratch_shapes=[pltpu.VMEM((keys, tokens), jnp.float32)],
        compiler_params=pltpu.CompilerParams(vmem_limit_bytes=40 * 1024 * 1024),
        cost_estimate=CHEAP,
        name="attend",
    )(run_word, block_lists, queries, key_heads, value_heads, *bands, first)

    if direct:
        held = [pltpu.VMEM((length, 2, tokens, features), jnp.bfloat16), pltpu.SemaphoreType.DMA((length,))]
        own_grad, other_grad = pl.pallas_call(
            functools.partial(grads_kernel, length),
            in_specs=[anywhere] * 7,
            out_specs=[whole] * 2,
            out_shape=[
                jax.ShapeDtypeStruct((tokens, features), jnp.float32),
                jax.ShapeDtypeStruct((tokens, features), jnp.bfloat16),
            ],
            scratch_shapes=[pltpu.VMEM((2 * tokens, length * width), jnp.bfloat16)] + held + [pltpu.SemaphoreType.DMA((2,))],
            compiler_params=pltpu.CompilerParams(vmem_limit_bytes=32 * 1024 * 1024),
            cost_estimate=CHEAP,
            name="project_grad",
        )(own_rows, other_rows, *weight_pieces)
        mixed_grad = (own_grad + swapped(other_grad, range(length)).astype(jnp.float32)).astype(jnp.bfloat16)
        mixed_other = tied(swapped(mixed, range(length)), other_grad)
        partial_out = pl.pallas_call(
            functools.partial(outs_kernel, length),
            in_specs=[whole] * 2 + [anywhere] * 5,
            out_specs=whole,
            out_shape=jax.ShapeDtypeStruct((2 * tokens, length * width), jnp.bfloat16),
            scratch_shapes=held,
            compiler_params=pltpu.CompilerParams(vmem_limit_bytes=32 * 1024 * 1024),
            cost_estimate=CHEAP,
            name="project_out",
        )(mixed, mixed_other, *weight_pieces)
        scattered = lax.psum_scatter(partial_out, "head", scatter_dimension=1, tiled=True)
        mine, theirs = scattered[:tokens], swapped(scattered[tokens:], range(length))
        attended = jnp.where(
            side == 0, jnp.concatenate([mine, theirs], axis=1), jnp.concatenate([theirs, mine], axis=1)
        )
        own_part, *weight_parts = pl.pallas_call(
            functools.partial(weight_kernel, length),
            in_specs=[anywhere] * 2 + [whole] * 2,
            out_specs=[whole] * length,
            out_shape=[jax.ShapeDtypeStruct((width, features), jnp.float32)]
            + [jax.ShapeDtypeStruct((width, features), jnp.bfloat16)] * (length - 1),
            scratch_shapes=[
                pltpu.VMEM((2 * tokens, length * width), jnp.bfloat16),
                pltpu.VMEM((2 * tokens, features), jnp.bfloat16),
                pltpu.SemaphoreType.DMA((2,)),
            ],
            compiler_params=pltpu.CompilerParams(vmem_limit_bytes=32 * 1024 * 1024),
            cost_estimate=CHEAP,
            name="weight_part",
        )(own_rows, other_rows, mixed, mixed_other)
        weight_grad = own_part
        for n, part in enumerate(weight_parts):
            weight_grad = weight_grad + turned(part, n + 1, length).astype(jnp.float32)
    else:
        partial_out = mm(mixed, full_weight, NT).astype(jnp.bfloat16)
        mixed_grad = mm(grad_full, full_weight, NN).astype(jnp.bfloat16)
        mixed_all = lax.all_gather(mixed, "ctx", axis=0, tiled=True)
        attended = lax.psum_scatter(partial_out, "head", scatter_dimension=1, tiled=True)
    early_bands = [band for o, band in zip(offsets, bands) if o in early]
    dfirst, *early_grads = pl.pallas_call(
        functools.partial(first_kernel, early, per_dev, scale),
        grid=(groups,),
        in_specs=[smem, smem, flat] + [pair] * len(early) + [head_pair, flat, flat, row],
        out_specs=[head_pair] + [pair] * len(early),
        out_shape=[jax.ShapeDtypeStruct((2, BLK, features), jnp.bfloat16)]
        + [jax.ShapeDtypeStruct((2, tokens, features), jnp.bfloat16)] * len(early),
        scratch_shapes=[pltpu.VMEM((1 + len(early), tokens, tokens), jnp.float32)],
        compiler_params=pltpu.CompilerParams(vmem_limit_bytes=32 * 1024 * 1024),
        cost_estimate=CHEAP,
        name="first_grad",
    )(run_word, block_lists, queries, *early_bands, first, mixed, mixed_grad, lse)

    lse_later = tied(lse, dfirst)
    results = pl.pallas_call(
        functools.partial(bwd_kernel, offsets, early, per_dev, scale),
        grid=(groups,),
        in_specs=[smem, smem, flat, flat, flat] + [pair] * len(offsets) + [head_pair, flat, flat, row],
        out_specs=[flat, pair] + [pair] * (len(offsets) - len(early)),
        out_shape=[
            jax.ShapeDtypeStruct((tokens, features), jnp.bfloat16),
            jax.ShapeDtypeStruct((2, tokens, features), jnp.float32),
        ]
        + [jax.ShapeDtypeStruct((2, tokens, features), jnp.bfloat16)] * (len(offsets) - len(early)),
        scratch_shapes=[pltpu.VMEM((1 + places, tokens, tokens), jnp.float32)],
        compiler_params=pltpu.CompilerParams(vmem_limit_bytes=40 * 1024 * 1024),
        cost_estimate=CHEAP,
        name="attend_grad",
    )(run_word, block_lists, queries, key_heads, value_heads, *bands, first, mixed, mixed_grad, lse_later)
    query_grad, own = results[:2]
    if direct:
        to_before, to_after, to_beside = results[2:]
        back = [(b, a) for a, b in hop]
        diagonal = lax.ppermute(early_grads[0], "ctx", back).astype(jnp.float32)
        first_sum = dfirst.astype(jnp.float32)
        first_sum = first_sum + lax.ppermute(dfirst, "ctx", gather_to).astype(jnp.float32)
        folded = jnp.pad(jnp.where(run == 2, first_sum, 0.0), ((0, 0), (0, tokens - BLK), (0, 0)))
        to_before = to_before.astype(jnp.float32) + jnp.where(side == 1, diagonal, 0.0) + folded
        to_after = to_after.astype(jnp.float32) + jnp.where(side == 0, diagonal, 0.0)
        near = first_sum.astype(jnp.bfloat16)
        for c in (1, length):
            first_sum = first_sum + lax.ppermute(near, "ctx", [(c, 0)]).astype(jnp.float32)
        back_pair = swapped(to_beside, range(length))
        back_down = shifted(to_before.astype(jnp.bfloat16), -2)
        back_up = shifted(to_after.astype(jnp.bfloat16), 2)
        wide = pl.BlockSpec((2, BLK, features), lambda n: (0, n, 0))
        top = pl.BlockSpec((2, BLK, features), lambda n: (0, 0, 0))
        slab = pl.BlockSpec((BLK, features), lambda n: (n, 0))
        key_grad, value_grad = pl.pallas_call(
            functools.partial(finish_kernel, scale),
            grid=(per_dev,),
            in_specs=[smem] + [wide] * 4 + [top],
            out_specs=[slab, slab],
            out_shape=[jax.ShapeDtypeStruct((tokens, features), jnp.bfloat16)] * 2,
            cost_estimate=CHEAP,
            name="finish",
        )(run_word, own, back_pair, back_down, back_up, first_sum)

    else:
        first_sum = to_first(dfirst.astype(jnp.float32))
        sums = own
        for o, part in zip(offsets, results[2:]):
            sums = sums + shifted(part, o).astype(jnp.float32)
        first_sum = jnp.where(run == 0, first_sum, 0.0)
        sums = sums + jnp.pad(first_sum, ((0, 0), (0, tokens - BLK), (0, 0)))
        key_grad = (sums[0] * scale).astype(jnp.bfloat16)
        value_grad = sums[1].astype(jnp.bfloat16)
    if not direct:
        weight_grad = mm(grad_rows, mixed_all, TN)
    return (attended, query_grad, key_grad, value_grad, weight_grad)


def solution(mesh):
    spec = P("ctx", "head")
    return jax.shard_map(
        local,
        mesh=mesh,
        in_specs=(spec, spec, spec, spec, P(), spec),
        out_specs=(spec,) * 5,
        check_vma=False,
    )
```

```python
import functools

import jax
import jax.numpy as jnp
from jax import lax
from jax.experimental import pallas as pl
from jax.experimental.pallas import tpu as pltpu
from jax.sharding import PartitionSpec as P

HD = 128
BLK = 128
REACH = 4

CHEAP = pl.CostEstimate(flops=1, bytes_accessed=1, transcendentals=0)

NT = (((1,), (1,)), ((), ()))
TN = (((0,), (0,)), ((), ()))
NN = (((1,), (0,)), ((), ()))


def mm(a, b, dims):
    return lax.dot_general(a, b, dims, preferred_element_type=jnp.float32)


def shifted(x, by):
    peers = lax.axis_size("ctx")
    return lax.ppermute(x, "ctx", [(i, i + by) for i in range(peers) if 0 <= i + by < peers])


def tree_strides(peers):
    strides = []
    stride = 1
    while stride < peers:
        strides.append(stride)
        stride *= 2
    return strides


def from_first(x):
    peers = lax.axis_size("ctx")
    me = lax.axis_index("ctx")
    for stride in reversed(tree_strides(peers)):
        pairs = [(i, i + stride) for i in range(0, peers, 2 * stride) if i + stride < peers]
        got = lax.ppermute(x, "ctx", pairs)
        x = jnp.where(me % (2 * stride) == stride, got, x)
    return x


def to_first(x):
    peers = lax.axis_size("ctx")
    for stride in tree_strides(peers):
        pairs = [(i + stride, i) for i in range(0, peers, 2 * stride) if i + stride < peers]
        x = x + lax.ppermute(x.astype(jnp.bfloat16), "ctx", pairs).astype(x.dtype)
    return x


def turned(x, by, length):
    return lax.ppermute(x, "ctx", [(2 * z + n, 2 * ((z + by) % length) + n) for z in range(length) for n in range(2)])


def swapped(piece, places):
    return lax.ppermute(piece, "ctx", [(2 * z + n, 2 * z + 1 - n) for z in places for n in range(2)])


def tied(x, *others):
    return lax.optimization_barrier((x,) + others)[0]


def start_weights(pieces, held_ref, sems):
    place = lax.div(lax.axis_index("ctx"), 2)
    own, beside, middle, outer, far, farthest = pieces
    low = place < 2
    inner = (place == 1) | (place == 2)

    def send(piece, slot):
        pltpu.make_async_copy(piece, held_ref.at[slot], sems.at[slot]).start()

    send(own, place)
    send(beside, place + 1 - 2 * lax.rem(place, 2))

    @pl.when(inner)
    def _():
        send(middle, 3 - place)
        send(far, jnp.where(low, 3, 0))

    @pl.when(jnp.logical_not(inner))
    def _():
        send(outer, jnp.where(low, 2, 1))
        send(farthest, 3 - place)


def weight_at(held_ref, sems, b):
    pltpu.make_async_copy(held_ref.at[b], held_ref.at[b], sems.at[b]).wait()
    return held_ref[b]


def grads_kernel(length, rows_hbm_ref, *rest):
    pieces = rest[:6]
    grad_ref, other_ref, rows_ref, held_ref, sems, row_sem = rest[6:]
    tokens = grad_ref.shape[0]
    width = rows_ref.shape[1] // length
    rows = pltpu.make_async_copy(rows_hbm_ref, rows_ref, row_sem)
    rows.start()
    start_weights(pieces, held_ref, sems)
    rows.wait()
    total = None
    for b in range(length):
        part = mm(rows_ref[:, b * width : (b + 1) * width], weight_at(held_ref, sems, b), NN)
        total = part if total is None else total + part
    grad_ref[...] = total[:tokens]
    other_ref[...] = total[tokens:].astype(jnp.bfloat16)


def outs_kernel(length, mixed_ref, other_ref, *rest):
    pieces = rest[:6]
    out_ref, held_ref, sems = rest[6:]
    tokens = mixed_ref.shape[0]
    width = out_ref.shape[1] // length
    start_weights(pieces, held_ref, sems)
    for b in range(length):
        weight = weight_at(held_ref, sems, b)
        columns = slice(b * width, (b + 1) * width)
        out_ref[:tokens, columns] = mm(mixed_ref[...], weight, NT).astype(jnp.bfloat16)
        out_ref[tokens:, columns] = mm(other_ref[...], weight, NT).astype(jnp.bfloat16)


def weight_kernel(length, rows_hbm_ref, mixed_ref, other_ref, own_ref, *rest):
    sends = rest[: length - 1]
    rows_ref, both_ref, row_sem = rest[length - 1 :]
    width = own_ref.shape[0]
    tokens = mixed_ref.shape[0]
    place = lax.div(lax.axis_index("ctx"), 2)
    rows = pltpu.make_async_copy(rows_hbm_ref, rows_ref, row_sem)
    rows.start()
    both_ref[:tokens, :] = mixed_ref[...]
    both_ref[tokens:, :] = other_ref[...]
    rows.wait()
    for n, out_ref in enumerate((own_ref,) + sends):
        column = pl.multiple_of(lax.rem(place + n, length) * width, 128)
        out_ref[...] = mm(rows_ref[:, pl.ds(column, width)], both_ref[...], TN).astype(out_ref.dtype)


def finish_kernel(scale, run_ref, own_ref, a_ref, b_ref, c_ref, first_ref, key_ref, value_ref):
    there = jnp.where((run_ref[0] == 0) & (pl.program_id(0) == 0), 1.0, 0.0).astype(jnp.float32)
    for n, out_ref in enumerate((key_ref, value_ref)):
        total = own_ref[n] + a_ref[n].astype(jnp.float32) + b_ref[n].astype(jnp.float32) + c_ref[n].astype(jnp.float32)
        total = total + there * first_ref[n]
        out_ref[...] = (total * (scale if n == 0 else 1.0)).astype(jnp.bfloat16)


def runs_away(offset, run):
    side = lax.rem(run, 2)
    if offset == "pair":
        return 1 - 2 * side
    if offset == "across":
        return 2 * side - 1
    return offset


def block_bias(lists_ref, run, per_dev, total_blocks, offset, i, j):
    row = run * per_dev + i
    key = (run + runs_away(offset, run)) * per_dev + j
    hit = (key - row <= 1) & (row - key <= 1)
    for n in range(lists_ref.shape[1]):
        hit = hit | (lists_ref[row, n] == key)
    hit = hit & (key >= 1) & (key < total_blocks)
    return jnp.where(hit, 0.0, -jnp.inf).astype(jnp.float32)


def fwd_kernel(offsets, per_dev, scale, run_ref, lists_ref, q_ref, k_ref, v_ref, *rest):
    bands = rest[: len(offsets)]
    first_ref, mixed_ref, lse_ref, s_ref = rest[len(offsets) :]
    total_blocks = lists_ref.shape[0]
    run = run_ref[0]
    q = q_ref[...]
    tokens = q.shape[0]

    def key_of(p):
        return k_ref[...] if p == 0 else bands[p - 1][0]

    def value_of(p):
        return v_ref[...] if p == 0 else bands[p - 1][1]

    places = (0,) + offsets
    top = None
    for p, offset in enumerate(places):
        s = mm(key_of(p), q, NT) * scale
        for j in range(per_dev):
            for i in range(per_dev):
                part = s[j * BLK : (j + 1) * BLK, i * BLK : (i + 1) * BLK]
                part = part + block_bias(lists_ref, run, per_dev, total_blocks, offset, i, j)
                s_ref[p * tokens + j * BLK : p * tokens + (j + 1) * BLK, i * BLK : (i + 1) * BLK] = part
    s_ref[len(places) * tokens :, :] = mm(first_ref[0], q, NT) * scale
    s = s_ref[...]
    top = jnp.max(s, axis=0, keepdims=True)
    e = jnp.exp(s - top)
    total = jnp.sum(e, axis=0, keepdims=True)
    inverse = 1.0 / total
    low = (e * inverse).astype(jnp.bfloat16)
    out = mm(first_ref[1], low[len(places) * tokens :], TN)
    for p in range(len(places)):
        out = out + mm(value_of(p), low[p * tokens : (p + 1) * tokens], TN)
    mixed_ref[...] = out.T.astype(jnp.bfloat16)
    lse_ref[0] = top + jnp.log(total)


def probs_of(lists_ref, s_ref, run, per_dev, s, offset, lse):
    if offset is None:
        return jnp.exp(s - lse)
    for j in range(per_dev):
        for i in range(per_dev):
            part = s[j * BLK : (j + 1) * BLK, i * BLK : (i + 1) * BLK]
            part = part + block_bias(lists_ref, run, per_dev, lists_ref.shape[0], offset, i, j)
            s_ref[j * BLK : (j + 1) * BLK, i * BLK : (i + 1) * BLK] = part
    return jnp.exp(s_ref[...] - lse)


def first_kernel(offsets, per_dev, scale, run_ref, lists_ref, q_ref, *rest):
    bands = rest[: len(offsets)]
    first_ref, mixed_ref, grad_ref, lse_ref, out_ref, s_ref = rest[len(offsets) :]
    q = q_ref[...]
    grad = grad_ref[...]
    lse = lse_ref[0]
    product = grad.astype(jnp.float32) * mixed_ref[...].astype(jnp.float32)
    delta = jnp.sum(product.T, axis=0, keepdims=True)
    at = 0
    for n, (offset, pair_ref) in enumerate(zip(tuple(offsets) + (None,), bands + (first_ref,))):
        p = probs_of(lists_ref, s_ref.at[n], run_ref[0], per_dev, mm(pair_ref[0], q, NT) * scale, offset, lse)
        slopes = (p * (mm(pair_ref[1], grad, NT) - delta)).astype(jnp.bfloat16)
        rows = slice(at, at + pair_ref.shape[1])
        at = rows.stop
        out_ref[0, rows, :] = mm(slopes, q, NN).astype(jnp.bfloat16)
        out_ref[1, rows, :] = mm(p.astype(jnp.bfloat16), grad, NN).astype(jnp.bfloat16)


def bwd_kernel(offsets, early, per_dev, scale, run_ref, lists_ref, q_ref, k_ref, v_ref, *rest):
    bands = rest[: len(offsets)]
    first_ref, mixed_ref, grad_ref, lse_ref = rest[len(offsets) : len(offsets) + 4]
    outs = rest[len(offsets) + 4 :]
    dq_ref, own_ref = outs[:2]
    band_outs = list(outs[2:-1])
    s_ref = outs[-1]
    q = q_ref[...]
    grad = grad_ref[...]
    lse = lse_ref[0]
    product = grad.astype(jnp.float32) * mixed_ref[...].astype(jnp.float32)
    delta = jnp.sum(product.T, axis=0, keepdims=True)
    dq = None
    plan = [(None, first_ref[0], first_ref[1], None)]
    for offset, pair_ref in zip(offsets, bands):
        plan.append((offset, pair_ref[0], pair_ref[1], None if offset in early else band_outs.pop(0)))
    plan.append((0, k_ref[...], v_ref[...], own_ref))
    for n, (offset, key, value, out_ref) in enumerate(plan):
        p = probs_of(lists_ref, s_ref.at[n], run_ref[0], per_dev, mm(key, q, NT) * scale, offset, lse)
        slopes = (p * (mm(value, grad, NT) - delta)).astype(jnp.bfloat16)
        more = mm(key, slopes, TN)
        dq = more if dq is None else dq + more
        if out_ref is not None:
            out_ref[0] = mm(slopes, q, NN).astype(out_ref.dtype)
            out_ref[1] = mm(p.astype(jnp.bfloat16), grad, NN).astype(out_ref.dtype)
    dq_ref[...] = (dq * scale).T.astype(jnp.bfloat16)


def local(queries, key_heads, value_heads, out_weight, block_lists, out_grad):
    scale = HD ** (-0.5)
    tokens, features = queries.shape
    groups = features // HD
    per_dev = tokens // BLK
    ctx = lax.axis_size("ctx")
    head = lax.axis_size("head")
    run = lax.axis_index("ctx")
    column = lax.axis_index("head")
    reach = -(-REACH // per_dev)
    length = ctx // 2
    direct = ctx == 8 and head == length and reach == 2 and out_grad.shape[1] == 2 * features
    place = run // 2
    side = run % 2
    if direct:
        offsets, early = (-2, 2, "pair", "across"), ("across",)
    else:
        offsets, early = tuple(o for o in range(-reach, reach + 1) if o != 0), ()
    places = 1 + len(offsets)
    smem = pl.BlockSpec(memory_space=pltpu.SMEM)
    whole = pl.BlockSpec(memory_space=pltpu.VMEM)
    anywhere = pl.BlockSpec(memory_space=pl.ANY)
    width = out_weight.shape[0]

    both = jnp.stack([key_heads, value_heads])
    head_rows = both[:, :BLK]
    if direct:
        half = out_grad.shape[1] // 2
        own_half = lax.dynamic_slice_in_dim(out_grad, side * half, half, 1)
        other_half = lax.dynamic_slice_in_dim(out_grad, (1 - side) * half, half, 1)
        before, after = shifted(both, 2), shifted(both, -2)
        beside = swapped(jnp.concatenate([both, other_half[None]], axis=0), range(length))
        grad_side = lax.all_gather(jnp.concatenate([own_half, beside[2]], axis=0), "head", axis=1, tiled=True)
        sent = jnp.where(side == 0, after, before)
        hop = [(2 * z, 2 * z + 1) for z in range(length - 1)] + [(2 * z + 1, 2 * z) for z in range(1, length)]
        across = lax.ppermute(sent, "ctx", hop)
        known = jnp.where(run == 1, beside[:2, :BLK], head_rows)
        known = jnp.where(run == 2, before[:, :BLK], known)
        known = jnp.where((run == 3) | (run == 4), lax.ppermute(known, "ctx", [(2, 4), (1, 3)]), known)
        first = jnp.where(run > 4, lax.ppermute(known, "ctx", [(4, 6), (2, 5), (3, 7)]), known)

        def between(x, places):
            return lax.ppermute(x, "ctx", [(2 * a + n, 2 * b + n) for a, b in places for n in range(2)])

        base = tied(out_weight, before, after)
        near = between(base, ((0, 1), (1, 0), (2, 3), (3, 2)))
        middle = between(base, ((1, 2), (2, 1)))
        far = between(near, ((1, 2), (2, 1)))
        outer = between(middle, ((1, 0), (2, 3)))
        farthest = between(far, ((1, 0), (2, 3)))
        weight_pieces = [base, near, middle, outer, far, farthest]
        bands = [before, after, beside, across]
    else:
        bands = [shifted(both, -o) for o in offsets]
        first = from_first(head_rows)
        grad_full = lax.all_gather(out_grad, "head", axis=1, tiled=True)
        full_weight = lax.all_gather(out_weight, "ctx", axis=0, tiled=True)
        rounds = ctx // head
        mine = jnp.zeros((rounds * tokens, width), jnp.bfloat16)
        for r in range(rounds):
            pairs = []
            for c in range(ctx):
                for h in range(head):
                    pairs.append((c * head + h, (rounds * h + (c + r) % rounds) * head + c // rounds))
            sent = lax.dynamic_slice_in_dim(out_grad, ((run + r) % rounds) * width, width, 1)
            got = lax.ppermute(sent, ("ctx", "head"), pairs)
            mine = lax.dynamic_update_slice_in_dim(mine, got, ((run - r) % rounds) * tokens, 0)
        grad_rows = lax.all_gather(mine, "head", axis=0, tiled=True)

    run_word = run.astype(jnp.int32).reshape(1)
    flat = pl.BlockSpec((tokens, HD), lambda h: (0, h))
    pair = pl.BlockSpec((2, tokens, HD), lambda h: (0, 0, h))
    head_pair = pl.BlockSpec((2, BLK, HD), lambda h: (0, 0, h))
    row = pl.BlockSpec((1, 1, tokens), lambda h: (h, 0, 0))
    keys = places * tokens + BLK
    mixed, lse = pl.pallas_call(
        functools.partial(fwd_kernel, offsets, per_dev, scale),
        grid=(groups,),
        in_specs=[smem, smem, flat, flat, flat] + [pair] * len(offsets) + [head_pair],
        out_specs=[flat, row],
        out_shape=[
            jax.ShapeDtypeStruct((tokens, features), jnp.bfloat16),
            jax.ShapeDtypeStruct((groups, 1, tokens), jnp.float32),
        ],
        scratch_shapes=[pltpu.VMEM((keys, tokens), jnp.float32)],
        compiler_params=pltpu.CompilerParams(vmem_limit_bytes=40 * 1024 * 1024),
        cost_estimate=CHEAP,
        name="attend",
    )(run_word, block_lists, queries, key_heads, value_heads, *bands, first)

    if direct:
        held = [pltpu.VMEM((length, width, features), jnp.bfloat16), pltpu.SemaphoreType.DMA((length,))]
        own_grad, other_grad = pl.pallas_call(
            functools.partial(grads_kernel, length),
            in_specs=[anywhere] * 7,
            out_specs=[whole] * 2,
            out_shape=[
                jax.ShapeDtypeStruct((tokens, features), jnp.float32),
                jax.ShapeDtypeStruct((tokens, features), jnp.bfloat16),
            ],
            scratch_shapes=[pltpu.VMEM((2 * tokens, length * width), jnp.bfloat16)] + held + [pltpu.SemaphoreType.DMA],
            compiler_params=pltpu.CompilerParams(vmem_limit_bytes=32 * 1024 * 1024),
            cost_estimate=CHEAP,
            name="project_grad",
        )(grad_side, *weight_pieces)
        mixed_grad = (own_grad + swapped(other_grad, range(length)).astype(jnp.float32)).astype(jnp.bfloat16)
        mixed_other = tied(swapped(mixed, range(length)), other_grad)
        partial_out = pl.pallas_call(
            functools.partial(outs_kernel, length),
            in_specs=[whole] * 2 + [anywhere] * 6,
            out_specs=pl.BlockSpec((2 * tokens, length * width), lambda: (0, 0)),
            out_shape=jax.ShapeDtypeStruct((2 * tokens, length * width), jnp.bfloat16),
            scratch_shapes=held,
            compiler_params=pltpu.CompilerParams(vmem_limit_bytes=32 * 1024 * 1024),
            cost_estimate=CHEAP,
            name="project_out",
        )(mixed, mixed_other, *weight_pieces)
        scattered = lax.psum_scatter(partial_out, "head", scatter_dimension=1, tiled=True)
        mine, theirs = scattered[:tokens], swapped(scattered[tokens:], range(length))
        attended = jnp.where(
            side == 0, jnp.concatenate([mine, theirs], axis=1), jnp.concatenate([theirs, mine], axis=1)
        )
        own_part, *weight_parts = pl.pallas_call(
            functools.partial(weight_kernel, length),
            in_specs=[anywhere] + [whole] * 2,
            out_specs=[whole] * length,
            out_shape=[jax.ShapeDtypeStruct((width, features), jnp.float32)]
            + [jax.ShapeDtypeStruct((width, features), jnp.bfloat16)] * (length - 1),
            scratch_shapes=[
                pltpu.VMEM((2 * tokens, length * width), jnp.bfloat16),
                pltpu.VMEM((2 * tokens, features), jnp.bfloat16),
                pltpu.SemaphoreType.DMA,
            ],
            compiler_params=pltpu.CompilerParams(vmem_limit_bytes=32 * 1024 * 1024),
            cost_estimate=CHEAP,
            name="weight_part",
        )(grad_side, mixed, mixed_other)
        mixed_grad = tied(mixed_grad, own_part, partial_out)
        weight_turns = [turned(part, n + 1, length) for n, part in enumerate(weight_parts)]
        weight_grad = own_part
        for part in weight_turns:
            weight_grad = weight_grad + part.astype(jnp.float32)
    else:
        partial_out = mm(mixed, full_weight, NT).astype(jnp.bfloat16)
        mixed_grad = mm(grad_full, full_weight, NN).astype(jnp.bfloat16)
        mixed_all = lax.all_gather(mixed, "ctx", axis=0, tiled=True)
        attended = lax.psum_scatter(partial_out, "head", scatter_dimension=1, tiled=True)
    early_bands = [band for o, band in zip(offsets, bands) if o in early]
    early_rows = len(early) * tokens + BLK
    early_grads = pl.pallas_call(
        functools.partial(first_kernel, early, per_dev, scale),
        grid=(groups,),
        in_specs=[smem, smem, flat] + [pair] * len(early) + [head_pair, flat, flat, row],
        out_specs=pl.BlockSpec((2, early_rows, HD), lambda h: (0, 0, h)),
        out_shape=jax.ShapeDtypeStruct((2, early_rows, features), jnp.bfloat16),
        scratch_shapes=[pltpu.VMEM((1 + len(early), tokens, tokens), jnp.float32)],
        compiler_params=pltpu.CompilerParams(vmem_limit_bytes=32 * 1024 * 1024),
        cost_estimate=pl.CostEstimate(flops=10_000_000_000, bytes_accessed=1, transcendentals=0),
        name="first_grad",
    )(run_word, block_lists, queries, *early_bands, first, mixed, mixed_grad, lse)

    lse_later = tied(lse, early_grads)
    results = pl.pallas_call(
        functools.partial(bwd_kernel, offsets, early, per_dev, scale),
        grid=(groups,),
        in_specs=[smem, smem, flat, flat, flat] + [pair] * len(offsets) + [head_pair, flat, flat, row],
        out_specs=[flat, pair] + [pair] * (len(offsets) - len(early)),
        out_shape=[
            jax.ShapeDtypeStruct((tokens, features), jnp.bfloat16),
            jax.ShapeDtypeStruct((2, tokens, features), jnp.float32),
        ]
        + [jax.ShapeDtypeStruct((2, tokens, features), jnp.bfloat16)] * (len(offsets) - len(early)),
        scratch_shapes=[pltpu.VMEM((1 + places, tokens, tokens), jnp.float32)],
        compiler_params=pltpu.CompilerParams(vmem_limit_bytes=40 * 1024 * 1024),
        cost_estimate=pl.CostEstimate(flops=30_000_000_000, bytes_accessed=1, transcendentals=0),
        name="attend_grad",
    )(run_word, block_lists, queries, key_heads, value_heads, *bands, first, mixed, mixed_grad, lse_later)
    query_grad, own = results[:2]
    if direct:
        to_before, to_after, to_beside = results[2:]
        swap = tied(swapped(early_grads, range(length)), query_grad)
        diagonal = swap[:, :tokens].astype(jnp.float32)
        first_sum = early_grads[:, tokens:].astype(jnp.float32) + swap[:, tokens:].astype(jnp.float32)
        folded = jnp.pad(jnp.where(run == 2, first_sum, 0.0), ((0, 0), (0, tokens - BLK), (0, 0)))
        to_before, to_after, _ = lax.optimization_barrier((to_before, to_after, weight_turns[0::2]))
        to_before = to_before.astype(jnp.float32) + jnp.where(side == 1, diagonal, 0.0) + folded
        to_after = to_after.astype(jnp.float32) + jnp.where(side == 0, diagonal, 0.0)
        near = first_sum.astype(jnp.bfloat16)
        for c in range(length, ctx, 2):
            first_sum = first_sum + lax.ppermute(near, "ctx", [(c, 0)]).astype(jnp.float32)
        back_pair = swapped(to_beside, range(length))
        back_down = shifted(to_before.astype(jnp.bfloat16), -2)
        back_up = shifted(to_after.astype(jnp.bfloat16), 2)
        wide = pl.BlockSpec((2, BLK, features), lambda n: (0, n, 0))
        top = pl.BlockSpec((2, BLK, features), lambda n: (0, 0, 0))
        slab = pl.BlockSpec((BLK, features), lambda n: (n, 0))
        key_grad, value_grad = pl.pallas_call(
            functools.partial(finish_kernel, scale),
            grid=(per_dev,),
            in_specs=[smem] + [wide] * 4 + [top],
            out_specs=[slab, slab],
            out_shape=[jax.ShapeDtypeStruct((tokens, features), jnp.bfloat16)] * 2,
            cost_estimate=CHEAP,
            name="finish",
        )(run_word, own, back_pair, back_down, back_up, first_sum)

    else:
        first_sum = to_first(early_grads.astype(jnp.float32))
        sums = own
        for o, part in zip(offsets, results[2:]):
            sums = sums + shifted(part, o).astype(jnp.float32)
        first_sum = jnp.where(run == 0, first_sum, 0.0)
        sums = sums + jnp.pad(first_sum, ((0, 0), (0, tokens - BLK), (0, 0)))
        key_grad = (sums[0] * scale).astype(jnp.bfloat16)
        value_grad = sums[1].astype(jnp.bfloat16)
    if not direct:
        weight_grad = mm(grad_rows, mixed_all, TN)
    return (attended, query_grad, key_grad, value_grad, weight_grad)


def solution(mesh):
    spec = P("ctx", "head")
    return jax.shard_map(
        local,
        mesh=mesh,
        in_specs=(spec, spec, spec, spec, P(), spec),
        out_specs=(spec,) * 5,
        check_vma=False,
    )
```

```python
import functools

import jax
import jax.numpy as jnp
from jax import lax
from jax.experimental import pallas as pl
from jax.experimental.pallas import tpu as pltpu
from jax.sharding import PartitionSpec as P

HD = 128
BLK = 128
REACH = 4

CHEAP = pl.CostEstimate(flops=1, bytes_accessed=1, transcendentals=0)

NT = (((1,), (1,)), ((), ()))
TN = (((0,), (0,)), ((), ()))
NN = (((1,), (0,)), ((), ()))


def mm(a, b, dims):
    return lax.dot_general(a, b, dims, preferred_element_type=jnp.float32)


def shifted(x, by):
    peers = lax.axis_size("ctx")
    return lax.ppermute(x, "ctx", [(i, i + by) for i in range(peers) if 0 <= i + by < peers])


def tree_strides(peers):
    strides = []
    stride = 1
    while stride < peers:
        strides.append(stride)
        stride *= 2
    return strides


def from_first(x):
    peers = lax.axis_size("ctx")
    me = lax.axis_index("ctx")
    for stride in reversed(tree_strides(peers)):
        pairs = [(i, i + stride) for i in range(0, peers, 2 * stride) if i + stride < peers]
        got = lax.ppermute(x, "ctx", pairs)
        x = jnp.where(me % (2 * stride) == stride, got, x)
    return x


def to_first(x):
    peers = lax.axis_size("ctx")
    for stride in tree_strides(peers):
        pairs = [(i + stride, i) for i in range(0, peers, 2 * stride) if i + stride < peers]
        x = x + lax.ppermute(x.astype(jnp.bfloat16), "ctx", pairs).astype(x.dtype)
    return x


def turned(x, by, length):
    return lax.ppermute(x, "ctx", [(2 * z + n, 2 * ((z + by) % length) + n) for z in range(length) for n in range(2)])


def swapped(piece, places):
    return lax.ppermute(piece, "ctx", [(2 * z + n, 2 * z + 1 - n) for z in places for n in range(2)])


def tied(x, *others):
    return lax.optimization_barrier((x,) + others)[0]


def start_weights(pieces, held_ref, sems):
    place = lax.div(lax.axis_index("ctx"), 2)
    own, beside, middle, outer, far, farthest = pieces
    low = place < 2
    inner = (place == 1) | (place == 2)

    def send(piece, slot):
        pltpu.make_async_copy(piece, held_ref.at[slot], sems.at[slot]).start()

    send(own, place)
    send(beside, place + 1 - 2 * lax.rem(place, 2))

    @pl.when(inner)
    def _():
        send(middle, 3 - place)
        send(far, jnp.where(low, 3, 0))

    @pl.when(jnp.logical_not(inner))
    def _():
        send(outer, jnp.where(low, 2, 1))
        send(farthest, 3 - place)


def weight_at(held_ref, sems, b):
    pltpu.make_async_copy(held_ref.at[b], held_ref.at[b], sems.at[b]).wait()
    return held_ref[b]


def grads_kernel(length, rows_hbm_ref, *rest):
    pieces = rest[:6]
    grad_ref, other_ref, rows_ref, held_ref, sems, row_sem = rest[6:]
    tokens = grad_ref.shape[0]
    width = rows_ref.shape[1] // length
    rows = pltpu.make_async_copy(rows_hbm_ref, rows_ref, row_sem)
    rows.start()
    start_weights(pieces, held_ref, sems)
    rows.wait()
    total = None
    for b in range(length):
        part = mm(rows_ref[:, b * width : (b + 1) * width], weight_at(held_ref, sems, b), NN)
        total = part if total is None else total + part
    grad_ref[...] = total[:tokens]
    other_ref[...] = total[tokens:].astype(jnp.bfloat16)


def outs_kernel(length, mixed_ref, other_ref, *rest):
    pieces = rest[:6]
    out_ref, held_ref, sems = rest[6:]
    tokens = mixed_ref.shape[0]
    width = out_ref.shape[1] // length
    start_weights(pieces, held_ref, sems)
    for b in range(length):
        weight = weight_at(held_ref, sems, b)
        columns = slice(b * width, (b + 1) * width)
        out_ref[:tokens, columns] = mm(mixed_ref[...], weight, NT).astype(jnp.bfloat16)
        out_ref[tokens:, columns] = mm(other_ref[...], weight, NT).astype(jnp.bfloat16)


def weight_kernel(length, rows_hbm_ref, mixed_ref, other_ref, own_ref, *rest):
    sends = rest[: length - 1]
    rows_ref, both_ref, row_sem = rest[length - 1 :]
    width = own_ref.shape[0]
    tokens = mixed_ref.shape[0]
    place = lax.div(lax.axis_index("ctx"), 2)
    rows = pltpu.make_async_copy(rows_hbm_ref, rows_ref, row_sem)
    rows.start()
    both_ref[:tokens, :] = mixed_ref[...]
    both_ref[tokens:, :] = other_ref[...]
    rows.wait()
    for n, out_ref in enumerate((own_ref,) + sends):
        column = pl.multiple_of(lax.rem(place + n, length) * width, 128)
        out_ref[...] = mm(rows_ref[:, pl.ds(column, width)], both_ref[...], TN).astype(out_ref.dtype)


def finish_kernel(scale, run_ref, own_ref, a_ref, b_ref, c_ref, first_ref, key_ref, value_ref):
    there = jnp.where((run_ref[0] == 0) & (pl.program_id(0) == 0), 1.0, 0.0).astype(jnp.float32)
    for n, out_ref in enumerate((key_ref, value_ref)):
        total = own_ref[n] + a_ref[n].astype(jnp.float32) + b_ref[n].astype(jnp.float32) + c_ref[n].astype(jnp.float32)
        total = total + there * first_ref[n]
        out_ref[...] = (total * (scale if n == 0 else 1.0)).astype(jnp.bfloat16)


def runs_away(offset, run):
    side = lax.rem(run, 2)
    if offset == "pair":
        return 1 - 2 * side
    if offset == "across":
        return 2 * side - 1
    return offset


def block_bias(lists_ref, run, per_dev, total_blocks, offset, i, j):
    row = run * per_dev + i
    key = (run + runs_away(offset, run)) * per_dev + j
    hit = (key - row <= 1) & (row - key <= 1)
    for n in range(lists_ref.shape[1]):
        hit = hit | (lists_ref[row, n] == key)
    hit = hit & (key >= 1) & (key < total_blocks)
    return jnp.where(hit, 0.0, -jnp.inf).astype(jnp.float32)


def fwd_kernel(offsets, per_dev, scale, run_ref, lists_ref, q_ref, k_ref, v_ref, *rest):
    bands = rest[: len(offsets)]
    first_ref, mixed_ref, lse_ref, s_ref = rest[len(offsets) :]
    total_blocks = lists_ref.shape[0]
    run = run_ref[0]
    q = q_ref[...]
    tokens = q.shape[0]

    def key_of(p):
        return k_ref[...] if p == 0 else bands[p - 1][0]

    def value_of(p):
        return v_ref[...] if p == 0 else bands[p - 1][1]

    places = (0,) + offsets
    top = None
    for p, offset in enumerate(places):
        s = mm(key_of(p), q, NT) * scale
        for j in range(per_dev):
            for i in range(per_dev):
                part = s[j * BLK : (j + 1) * BLK, i * BLK : (i + 1) * BLK]
                part = part + block_bias(lists_ref, run, per_dev, total_blocks, offset, i, j)
                s_ref[p * tokens + j * BLK : p * tokens + (j + 1) * BLK, i * BLK : (i + 1) * BLK] = part
    s_ref[len(places) * tokens :, :] = mm(first_ref[0], q, NT) * scale
    s = s_ref[...]
    top = jnp.max(s, axis=0, keepdims=True)
    e = jnp.exp(s - top)
    total = jnp.sum(e, axis=0, keepdims=True)
    inverse = 1.0 / total
    low = (e * inverse).astype(jnp.bfloat16)
    out = mm(first_ref[1], low[len(places) * tokens :], TN)
    for p in range(len(places)):
        out = out + mm(value_of(p), low[p * tokens : (p + 1) * tokens], TN)
    mixed_ref[...] = out.T.astype(jnp.bfloat16)
    lse_ref[0] = top + jnp.log(total)


def probs_of(lists_ref, s_ref, run, per_dev, s, offset, lse):
    if offset is None:
        return jnp.exp(s - lse)
    for j in range(per_dev):
        for i in range(per_dev):
            part = s[j * BLK : (j + 1) * BLK, i * BLK : (i + 1) * BLK]
            part = part + block_bias(lists_ref, run, per_dev, lists_ref.shape[0], offset, i, j)
            s_ref[j * BLK : (j + 1) * BLK, i * BLK : (i + 1) * BLK] = part
    return jnp.exp(s_ref[...] - lse)


def first_kernel(offsets, per_dev, scale, run_ref, lists_ref, q_ref, *rest):
    bands = rest[: len(offsets)]
    first_ref, mixed_ref, grad_ref, lse_ref, out_ref, s_ref = rest[len(offsets) :]
    q = q_ref[...]
    grad = grad_ref[...]
    lse = lse_ref[0]
    product = grad.astype(jnp.float32) * mixed_ref[...].astype(jnp.float32)
    delta = jnp.sum(product.T, axis=0, keepdims=True)
    at = 0
    for n, (offset, pair_ref) in enumerate(zip(tuple(offsets) + (None,), bands + (first_ref,))):
        p = probs_of(lists_ref, s_ref.at[n], run_ref[0], per_dev, mm(pair_ref[0], q, NT) * scale, offset, lse)
        slopes = (p * (mm(pair_ref[1], grad, NT) - delta)).astype(jnp.bfloat16)
        rows = slice(at, at + pair_ref.shape[1])
        at = rows.stop
        out_ref[0, rows, :] = mm(slopes, q, NN).astype(jnp.bfloat16)
        out_ref[1, rows, :] = mm(p.astype(jnp.bfloat16), grad, NN).astype(jnp.bfloat16)


def bwd_kernel(offsets, early, per_dev, scale, run_ref, lists_ref, q_ref, k_ref, v_ref, *rest):
    bands = rest[: len(offsets)]
    first_ref, mixed_ref, grad_ref, lse_ref = rest[len(offsets) : len(offsets) + 4]
    outs = rest[len(offsets) + 4 :]
    dq_ref, own_ref = outs[:2]
    band_outs = list(outs[2:-1])
    s_ref = outs[-1]
    q = q_ref[...]
    grad = grad_ref[...]
    lse = lse_ref[0]
    product = grad.astype(jnp.float32) * mixed_ref[...].astype(jnp.float32)
    delta = jnp.sum(product.T, axis=0, keepdims=True)
    dq = None
    plan = [(None, first_ref[0], first_ref[1], None)]
    for offset, pair_ref in zip(offsets, bands):
        plan.append((offset, pair_ref[0], pair_ref[1], None if offset in early else band_outs.pop(0)))
    plan.append((0, k_ref[...], v_ref[...], own_ref))
    for n, (offset, key, value, out_ref) in enumerate(plan):
        p = probs_of(lists_ref, s_ref.at[n], run_ref[0], per_dev, mm(key, q, NT) * scale, offset, lse)
        slopes = (p * (mm(value, grad, NT) - delta)).astype(jnp.bfloat16)
        more = mm(key, slopes, TN)
        dq = more if dq is None else dq + more
        if out_ref is not None:
            out_ref[0] = mm(slopes, q, NN).astype(out_ref.dtype)
            out_ref[1] = mm(p.astype(jnp.bfloat16), grad, NN).astype(out_ref.dtype)
    dq_ref[...] = (dq * scale).T.astype(jnp.bfloat16)


def local(queries, key_heads, value_heads, out_weight, block_lists, out_grad):
    scale = HD ** (-0.5)
    tokens, features = queries.shape
    groups = features // HD
    per_dev = tokens // BLK
    ctx = lax.axis_size("ctx")
    head = lax.axis_size("head")
    run = lax.axis_index("ctx")
    column = lax.axis_index("head")
    reach = -(-REACH // per_dev)
    length = ctx // 2
    direct = ctx == 8 and head == length and reach == 2 and out_grad.shape[1] == 2 * features
    place = run // 2
    side = run % 2
    if direct:
        offsets, early = (-2, 2, "pair", "across"), ("across",)
    else:
        offsets, early = tuple(o for o in range(-reach, reach + 1) if o != 0), ()
    places = 1 + len(offsets)
    smem = pl.BlockSpec(memory_space=pltpu.SMEM)
    whole = pl.BlockSpec(memory_space=pltpu.VMEM)
    distant = pl.BlockSpec(memory_space=pltpu.HBM)
    anywhere = pl.BlockSpec(memory_space=pl.ANY)
    width = out_weight.shape[0]

    both = jnp.stack([key_heads, value_heads])
    head_rows = both[:, :BLK]
    if direct:
        half = out_grad.shape[1] // 2
        own_half = lax.dynamic_slice_in_dim(out_grad, side * half, half, 1)
        other_half = lax.dynamic_slice_in_dim(out_grad, (1 - side) * half, half, 1)
        before, after = shifted(both, 2), shifted(both, -2)
        beside = swapped(jnp.concatenate([both, other_half[None]], axis=0), range(length))
        grad_side = lax.all_gather(jnp.concatenate([own_half, tied(beside[2], before, after)], axis=0), "head", axis=1, tiled=True)
        sent = jnp.where(side == 0, after, before)
        hop = [(2 * z, 2 * z + 1) for z in range(length - 1)] + [(2 * z + 1, 2 * z) for z in range(1, length)]
        across = lax.ppermute(sent, "ctx", hop)
        known = jnp.where(run == 1, beside[:2, :BLK], head_rows)
        known = jnp.where(run == 2, before[:, :BLK], known)
        middle_rows = lax.ppermute(head_rows, "ctx", [(0, length)])
        known = jnp.where(run == length, middle_rows, known)
        late = lax.ppermute(known, "ctx", [(1, 7), (0, 3), (4, 5), (2, 6)])
        first = jnp.where((run == 3) | (run > length), late, known)

        def between(x, places):
            return lax.ppermute(x, "ctx", [(2 * a + n, 2 * b + n) for a, b in places for n in range(2)])

        base = tied(out_weight, before, after, middle_rows)
        near = between(base, ((0, 1), (1, 0), (2, 3), (3, 2)))
        middle = between(base, ((1, 2), (2, 1)))
        far = between(near, ((1, 2), (2, 1)))
        outer = between(middle, ((1, 0), (2, 3)))
        farthest = between(far, ((1, 0), (2, 3)))
        weight_pieces = [base, near, middle, outer, far, farthest]
        bands = [before, after, beside, across]
    else:
        bands = [shifted(both, -o) for o in offsets]
        first = from_first(head_rows)
        grad_full = lax.all_gather(out_grad, "head", axis=1, tiled=True)
        full_weight = lax.all_gather(out_weight, "ctx", axis=0, tiled=True)
        rounds = ctx // head
        mine = jnp.zeros((rounds * tokens, width), jnp.bfloat16)
        for r in range(rounds):
            pairs = []
            for c in range(ctx):
                for h in range(head):
                    pairs.append((c * head + h, (rounds * h + (c + r) % rounds) * head + c // rounds))
            sent = lax.dynamic_slice_in_dim(out_grad, ((run + r) % rounds) * width, width, 1)
            got = lax.ppermute(sent, ("ctx", "head"), pairs)
            mine = lax.dynamic_update_slice_in_dim(mine, got, ((run - r) % rounds) * tokens, 0)
        grad_rows = lax.all_gather(mine, "head", axis=0, tiled=True)

    run_word = run.astype(jnp.int32).reshape(1)
    flat = pl.BlockSpec((tokens, HD), lambda h: (0, h))
    pair = pl.BlockSpec((2, tokens, HD), lambda h: (0, 0, h))
    head_pair = pl.BlockSpec((2, BLK, HD), lambda h: (0, 0, h))
    row = pl.BlockSpec((1, 1, tokens), lambda h: (h, 0, 0))
    keys = places * tokens + BLK
    mixed, lse = pl.pallas_call(
        functools.partial(fwd_kernel, offsets, per_dev, scale),
        grid=(groups,),
        in_specs=[smem, smem, flat, flat, flat] + [pair] * len(offsets) + [head_pair],
        out_specs=[flat, row],
        out_shape=[
            jax.ShapeDtypeStruct((tokens, features), jnp.bfloat16),
            jax.ShapeDtypeStruct((groups, 1, tokens), jnp.float32),
        ],
        scratch_shapes=[pltpu.VMEM((keys, tokens), jnp.float32)],
        compiler_params=pltpu.CompilerParams(vmem_limit_bytes=40 * 1024 * 1024),
        cost_estimate=CHEAP,
        name="attend",
    )(run_word, block_lists, queries, key_heads, value_heads, *bands, first)

    if direct:
        held = [pltpu.VMEM((length, width, features), jnp.bfloat16), pltpu.SemaphoreType.DMA((length,))]
        own_grad, other_grad = pl.pallas_call(
            functools.partial(grads_kernel, length),
            in_specs=[distant] + [anywhere] * 6,
            out_specs=[whole] * 2,
            out_shape=[
                jax.ShapeDtypeStruct((tokens, features), jnp.float32),
                jax.ShapeDtypeStruct((tokens, features), jnp.bfloat16),
            ],
            scratch_shapes=[pltpu.VMEM((2 * tokens, length * width), jnp.bfloat16)] + held + [pltpu.SemaphoreType.DMA],
            compiler_params=pltpu.CompilerParams(vmem_limit_bytes=32 * 1024 * 1024),
            cost_estimate=CHEAP,
            name="project_grad",
        )(grad_side, *weight_pieces)
        mixed_grad = (own_grad + swapped(other_grad, range(length)).astype(jnp.float32)).astype(jnp.bfloat16)
        mixed_other = tied(swapped(mixed, range(length)), other_grad)
        partial_out = pl.pallas_call(
            functools.partial(outs_kernel, length),
            in_specs=[whole] * 2 + [anywhere] * 6,
            out_specs=pl.BlockSpec((2 * tokens, length * width), lambda: (0, 0)),
            out_shape=jax.ShapeDtypeStruct((2 * tokens, length * width), jnp.bfloat16),
            scratch_shapes=held,
            compiler_params=pltpu.CompilerParams(vmem_limit_bytes=32 * 1024 * 1024),
            cost_estimate=CHEAP,
            name="project_out",
        )(mixed, mixed_other, *weight_pieces)
        scattered = lax.psum_scatter(partial_out, "head", scatter_dimension=1, tiled=True)
        mine, theirs = scattered[:tokens], swapped(scattered[tokens:], range(length))
        attended = jnp.where(
            side == 0, jnp.concatenate([mine, theirs], axis=1), jnp.concatenate([theirs, mine], axis=1)
        )
        own_part, *weight_parts = pl.pallas_call(
            functools.partial(weight_kernel, length),
            in_specs=[distant] + [whole] * 2,
            out_specs=[whole] * length,
            out_shape=[jax.ShapeDtypeStruct((width, features), jnp.float32)]
            + [jax.ShapeDtypeStruct((width, features), jnp.bfloat16)] * (length - 1),
            scratch_shapes=[
                pltpu.VMEM((2 * tokens, length * width), jnp.bfloat16),
                pltpu.VMEM((2 * tokens, features), jnp.bfloat16),
                pltpu.SemaphoreType.DMA,
            ],
            compiler_params=pltpu.CompilerParams(vmem_limit_bytes=32 * 1024 * 1024),
            cost_estimate=CHEAP,
            name="weight_part",
        )(grad_side, mixed, mixed_other)
        mixed_grad = tied(mixed_grad, own_part, partial_out)
        weight_turns = [turned(weight_parts[n - 1], n, length) for n in (1, 3)]
    else:
        partial_out = mm(mixed, full_weight, NT).astype(jnp.bfloat16)
        mixed_grad = mm(grad_full, full_weight, NN).astype(jnp.bfloat16)
        mixed_all = lax.all_gather(mixed, "ctx", axis=0, tiled=True)
        attended = lax.psum_scatter(partial_out, "head", scatter_dimension=1, tiled=True)
    early_bands = [band for o, band in zip(offsets, bands) if o in early]
    early_rows = len(early) * tokens + BLK
    early_grads = pl.pallas_call(
        functools.partial(first_kernel, early, per_dev, scale),
        grid=(groups,),
        in_specs=[smem, smem, flat] + [pair] * len(early) + [head_pair, flat, flat, row],
        out_specs=pl.BlockSpec((2, early_rows, HD), lambda h: (0, 0, h)),
        out_shape=jax.ShapeDtypeStruct((2, early_rows, features), jnp.bfloat16),
        scratch_shapes=[pltpu.VMEM((1 + len(early), tokens, tokens), jnp.float32)],
        compiler_params=pltpu.CompilerParams(vmem_limit_bytes=32 * 1024 * 1024),
        cost_estimate=pl.CostEstimate(flops=10_000_000_000, bytes_accessed=1, transcendentals=0),
        name="first_grad",
    )(run_word, block_lists, queries, *early_bands, first, mixed, mixed_grad, lse)

    lse_later = tied(lse, early_grads)
    results = pl.pallas_call(
        functools.partial(bwd_kernel, offsets, early, per_dev, scale),
        grid=(groups,),
        in_specs=[smem, smem, flat, flat, flat] + [pair] * len(offsets) + [head_pair, flat, flat, row],
        out_specs=[flat, pair] + [pair] * (len(offsets) - len(early)),
        out_shape=[
            jax.ShapeDtypeStruct((tokens, features), jnp.bfloat16),
            jax.ShapeDtypeStruct((2, tokens, features), jnp.float32),
        ]
        + [jax.ShapeDtypeStruct((2, tokens, features), jnp.bfloat16)] * (len(offsets) - len(early)),
        scratch_shapes=[pltpu.VMEM((1 + places, tokens, tokens), jnp.float32)],
        compiler_params=pltpu.CompilerParams(vmem_limit_bytes=40 * 1024 * 1024),
        cost_estimate=pl.CostEstimate(flops=30_000_000_000, bytes_accessed=1, transcendentals=0),
        name="attend_grad",
    )(run_word, block_lists, queries, key_heads, value_heads, *bands, first, mixed, mixed_grad, lse_later)
    query_grad, own = results[:2]
    if direct:
        to_before, to_after, to_beside = results[2:]
        swap = tied(swapped(early_grads, range(length)), query_grad)
        diagonal = swap[:, :tokens].astype(jnp.float32)
        first_sum = early_grads[:, tokens:].astype(jnp.float32) + swap[:, tokens:].astype(jnp.float32)
        folded = jnp.pad(jnp.where(run == 2, first_sum, 0.0), ((0, 0), (0, tokens - BLK), (0, 0)))
        to_before, to_after, _ = lax.optimization_barrier((to_before, to_after, weight_turns))
        to_before = to_before.astype(jnp.float32) + jnp.where(side == 1, diagonal, 0.0) + folded
        to_after = to_after.astype(jnp.float32) + jnp.where(side == 0, diagonal, 0.0)
        back_pair = swapped(to_beside, range(length))
        to_before, to_after = to_before.astype(jnp.bfloat16), to_after.astype(jnp.bfloat16)
        to_before, to_after, near, last_part = lax.optimization_barrier(
            (to_before, to_after, first_sum.astype(jnp.bfloat16), weight_parts[1])
        )
        back_down = shifted(to_before, -2)
        back_up = shifted(to_after, 2)
        for c in range(length, ctx, 2):
            got = tied(lax.ppermute(near, "ctx", [(c, 0)]), back_down, back_up)
            first_sum = first_sum + got.astype(jnp.float32)
        weight_grad = own_part
        for part in weight_turns + [turned(last_part, 2, length)]:
            weight_grad = weight_grad + part.astype(jnp.float32)
        wide = pl.BlockSpec((2, BLK, features), lambda n: (0, n, 0))
        top = pl.BlockSpec((2, BLK, features), lambda n: (0, 0, 0))
        slab = pl.BlockSpec((BLK, features), lambda n: (n, 0))
        key_grad, value_grad = pl.pallas_call(
            functools.partial(finish_kernel, scale),
            grid=(per_dev,),
            in_specs=[smem] + [wide] * 4 + [top],
            out_specs=[slab, slab],
            out_shape=[jax.ShapeDtypeStruct((tokens, features), jnp.bfloat16)] * 2,
            cost_estimate=CHEAP,
            name="finish",
        )(run_word, own, back_pair, back_down, back_up, first_sum)

    else:
        first_sum = to_first(early_grads.astype(jnp.float32))
        sums = own
        for o, part in zip(offsets, results[2:]):
            sums = sums + shifted(part, o).astype(jnp.float32)
        first_sum = jnp.where(run == 0, first_sum, 0.0)
        sums = sums + jnp.pad(first_sum, ((0, 0), (0, tokens - BLK), (0, 0)))
        key_grad = (sums[0] * scale).astype(jnp.bfloat16)
        value_grad = sums[1].astype(jnp.bfloat16)
    if not direct:
        weight_grad = mm(grad_rows, mixed_all, TN)
    return (attended, query_grad, key_grad, value_grad, weight_grad)


def solution(mesh):
    spec = P("ctx", "head")
    return jax.shard_map(
        local,
        mesh=mesh,
        in_specs=(spec, spec, spec, spec, P(), spec),
        out_specs=(spec,) * 5,
        check_vma=False,
    )
```

```python
import functools

import jax
import jax.numpy as jnp
from jax import lax
from jax.experimental import pallas as pl
from jax.experimental.pallas import tpu as pltpu
from jax.sharding import PartitionSpec as P

HD = 128
BLK = 128
REACH = 4

CHEAP = pl.CostEstimate(flops=1, bytes_accessed=1, transcendentals=0)

NT = (((1,), (1,)), ((), ()))
TN = (((0,), (0,)), ((), ()))
NN = (((1,), (0,)), ((), ()))


def mm(a, b, dims):
    return lax.dot_general(a, b, dims, preferred_element_type=jnp.float32)


def shifted(x, by):
    peers = lax.axis_size("ctx")
    return lax.ppermute(x, "ctx", [(i, i + by) for i in range(peers) if 0 <= i + by < peers])


def tree_strides(peers):
    strides = []
    stride = 1
    while stride < peers:
        strides.append(stride)
        stride *= 2
    return strides


def from_first(x):
    peers = lax.axis_size("ctx")
    me = lax.axis_index("ctx")
    for stride in reversed(tree_strides(peers)):
        pairs = [(i, i + stride) for i in range(0, peers, 2 * stride) if i + stride < peers]
        got = lax.ppermute(x, "ctx", pairs)
        x = jnp.where(me % (2 * stride) == stride, got, x)
    return x


def to_first(x):
    peers = lax.axis_size("ctx")
    for stride in tree_strides(peers):
        pairs = [(i + stride, i) for i in range(0, peers, 2 * stride) if i + stride < peers]
        x = x + lax.ppermute(x.astype(jnp.bfloat16), "ctx", pairs).astype(x.dtype)
    return x


def turned(x, by, length):
    return lax.ppermute(x, "ctx", [(2 * z + n, 2 * ((z + by) % length) + n) for z in range(length) for n in range(2)])


def swapped(piece, places):
    return lax.ppermute(piece, "ctx", [(2 * z + n, 2 * z + 1 - n) for z in places for n in range(2)])


def tied(x, *others):
    return lax.optimization_barrier((x,) + others)[0]


def start_weights(pieces, held_ref, sems):
    place = lax.div(lax.axis_index("ctx"), 2)
    own, beside, middle, outer, far, farthest = pieces
    low = place < 2
    inner = (place == 1) | (place == 2)

    def send(piece, slot):
        pltpu.make_async_copy(piece, held_ref.at[slot], sems.at[slot]).start()

    send(own, place)
    send(beside, place + 1 - 2 * lax.rem(place, 2))

    @pl.when(inner)
    def _():
        send(middle, 3 - place)
        send(far, jnp.where(low, 3, 0))

    @pl.when(jnp.logical_not(inner))
    def _():
        send(outer, jnp.where(low, 2, 1))
        send(farthest, 3 - place)


def weight_at(held_ref, sems, b):
    pltpu.make_async_copy(held_ref.at[b], held_ref.at[b], sems.at[b]).wait()
    return held_ref[b]


def grads_kernel(length, rows_ref, *rest):
    pieces = rest[:6]
    grad_ref, other_ref, held_ref, sems = rest[6:]
    tokens = grad_ref.shape[0]
    width = rows_ref.shape[1] // length
    start_weights(pieces, held_ref, sems)
    total = None
    for b in range(length):
        part = mm(rows_ref[:, b * width : (b + 1) * width], weight_at(held_ref, sems, b), NN)
        total = part if total is None else total + part
    grad_ref[...] = total[:tokens]
    other_ref[...] = total[tokens:].astype(jnp.bfloat16)


def outs_kernel(length, mixed_ref, other_ref, *rest):
    pieces = rest[:6]
    out_ref, held_ref, sems = rest[6:]
    tokens = mixed_ref.shape[0]
    width = out_ref.shape[1] // length
    start_weights(pieces, held_ref, sems)
    for b in range(length):
        weight = weight_at(held_ref, sems, b)
        columns = slice(b * width, (b + 1) * width)
        out_ref[:tokens, columns] = mm(mixed_ref[...], weight, NT).astype(jnp.bfloat16)
        out_ref[tokens:, columns] = mm(other_ref[...], weight, NT).astype(jnp.bfloat16)


def weight_kernel(length, rows_ref, mixed_ref, other_ref, own_ref, *rest):
    sends = rest[: length - 1]
    (both_ref,) = rest[length - 1 :]
    width = own_ref.shape[0]
    tokens = mixed_ref.shape[0]
    place = lax.div(lax.axis_index("ctx"), 2)
    both_ref[:tokens, :] = mixed_ref[...]
    both_ref[tokens:, :] = other_ref[...]
    for n, out_ref in enumerate((own_ref,) + sends):
        column = pl.multiple_of(lax.rem(place + n, length) * width, 128)
        out_ref[...] = mm(rows_ref[:, pl.ds(column, width)], both_ref[...], TN).astype(out_ref.dtype)


def finish_kernel(scale, run_ref, own_ref, a_ref, b_ref, c_ref, first_ref, key_ref, value_ref):
    there = jnp.where((run_ref[0] == 0) & (pl.program_id(0) == 0), 1.0, 0.0).astype(jnp.float32)
    for n, out_ref in enumerate((key_ref, value_ref)):
        total = own_ref[n] + a_ref[n].astype(jnp.float32) + b_ref[n].astype(jnp.float32) + c_ref[n].astype(jnp.float32)
        total = total + there * first_ref[n]
        out_ref[...] = (total * (scale if n == 0 else 1.0)).astype(jnp.bfloat16)


def runs_away(offset, run):
    side = lax.rem(run, 2)
    if offset == "pair":
        return 1 - 2 * side
    if offset == "across":
        return 2 * side - 1
    return offset


def block_bias(lists_ref, run, per_dev, total_blocks, offset, i, j):
    row = run * per_dev + i
    key = (run + runs_away(offset, run)) * per_dev + j
    hit = (key - row <= 1) & (row - key <= 1)
    for n in range(lists_ref.shape[1]):
        hit = hit | (lists_ref[row, n] == key)
    hit = hit & (key >= 1) & (key < total_blocks)
    return jnp.where(hit, 0.0, -jnp.inf).astype(jnp.float32)


def fwd_kernel(offsets, per_dev, scale, run_ref, lists_ref, q_ref, k_ref, v_ref, *rest):
    bands = rest[: len(offsets)]
    first_ref, mixed_ref, lse_ref, s_ref = rest[len(offsets) :]
    total_blocks = lists_ref.shape[0]
    run = run_ref[0]
    q = q_ref[...]
    tokens = q.shape[0]

    def key_of(p):
        return k_ref[...] if p == 0 else bands[p - 1][0]

    def value_of(p):
        return v_ref[...] if p == 0 else bands[p - 1][1]

    places = (0,) + offsets
    top = None
    for p, offset in enumerate(places):
        s = mm(key_of(p), q, NT) * scale
        for j in range(per_dev):
            for i in range(per_dev):
                part = s[j * BLK : (j + 1) * BLK, i * BLK : (i + 1) * BLK]
                part = part + block_bias(lists_ref, run, per_dev, total_blocks, offset, i, j)
                s_ref[p * tokens + j * BLK : p * tokens + (j + 1) * BLK, i * BLK : (i + 1) * BLK] = part
    s_ref[len(places) * tokens :, :] = mm(first_ref[0], q, NT) * scale
    s = s_ref[...]
    top = jnp.max(s, axis=0, keepdims=True)
    e = jnp.exp(s - top)
    total = jnp.sum(e, axis=0, keepdims=True)
    inverse = 1.0 / total
    low = (e * inverse).astype(jnp.bfloat16)
    out = mm(first_ref[1], low[len(places) * tokens :], TN)
    for p in range(len(places)):
        out = out + mm(value_of(p), low[p * tokens : (p + 1) * tokens], TN)
    mixed_ref[...] = out.T.astype(jnp.bfloat16)
    lse_ref[0] = top + jnp.log(total)


def probs_of(lists_ref, s_ref, run, per_dev, s, offset, lse):
    if offset is None:
        return jnp.exp(s - lse)
    for j in range(per_dev):
        for i in range(per_dev):
            part = s[j * BLK : (j + 1) * BLK, i * BLK : (i + 1) * BLK]
            part = part + block_bias(lists_ref, run, per_dev, lists_ref.shape[0], offset, i, j)
            s_ref[j * BLK : (j + 1) * BLK, i * BLK : (i + 1) * BLK] = part
    return jnp.exp(s_ref[...] - lse)


def first_kernel(offsets, per_dev, scale, run_ref, lists_ref, q_ref, *rest):
    bands = rest[: len(offsets)]
    first_ref, mixed_ref, grad_ref, lse_ref, out_ref, s_ref = rest[len(offsets) :]
    q = q_ref[...]
    grad = grad_ref[...]
    lse = lse_ref[0]
    product = grad.astype(jnp.float32) * mixed_ref[...].astype(jnp.float32)
    delta = jnp.sum(product.T, axis=0, keepdims=True)
    at = 0
    for n, (offset, pair_ref) in enumerate(zip(tuple(offsets) + (None,), bands + (first_ref,))):
        p = probs_of(lists_ref, s_ref.at[n], run_ref[0], per_dev, mm(pair_ref[0], q, NT) * scale, offset, lse)
        slopes = (p * (mm(pair_ref[1], grad, NT) - delta)).astype(jnp.bfloat16)
        rows = slice(at, at + pair_ref.shape[1])
        at = rows.stop
        out_ref[0, rows, :] = mm(slopes, q, NN).astype(jnp.bfloat16)
        out_ref[1, rows, :] = mm(p.astype(jnp.bfloat16), grad, NN).astype(jnp.bfloat16)


def bwd_kernel(offsets, early, per_dev, scale, run_ref, lists_ref, q_ref, k_ref, v_ref, *rest):
    bands = rest[: len(offsets)]
    first_ref, mixed_ref, grad_ref, lse_ref = rest[len(offsets) : len(offsets) + 4]
    outs = rest[len(offsets) + 4 :]
    dq_ref, own_ref = outs[:2]
    band_outs = list(outs[2:-1])
    s_ref = outs[-1]
    q = q_ref[...]
    grad = grad_ref[...]
    lse = lse_ref[0]
    product = grad.astype(jnp.float32) * mixed_ref[...].astype(jnp.float32)
    delta = jnp.sum(product.T, axis=0, keepdims=True)
    dq = None
    plan = [(None, first_ref[0], first_ref[1], None)]
    for offset, pair_ref in zip(offsets, bands):
        plan.append((offset, pair_ref[0], pair_ref[1], None if offset in early else band_outs.pop(0)))
    plan.append((0, k_ref[...], v_ref[...], own_ref))
    for n, (offset, key, value, out_ref) in enumerate(plan):
        p = probs_of(lists_ref, s_ref.at[n], run_ref[0], per_dev, mm(key, q, NT) * scale, offset, lse)
        slopes = (p * (mm(value, grad, NT) - delta)).astype(jnp.bfloat16)
        more = mm(key, slopes, TN)
        dq = more if dq is None else dq + more
        if out_ref is not None:
            out_ref[0] = mm(slopes, q, NN).astype(out_ref.dtype)
            out_ref[1] = mm(p.astype(jnp.bfloat16), grad, NN).astype(out_ref.dtype)
    dq_ref[...] = (dq * scale).T.astype(jnp.bfloat16)


def local(queries, key_heads, value_heads, out_weight, block_lists, out_grad):
    scale = HD ** (-0.5)
    tokens, features = queries.shape
    groups = features // HD
    per_dev = tokens // BLK
    ctx = lax.axis_size("ctx")
    head = lax.axis_size("head")
    run = lax.axis_index("ctx")
    column = lax.axis_index("head")
    reach = -(-REACH // per_dev)
    length = ctx // 2
    direct = ctx == 8 and head == length and reach == 2 and out_grad.shape[1] == 2 * features
    place = run // 2
    side = run % 2
    if direct:
        offsets, early = (-2, 2, "pair", "across"), ("across",)
    else:
        offsets, early = tuple(o for o in range(-reach, reach + 1) if o != 0), ()
    places = 1 + len(offsets)
    smem = pl.BlockSpec(memory_space=pltpu.SMEM)
    whole = pl.BlockSpec(memory_space=pltpu.VMEM)
    anywhere = pl.BlockSpec(memory_space=pl.ANY)
    width = out_weight.shape[0]

    both = jnp.stack([key_heads, value_heads])
    head_rows = both[:, :BLK]
    if direct:
        half = out_grad.shape[1] // 2
        own_half = lax.dynamic_slice_in_dim(out_grad, side * half, half, 1)
        other_half = lax.dynamic_slice_in_dim(out_grad, (1 - side) * half, half, 1)
        before, after = shifted(both, 2), shifted(both, -2)
        beside = swapped(jnp.concatenate([both, other_half[None]], axis=0), range(length))
        grad_side = lax.all_gather(jnp.concatenate([own_half, tied(beside[2], before, after)], axis=0), "head", axis=1, tiled=True)
        sent = jnp.where(side == 0, after, before)
        hop = [(2 * z, 2 * z + 1) for z in range(length - 1)] + [(2 * z + 1, 2 * z) for z in range(1, length)]
        across = lax.ppermute(sent, "ctx", hop)
        known = jnp.where(run == 2, before[:, :BLK], head_rows)
        known = jnp.where((run == 3) | (run == 4), lax.ppermute(known, "ctx", [(2, 4), (0, 3)]), known)
        known = jnp.where(run == 1, beside[:2, :BLK], known)
        first = jnp.where(run > length, lax.ppermute(known, "ctx", [(4, 6), (3, 5), (2, 7)]), known)

        def between(x, places):
            return lax.ppermute(x, "ctx", [(2 * a + n, 2 * b + n) for a, b in places for n in range(2)])

        base = tied(out_weight, before, after)
        near = between(base, ((0, 1), (1, 0), (2, 3), (3, 2)))
        middle = between(base, ((1, 2), (2, 1)))
        near, middle, across, first = lax.optimization_barrier((near, middle, across, first))
        far = between(near, ((1, 2), (2, 1)))
        outer = between(middle, ((1, 0), (2, 3)))
        farthest = between(far, ((1, 0), (2, 3)))
        weight_pieces = [base, near, middle, outer, far, farthest]
        bands = [before, after, beside, across]
    else:
        bands = [shifted(both, -o) for o in offsets]
        first = from_first(head_rows)
        grad_full = lax.all_gather(out_grad, "head", axis=1, tiled=True)
        full_weight = lax.all_gather(out_weight, "ctx", axis=0, tiled=True)
        rounds = ctx // head
        mine = jnp.zeros((rounds * tokens, width), jnp.bfloat16)
        for r in range(rounds):
            pairs = []
            for c in range(ctx):
                for h in range(head):
                    pairs.append((c * head + h, (rounds * h + (c + r) % rounds) * head + c // rounds))
            sent = lax.dynamic_slice_in_dim(out_grad, ((run + r) % rounds) * width, width, 1)
            got = lax.ppermute(sent, ("ctx", "head"), pairs)
            mine = lax.dynamic_update_slice_in_dim(mine, got, ((run - r) % rounds) * tokens, 0)
        grad_rows = lax.all_gather(mine, "head", axis=0, tiled=True)

    run_word = run.astype(jnp.int32).reshape(1)
    flat = pl.BlockSpec((tokens, HD), lambda h: (0, h))
    pair = pl.BlockSpec((2, tokens, HD), lambda h: (0, 0, h))
    head_pair = pl.BlockSpec((2, BLK, HD), lambda h: (0, 0, h))
    row = pl.BlockSpec((1, 1, tokens), lambda h: (h, 0, 0))
    keys = places * tokens + BLK
    mixed, lse = pl.pallas_call(
        functools.partial(fwd_kernel, offsets, per_dev, scale),
        grid=(groups,),
        in_specs=[smem, smem, flat, flat, flat] + [pair] * len(offsets) + [head_pair],
        out_specs=[flat, row],
        out_shape=[
            jax.ShapeDtypeStruct((tokens, features), jnp.bfloat16),
            jax.ShapeDtypeStruct((groups, 1, tokens), jnp.float32),
        ],
        scratch_shapes=[pltpu.VMEM((keys, tokens), jnp.float32)],
        compiler_params=pltpu.CompilerParams(vmem_limit_bytes=40 * 1024 * 1024),
        cost_estimate=CHEAP,
        name="attend",
    )(run_word, block_lists, queries, key_heads, value_heads, *bands, first)

    if direct:
        held = [pltpu.VMEM((length, width, features), jnp.bfloat16), pltpu.SemaphoreType.DMA((length,))]
        mixed_other = swapped(mixed, range(length))
        own_part, *weight_parts = pl.pallas_call(
            functools.partial(weight_kernel, length),
            in_specs=[whole] + [whole] * 2,
            out_specs=[whole] * length,
            out_shape=[jax.ShapeDtypeStruct((width, features), jnp.float32)]
            + [jax.ShapeDtypeStruct((width, features), jnp.bfloat16)] * (length - 1),
            scratch_shapes=[pltpu.VMEM((2 * tokens, features), jnp.bfloat16)],
            compiler_params=pltpu.CompilerParams(vmem_limit_bytes=32 * 1024 * 1024),
            cost_estimate=CHEAP,
            name="weight_part",
        )(grad_side, mixed, mixed_other)
        own_grad, other_grad = pl.pallas_call(
            functools.partial(grads_kernel, length),
            in_specs=[whole] + [anywhere] * 6,
            out_specs=[whole] * 2,
            out_shape=[
                jax.ShapeDtypeStruct((tokens, features), jnp.float32),
                jax.ShapeDtypeStruct((tokens, features), jnp.bfloat16),
            ],
            scratch_shapes=held,
            compiler_params=pltpu.CompilerParams(vmem_limit_bytes=32 * 1024 * 1024),
            cost_estimate=CHEAP,
            name="project_grad",
        )(tied(grad_side, own_part), *weight_pieces)
        mixed_grad = (own_grad + swapped(other_grad, range(length)).astype(jnp.float32)).astype(jnp.bfloat16)
        partial_out = pl.pallas_call(
            functools.partial(outs_kernel, length),
            in_specs=[whole] * 2 + [anywhere] * 6,
            out_specs=pl.BlockSpec((2 * tokens, length * width), lambda: (0, 0)),
            out_shape=jax.ShapeDtypeStruct((2 * tokens, length * width), jnp.bfloat16),
            scratch_shapes=held,
            compiler_params=pltpu.CompilerParams(vmem_limit_bytes=32 * 1024 * 1024),
            cost_estimate=CHEAP,
            name="project_out",
        )(mixed, tied(mixed_other, other_grad), *weight_pieces)
        scattered = lax.psum_scatter(partial_out, "head", scatter_dimension=1, tiled=True)
        mine, theirs = scattered[:tokens], swapped(scattered[tokens:], range(length))
        attended = jnp.where(
            side == 0, jnp.concatenate([mine, theirs], axis=1), jnp.concatenate([theirs, mine], axis=1)
        )
        mixed_grad = tied(mixed_grad, partial_out)
        weight_turns = [turned(weight_parts[n - 1], n, length) for n in (1, 3)]
    else:
        partial_out = mm(mixed, full_weight, NT).astype(jnp.bfloat16)
        mixed_grad = mm(grad_full, full_weight, NN).astype(jnp.bfloat16)
        mixed_all = lax.all_gather(mixed, "ctx", axis=0, tiled=True)
        attended = lax.psum_scatter(partial_out, "head", scatter_dimension=1, tiled=True)
    early_bands = [band for o, band in zip(offsets, bands) if o in early]
    early_rows = len(early) * tokens + BLK
    early_grads = pl.pallas_call(
        functools.partial(first_kernel, early, per_dev, scale),
        grid=(groups,),
        in_specs=[smem, smem, flat] + [pair] * len(early) + [head_pair, flat, flat, row],
        out_specs=pl.BlockSpec((2, early_rows, HD), lambda h: (0, 0, h)),
        out_shape=jax.ShapeDtypeStruct((2, early_rows, features), jnp.bfloat16),
        scratch_shapes=[pltpu.VMEM((1 + len(early), tokens, tokens), jnp.float32)],
        compiler_params=pltpu.CompilerParams(vmem_limit_bytes=32 * 1024 * 1024),
        cost_estimate=pl.CostEstimate(flops=10_000_000_000, bytes_accessed=1, transcendentals=0),
        name="first_grad",
    )(run_word, block_lists, queries, *early_bands, first, mixed, mixed_grad, lse)

    lse_later = tied(lse, early_grads)
    results = pl.pallas_call(
        functools.partial(bwd_kernel, offsets, early, per_dev, scale),
        grid=(groups,),
        in_specs=[smem, smem, flat, flat, flat] + [pair] * len(offsets) + [head_pair, flat, flat, row],
        out_specs=[flat, pair] + [pair] * (len(offsets) - len(early)),
        out_shape=[
            jax.ShapeDtypeStruct((tokens, features), jnp.bfloat16),
            jax.ShapeDtypeStruct((2, tokens, features), jnp.float32),
        ]
        + [jax.ShapeDtypeStruct((2, tokens, features), jnp.bfloat16)] * (len(offsets) - len(early)),
        scratch_shapes=[pltpu.VMEM((1 + places, tokens, tokens), jnp.float32)],
        compiler_params=pltpu.CompilerParams(vmem_limit_bytes=40 * 1024 * 1024),
        cost_estimate=pl.CostEstimate(flops=30_000_000_000, bytes_accessed=1, transcendentals=0),
        name="attend_grad",
    )(run_word, block_lists, queries, key_heads, value_heads, *bands, first, mixed, mixed_grad, lse_later)
    query_grad, own = results[:2]
    if direct:
        to_before, to_after, to_beside = results[2:]
        swap = tied(swapped(early_grads, range(length)), query_grad)
        diagonal = swap[:, :tokens].astype(jnp.float32)
        first_sum = early_grads[:, tokens:].astype(jnp.float32) + swap[:, tokens:].astype(jnp.float32)
        folded = jnp.pad(jnp.where(run == 2, first_sum, 0.0), ((0, 0), (0, tokens - BLK), (0, 0)))
        to_before, to_after, _ = lax.optimization_barrier((to_before, to_after, weight_turns))
        to_before = to_before.astype(jnp.float32) + jnp.where(side == 1, diagonal, 0.0) + folded
        to_after = to_after.astype(jnp.float32) + jnp.where(side == 0, diagonal, 0.0)
        back_pair = swapped(to_beside, range(length))
        to_before, to_after = to_before.astype(jnp.bfloat16), to_after.astype(jnp.bfloat16)
        to_before, to_after, near, last_part = lax.optimization_barrier(
            (to_before, to_after, first_sum.astype(jnp.bfloat16), weight_parts[1])
        )
        back_down = shifted(to_before, -2)
        back_up = shifted(to_after, 2)
        for c in range(length, ctx, 2):
            got = tied(lax.ppermute(near, "ctx", [(c, 0)]), back_down, back_up)
            first_sum = first_sum + got.astype(jnp.float32)
        weight_grad = own_part
        for part in weight_turns + [turned(last_part, 2, length)]:
            weight_grad = weight_grad + part.astype(jnp.float32)
        wide = pl.BlockSpec((2, BLK, features), lambda n: (0, n, 0))
        top = pl.BlockSpec((2, BLK, features), lambda n: (0, 0, 0))
        slab = pl.BlockSpec((BLK, features), lambda n: (n, 0))
        key_grad, value_grad = pl.pallas_call(
            functools.partial(finish_kernel, scale),
            grid=(per_dev,),
            in_specs=[smem] + [wide] * 4 + [top],
            out_specs=[slab, slab],
            out_shape=[jax.ShapeDtypeStruct((tokens, features), jnp.bfloat16)] * 2,
            cost_estimate=CHEAP,
            name="finish",
        )(run_word, tied(own, theirs), back_pair, back_down, back_up, first_sum)

    else:
        first_sum = to_first(early_grads.astype(jnp.float32))
        sums = own
        for o, part in zip(offsets, results[2:]):
            sums = sums + shifted(part, o).astype(jnp.float32)
        first_sum = jnp.where(run == 0, first_sum, 0.0)
        sums = sums + jnp.pad(first_sum, ((0, 0), (0, tokens - BLK), (0, 0)))
        key_grad = (sums[0] * scale).astype(jnp.bfloat16)
        value_grad = sums[1].astype(jnp.bfloat16)
    if not direct:
        weight_grad = mm(grad_rows, mixed_all, TN)
    return (attended, query_grad, key_grad, value_grad, weight_grad)


def solution(mesh):
    spec = P("ctx", "head")
    return jax.shard_map(
        local,
        mesh=mesh,
        in_specs=(spec, spec, spec, spec, P(), spec),
        out_specs=(spec,) * 5,
        check_vma=False,
    )
```

```python
import functools

import jax
import jax.numpy as jnp
from jax import lax
from jax.experimental import pallas as pl
from jax.experimental.pallas import tpu as pltpu
from jax.sharding import PartitionSpec as P

HD = 128
BLK = 128
REACH = 4

CHEAP = pl.CostEstimate(flops=1, bytes_accessed=1, transcendentals=0)

NT = (((1,), (1,)), ((), ()))
TN = (((0,), (0,)), ((), ()))
NN = (((1,), (0,)), ((), ()))


def mm(a, b, dims):
    return lax.dot_general(a, b, dims, preferred_element_type=jnp.float32)


def shifted(x, by):
    peers = lax.axis_size("ctx")
    return lax.ppermute(x, "ctx", [(i, i + by) for i in range(peers) if 0 <= i + by < peers])


def tree_strides(peers):
    strides = []
    stride = 1
    while stride < peers:
        strides.append(stride)
        stride *= 2
    return strides


def from_first(x):
    peers = lax.axis_size("ctx")
    me = lax.axis_index("ctx")
    for stride in reversed(tree_strides(peers)):
        pairs = [(i, i + stride) for i in range(0, peers, 2 * stride) if i + stride < peers]
        got = lax.ppermute(x, "ctx", pairs)
        x = jnp.where(me % (2 * stride) == stride, got, x)
    return x


def to_first(x):
    peers = lax.axis_size("ctx")
    for stride in tree_strides(peers):
        pairs = [(i + stride, i) for i in range(0, peers, 2 * stride) if i + stride < peers]
        x = x + lax.ppermute(x.astype(jnp.bfloat16), "ctx", pairs).astype(x.dtype)
    return x


def turned(x, by, length):
    return lax.ppermute(x, "ctx", [(2 * z + n, 2 * ((z + by) % length) + n) for z in range(length) for n in range(2)])


def swapped(piece, places):
    return lax.ppermute(piece, "ctx", [(2 * z + n, 2 * z + 1 - n) for z in places for n in range(2)])


def tied(x, *others):
    return lax.optimization_barrier((x,) + others)[0]


def start_weights(pieces, held_ref, sems):
    place = lax.div(lax.axis_index("ctx"), 2)
    own, beside, middle, outer, far, farthest = pieces
    low = place < 2
    inner = (place == 1) | (place == 2)

    def send(piece, slot):
        pltpu.make_async_copy(piece, held_ref.at[slot], sems.at[slot]).start()

    send(own, place)
    send(beside, place + 1 - 2 * lax.rem(place, 2))

    @pl.when(inner)
    def _():
        send(middle, 3 - place)
        send(far, jnp.where(low, 3, 0))

    @pl.when(jnp.logical_not(inner))
    def _():
        send(outer, jnp.where(low, 2, 1))
        send(farthest, 3 - place)


def weight_at(held_ref, sems, b):
    pltpu.make_async_copy(held_ref.at[b], held_ref.at[b], sems.at[b]).wait()
    return held_ref[b]


def grads_kernel(length, rows_ref, *rest):
    pieces = rest[:6]
    grad_ref, other_ref, held_ref, sems = rest[6:]
    tokens = grad_ref.shape[0]
    width = rows_ref.shape[1] // length
    start_weights(pieces, held_ref, sems)
    total = None
    for b in range(length):
        part = mm(rows_ref[:, b * width : (b + 1) * width], weight_at(held_ref, sems, b), NN)
        total = part if total is None else total + part
    grad_ref[...] = total[:tokens]
    other_ref[...] = total[tokens:].astype(jnp.bfloat16)


def outs_kernel(length, mixed_ref, other_ref, *rest):
    pieces = rest[:6]
    out_ref, held_ref, sems = rest[6:]
    tokens = mixed_ref.shape[0]
    width = out_ref.shape[1] // length
    start_weights(pieces, held_ref, sems)
    for b in range(length):
        weight = weight_at(held_ref, sems, b)
        columns = slice(b * width, (b + 1) * width)
        out_ref[:tokens, columns] = mm(mixed_ref[...], weight, NT).astype(jnp.bfloat16)
        out_ref[tokens:, columns] = mm(other_ref[...], weight, NT).astype(jnp.bfloat16)


def shuffled(n, length):
    return (n % (length // 2)) * 2 + n // (length // 2)


def weight_kernel(length, rows_ref, *rest):
    pieces = rest[:length]
    own_ref, other_ref, held_ref, sems = rest[length:]
    width = own_ref.shape[0]
    place = lax.div(lax.axis_index("ctx"), 2)
    side = lax.rem(lax.axis_index("ctx"), 2)
    for n, piece in enumerate(pieces):
        origin = lax.rem(place - n + length, length)
        slot = lax.rem(origin, length // 2) * 2 + lax.div(origin, length // 2)
        pltpu.make_async_copy(piece, held_ref.at[slot], sems.at[slot]).start()
    for b in range(length):
        pltpu.make_async_copy(held_ref.at[b], held_ref.at[b], sems.at[b]).wait()
    mixed = held_ref[...].reshape(rows_ref.shape[0], -1)
    other = rows_ref[:, pl.ds(pl.multiple_of((1 - side) * width, 128), width)]
    other_ref[...] = mm(other, mixed, TN).astype(jnp.bfloat16)
    own = rows_ref[:, pl.ds(pl.multiple_of(side * width, 128), width)]
    own_ref[...] = mm(own, mixed, TN)


def finish_kernel(scale, run_ref, own_ref, a_ref, b_ref, c_ref, first_ref, key_ref, value_ref):
    there = jnp.where((run_ref[0] == 0) & (pl.program_id(0) == 0), 1.0, 0.0).astype(jnp.float32)
    for n, out_ref in enumerate((key_ref, value_ref)):
        total = own_ref[n] + a_ref[n].astype(jnp.float32) + b_ref[n].astype(jnp.float32) + c_ref[n].astype(jnp.float32)
        total = total + there * first_ref[n]
        out_ref[...] = (total * (scale if n == 0 else 1.0)).astype(jnp.bfloat16)


def runs_away(offset, run):
    side = lax.rem(run, 2)
    if offset == "pair":
        return 1 - 2 * side
    if offset == "across":
        return 2 * side - 1
    return offset


def block_bias(lists_ref, run, per_dev, total_blocks, offset, i, j):
    row = run * per_dev + i
    key = (run + runs_away(offset, run)) * per_dev + j
    hit = (key - row <= 1) & (row - key <= 1)
    for n in range(lists_ref.shape[1]):
        hit = hit | (lists_ref[row, n] == key)
    hit = hit & (key >= 1) & (key < total_blocks)
    return jnp.where(hit, 0.0, -jnp.inf).astype(jnp.float32)


def fwd_kernel(offsets, per_dev, scale, run_ref, lists_ref, q_ref, k_ref, v_ref, *rest):
    bands = rest[: len(offsets)]
    first_ref, mixed_ref, lse_ref, s_ref = rest[len(offsets) :]
    total_blocks = lists_ref.shape[0]
    run = run_ref[0]
    q = q_ref[...]
    tokens = q.shape[0]

    def key_of(p):
        return k_ref[...] if p == 0 else bands[p - 1][0]

    def value_of(p):
        return v_ref[...] if p == 0 else bands[p - 1][1]

    places = (0,) + offsets
    top = None
    for p, offset in enumerate(places):
        s = mm(key_of(p), q, NT) * scale
        for j in range(per_dev):
            for i in range(per_dev):
                part = s[j * BLK : (j + 1) * BLK, i * BLK : (i + 1) * BLK]
                part = part + block_bias(lists_ref, run, per_dev, total_blocks, offset, i, j)
                s_ref[p * tokens + j * BLK : p * tokens + (j + 1) * BLK, i * BLK : (i + 1) * BLK] = part
    s_ref[len(places) * tokens :, :] = mm(first_ref[0], q, NT) * scale
    s = s_ref[...]
    top = jnp.max(s, axis=0, keepdims=True)
    e = jnp.exp(s - top)
    total = jnp.sum(e, axis=0, keepdims=True)
    inverse = 1.0 / total
    low = (e * inverse).astype(jnp.bfloat16)
    out = mm(first_ref[1], low[len(places) * tokens :], TN)
    for p in range(len(places)):
        out = out + mm(value_of(p), low[p * tokens : (p + 1) * tokens], TN)
    mixed_ref[...] = out.T.astype(jnp.bfloat16)
    lse_ref[0] = top + jnp.log(total)


def probs_of(lists_ref, s_ref, run, per_dev, s, offset, lse):
    if offset is None:
        return jnp.exp(s - lse)
    for j in range(per_dev):
        for i in range(per_dev):
            part = s[j * BLK : (j + 1) * BLK, i * BLK : (i + 1) * BLK]
            part = part + block_bias(lists_ref, run, per_dev, lists_ref.shape[0], offset, i, j)
            s_ref[j * BLK : (j + 1) * BLK, i * BLK : (i + 1) * BLK] = part
    return jnp.exp(s_ref[...] - lse)


def first_kernel(offsets, per_dev, scale, run_ref, lists_ref, q_ref, *rest):
    bands = rest[: len(offsets)]
    first_ref, mixed_ref, grad_ref, lse_ref, out_ref, s_ref = rest[len(offsets) :]
    q = q_ref[...]
    grad = grad_ref[...]
    lse = lse_ref[0]
    product = grad.astype(jnp.float32) * mixed_ref[...].astype(jnp.float32)
    delta = jnp.sum(product.T, axis=0, keepdims=True)
    at = 0
    for n, (offset, pair_ref) in enumerate(zip(tuple(offsets) + (None,), bands + (first_ref,))):
        p = probs_of(lists_ref, s_ref.at[n], run_ref[0], per_dev, mm(pair_ref[0], q, NT) * scale, offset, lse)
        slopes = (p * (mm(pair_ref[1], grad, NT) - delta)).astype(jnp.bfloat16)
        rows = slice(at, at + pair_ref.shape[1])
        at = rows.stop
        out_ref[0, rows, :] = mm(slopes, q, NN).astype(jnp.bfloat16)
        out_ref[1, rows, :] = mm(p.astype(jnp.bfloat16), grad, NN).astype(jnp.bfloat16)


def bwd_kernel(offsets, early, per_dev, scale, run_ref, lists_ref, q_ref, k_ref, v_ref, *rest):
    bands = rest[: len(offsets)]
    first_ref, mixed_ref, grad_ref, lse_ref = rest[len(offsets) : len(offsets) + 4]
    outs = rest[len(offsets) + 4 :]
    dq_ref, own_ref = outs[:2]
    band_outs = list(outs[2:-1])
    s_ref = outs[-1]
    q = q_ref[...]
    grad = grad_ref[...]
    lse = lse_ref[0]
    product = grad.astype(jnp.float32) * mixed_ref[...].astype(jnp.float32)
    delta = jnp.sum(product.T, axis=0, keepdims=True)
    dq = None
    plan = [(None, first_ref[0], first_ref[1], None)]
    for offset, pair_ref in zip(offsets, bands):
        plan.append((offset, pair_ref[0], pair_ref[1], None if offset in early else band_outs.pop(0)))
    plan.append((0, k_ref[...], v_ref[...], own_ref))
    for n, (offset, key, value, out_ref) in enumerate(plan):
        p = probs_of(lists_ref, s_ref.at[n], run_ref[0], per_dev, mm(key, q, NT) * scale, offset, lse)
        slopes = (p * (mm(value, grad, NT) - delta)).astype(jnp.bfloat16)
        more = mm(key, slopes, TN)
        dq = more if dq is None else dq + more
        if out_ref is not None:
            out_ref[0] = mm(slopes, q, NN).astype(out_ref.dtype)
            out_ref[1] = mm(p.astype(jnp.bfloat16), grad, NN).astype(out_ref.dtype)
    dq_ref[...] = (dq * scale).T.astype(jnp.bfloat16)


def local(queries, key_heads, value_heads, out_weight, block_lists, out_grad):
    scale = HD ** (-0.5)
    tokens, features = queries.shape
    groups = features // HD
    per_dev = tokens // BLK
    ctx = lax.axis_size("ctx")
    head = lax.axis_size("head")
    run = lax.axis_index("ctx")
    column = lax.axis_index("head")
    reach = -(-REACH // per_dev)
    length = ctx // 2
    direct = ctx == 8 and head == length and reach == 2 and out_grad.shape[1] == 2 * features
    place = run // 2
    side = run % 2
    if direct:
        offsets, early = (-2, 2, "pair", "across"), ("across",)
    else:
        offsets, early = tuple(o for o in range(-reach, reach + 1) if o != 0), ()
    places = 1 + len(offsets)
    smem = pl.BlockSpec(memory_space=pltpu.SMEM)
    whole = pl.BlockSpec(memory_space=pltpu.VMEM)
    anywhere = pl.BlockSpec(memory_space=pl.ANY)
    width = out_weight.shape[0]

    both = jnp.stack([key_heads, value_heads])
    head_rows = both[:, :BLK]
    if direct:
        half = out_grad.shape[1] // 2
        own_half = lax.dynamic_slice_in_dim(out_grad, side * half, half, 1)
        other_half = lax.dynamic_slice_in_dim(out_grad, (1 - side) * half, half, 1)
        before, after = shifted(both, 2), shifted(both, -2)
        beside = swapped(jnp.concatenate([both, other_half[None]], axis=0), range(length))
        grad_side = lax.all_gather(jnp.concatenate([own_half, tied(beside[2], before, after)], axis=0), "head", axis=1, tiled=True)
        sent = jnp.where(side == 0, after, before)
        hop = [(2 * z, 2 * z + 1) for z in range(length - 1)] + [(2 * z + 1, 2 * z) for z in range(1, length)]
        across = lax.ppermute(sent, "ctx", hop)
        known = jnp.where(run == 2, before[:, :BLK], head_rows)
        known = jnp.where((run == 3) | (run == 4), lax.ppermute(known, "ctx", [(2, 4), (0, 3)]), known)
        late = lax.ppermute(known, "ctx", [(4, 6), (3, 5), (2, 7)])
        first = jnp.where(run == 1, beside[:2, :BLK], jnp.where(run > length, late, known))

        def between(x, places):
            return lax.ppermute(x, "ctx", [(2 * a + n, 2 * b + n) for a, b in places for n in range(2)])

        pairs = []
        for c in range(ctx):
            for h in range(head):
                pairs.append((c * head + h, (2 * h + c % 2) * head + shuffled(c // 2, length)))
        far_rows = lax.ppermute(out_grad, ("ctx", "head"), pairs)
        grad_rows = lax.all_gather(tied(far_rows, first), "head", axis=0, tiled=True)
        base = tied(out_weight, before, after)
        near = between(base, ((0, 1), (1, 0), (2, 3), (3, 2)))
        middle = between(base, ((1, 2), (2, 1)))
        near, middle, _ = lax.optimization_barrier((near, middle, known))
        far = between(near, ((1, 2), (2, 1)))
        outer = between(middle, ((1, 0), (2, 3)))
        farthest = between(far, ((1, 0), (2, 3)))
        weight_pieces = [base, near, middle, outer, far, farthest]
        bands = [before, after, beside, across]
    else:
        bands = [shifted(both, -o) for o in offsets]
        first = from_first(head_rows)
        grad_full = lax.all_gather(out_grad, "head", axis=1, tiled=True)
        full_weight = lax.all_gather(out_weight, "ctx", axis=0, tiled=True)
        rounds = ctx // head
        mine = jnp.zeros((rounds * tokens, width), jnp.bfloat16)
        for r in range(rounds):
            pairs = []
            for c in range(ctx):
                for h in range(head):
                    pairs.append((c * head + h, (rounds * h + (c + r) % rounds) * head + c // rounds))
            sent = lax.dynamic_slice_in_dim(out_grad, ((run + r) % rounds) * width, width, 1)
            got = lax.ppermute(sent, ("ctx", "head"), pairs)
            mine = lax.dynamic_update_slice_in_dim(mine, got, ((run - r) % rounds) * tokens, 0)
        grad_rows = lax.all_gather(mine, "head", axis=0, tiled=True)

    run_word = run.astype(jnp.int32).reshape(1)
    flat = pl.BlockSpec((tokens, HD), lambda h: (0, h))
    pair = pl.BlockSpec((2, tokens, HD), lambda h: (0, 0, h))
    head_pair = pl.BlockSpec((2, BLK, HD), lambda h: (0, 0, h))
    row = pl.BlockSpec((1, 1, tokens), lambda h: (h, 0, 0))
    keys = places * tokens + BLK
    mixed, lse = pl.pallas_call(
        functools.partial(fwd_kernel, offsets, per_dev, scale),
        grid=(groups,),
        in_specs=[smem, smem, flat, flat, flat] + [pair] * len(offsets) + [head_pair],
        out_specs=[flat, row],
        out_shape=[
            jax.ShapeDtypeStruct((tokens, features), jnp.bfloat16),
            jax.ShapeDtypeStruct((groups, 1, tokens), jnp.float32),
        ],
        scratch_shapes=[pltpu.VMEM((keys, tokens), jnp.float32)],
        compiler_params=pltpu.CompilerParams(vmem_limit_bytes=40 * 1024 * 1024),
        cost_estimate=CHEAP,
        name="attend",
    )(run_word, block_lists, queries, key_heads, value_heads, *bands, first)

    if direct:
        held = [pltpu.VMEM((length, width, features), jnp.bfloat16), pltpu.SemaphoreType.DMA((length,))]
        own_grad, other_grad = pl.pallas_call(
            functools.partial(grads_kernel, length),
            in_specs=[whole] + [anywhere] * 6,
            out_specs=[whole] * 2,
            out_shape=[
                jax.ShapeDtypeStruct((tokens, features), jnp.float32),
                jax.ShapeDtypeStruct((tokens, features), jnp.bfloat16),
            ],
            scratch_shapes=held,
            compiler_params=pltpu.CompilerParams(vmem_limit_bytes=32 * 1024 * 1024),
            cost_estimate=CHEAP,
            name="project_grad",
        )(tied(grad_side, far_rows), *weight_pieces)
        mixed_grad = (own_grad + swapped(other_grad, range(length)).astype(jnp.float32)).astype(jnp.bfloat16)
        mixed_other = tied(swapped(mixed, range(length)), other_grad)
        partial_out = pl.pallas_call(
            functools.partial(outs_kernel, length),
            in_specs=[whole] * 2 + [anywhere] * 6,
            out_specs=pl.BlockSpec((2 * tokens, length * width), lambda: (0, 0)),
            out_shape=jax.ShapeDtypeStruct((2 * tokens, length * width), jnp.bfloat16),
            scratch_shapes=held,
            compiler_params=pltpu.CompilerParams(vmem_limit_bytes=32 * 1024 * 1024),
            cost_estimate=CHEAP,
            name="project_out",
        )(mixed, mixed_other, *weight_pieces)
        scattered = lax.psum_scatter(partial_out, "head", scatter_dimension=1, tiled=True)
        mine, theirs = scattered[:tokens], swapped(scattered[tokens:], range(length))
        attended = jnp.where(
            side == 0, jnp.concatenate([mine, theirs], axis=1), jnp.concatenate([theirs, mine], axis=1)
        )
        mixed_grad = tied(mixed_grad, partial_out)
        mixed_turns = [turned(mixed, n, length) for n in range(1, length)]
    else:
        partial_out = mm(mixed, full_weight, NT).astype(jnp.bfloat16)
        mixed_grad = mm(grad_full, full_weight, NN).astype(jnp.bfloat16)
        mixed_all = lax.all_gather(mixed, "ctx", axis=0, tiled=True)
        attended = lax.psum_scatter(partial_out, "head", scatter_dimension=1, tiled=True)
    early_bands = [band for o, band in zip(offsets, bands) if o in early]
    early_rows = len(early) * tokens + BLK
    early_grads = pl.pallas_call(
        functools.partial(first_kernel, early, per_dev, scale),
        grid=(groups,),
        in_specs=[smem, smem, flat] + [pair] * len(early) + [head_pair, flat, flat, row],
        out_specs=pl.BlockSpec((2, early_rows, HD), lambda h: (0, 0, h)),
        out_shape=jax.ShapeDtypeStruct((2, early_rows, features), jnp.bfloat16),
        scratch_shapes=[pltpu.VMEM((1 + len(early), tokens, tokens), jnp.float32)],
        compiler_params=pltpu.CompilerParams(vmem_limit_bytes=32 * 1024 * 1024),
        cost_estimate=pl.CostEstimate(flops=10_000_000_000, bytes_accessed=1, transcendentals=0),
        name="first_grad",
    )(run_word, block_lists, queries, *early_bands, first, mixed, mixed_grad, lse)

    lse_later = tied(lse, early_grads, *(mixed_turns if direct else ()))
    results = pl.pallas_call(
        functools.partial(bwd_kernel, offsets, early, per_dev, scale),
        grid=(groups,),
        in_specs=[smem, smem, flat, flat, flat] + [pair] * len(offsets) + [head_pair, flat, flat, row],
        out_specs=[flat, pair] + [pair] * (len(offsets) - len(early)),
        out_shape=[
            jax.ShapeDtypeStruct((tokens, features), jnp.bfloat16),
            jax.ShapeDtypeStruct((2, tokens, features), jnp.float32),
        ]
        + [jax.ShapeDtypeStruct((2, tokens, features), jnp.bfloat16)] * (len(offsets) - len(early)),
        scratch_shapes=[pltpu.VMEM((1 + places, tokens, tokens), jnp.float32)],
        compiler_params=pltpu.CompilerParams(vmem_limit_bytes=40 * 1024 * 1024),
        cost_estimate=pl.CostEstimate(flops=30_000_000_000, bytes_accessed=1, transcendentals=0),
        name="attend_grad",
    )(run_word, block_lists, queries, key_heads, value_heads, *bands, first, mixed, mixed_grad, lse_later)
    query_grad, own = results[:2]
    if direct:
        to_before, to_after, to_beside = results[2:]
        swap = tied(swapped(early_grads, range(length)), query_grad)
        diagonal = swap[:, :tokens].astype(jnp.float32)
        first_sum = early_grads[:, tokens:].astype(jnp.float32) + swap[:, tokens:].astype(jnp.float32)
        folded = jnp.pad(jnp.where(run == 2, first_sum, 0.0), ((0, 0), (0, tokens - BLK), (0, 0)))
        to_before = to_before.astype(jnp.float32) + jnp.where(side == 1, diagonal, 0.0) + folded
        to_after = to_after.astype(jnp.float32) + jnp.where(side == 0, diagonal, 0.0)
        back_pair = swapped(to_beside, range(length))
        to_before, to_after = to_before.astype(jnp.bfloat16), to_after.astype(jnp.bfloat16)
        to_before, to_after, near = lax.optimization_barrier((to_before, to_after, first_sum.astype(jnp.bfloat16)))
        back_down = shifted(to_before, -2)
        back_up = shifted(to_after, 2)
        for c in range(length, ctx, 2):
            got = tied(lax.ppermute(near, "ctx", [(c, 0)]), back_down, back_up)
            first_sum = first_sum + got.astype(jnp.float32)
        own_part, other_part = pl.pallas_call(
            functools.partial(weight_kernel, length),
            in_specs=[whole] + [anywhere] * length,
            out_specs=[whole, whole],
            out_shape=[
                jax.ShapeDtypeStruct((width, features), jnp.float32),
                jax.ShapeDtypeStruct((width, features), jnp.bfloat16),
            ],
            scratch_shapes=[pltpu.VMEM((length, tokens, features), jnp.bfloat16), pltpu.SemaphoreType.DMA((length,))],
            compiler_params=pltpu.CompilerParams(vmem_limit_bytes=32 * 1024 * 1024),
            cost_estimate=CHEAP,
            name="weight_sum",
        )(grad_rows, tied(mixed, to_before, to_after), *mixed_turns)
        weight_grad = own_part + swapped(other_part, range(length)).astype(jnp.float32)
        wide = pl.BlockSpec((2, BLK, features), lambda n: (0, n, 0))
        top = pl.BlockSpec((2, BLK, features), lambda n: (0, 0, 0))
        slab = pl.BlockSpec((BLK, features), lambda n: (n, 0))
        key_grad, value_grad = pl.pallas_call(
            functools.partial(finish_kernel, scale),
            grid=(per_dev,),
            in_specs=[smem] + [wide] * 4 + [top],
            out_specs=[slab, slab],
            out_shape=[jax.ShapeDtypeStruct((tokens, features), jnp.bfloat16)] * 2,
            cost_estimate=CHEAP,
            name="finish",
        )(run_word, tied(own, theirs), back_pair, back_down, back_up, first_sum)

    else:
        first_sum = to_first(early_grads.astype(jnp.float32))
        sums = own
        for o, part in zip(offsets, results[2:]):
            sums = sums + shifted(part, o).astype(jnp.float32)
        first_sum = jnp.where(run == 0, first_sum, 0.0)
        sums = sums + jnp.pad(first_sum, ((0, 0), (0, tokens - BLK), (0, 0)))
        key_grad = (sums[0] * scale).astype(jnp.bfloat16)
        value_grad = sums[1].astype(jnp.bfloat16)
    if not direct:
        weight_grad = mm(grad_rows, mixed_all, TN)
    return (attended, query_grad, key_grad, value_grad, weight_grad)


def solution(mesh):
    spec = P("ctx", "head")
    return jax.shard_map(
        local,
        mesh=mesh,
        in_specs=(spec, spec, spec, spec, P(), spec),
        out_specs=(spec,) * 5,
        check_vma=False,
    )
```

```python
import functools

import jax
import jax.numpy as jnp
from jax import lax
from jax.experimental import pallas as pl
from jax.experimental.pallas import tpu as pltpu
from jax.sharding import PartitionSpec as P

HD = 128
BLK = 128
REACH = 4

CHEAP = pl.CostEstimate(flops=1, bytes_accessed=1, transcendentals=0)

NT = (((1,), (1,)), ((), ()))
TN = (((0,), (0,)), ((), ()))
NN = (((1,), (0,)), ((), ()))


def mm(a, b, dims):
    return lax.dot_general(a, b, dims, preferred_element_type=jnp.float32)


def shifted(x, by):
    peers = lax.axis_size("ctx")
    return lax.ppermute(x, "ctx", [(i, i + by) for i in range(peers) if 0 <= i + by < peers])


def tree_strides(peers):
    strides = []
    stride = 1
    while stride < peers:
        strides.append(stride)
        stride *= 2
    return strides


def from_first(x):
    peers = lax.axis_size("ctx")
    me = lax.axis_index("ctx")
    for stride in reversed(tree_strides(peers)):
        pairs = [(i, i + stride) for i in range(0, peers, 2 * stride) if i + stride < peers]
        got = lax.ppermute(x, "ctx", pairs)
        x = jnp.where(me % (2 * stride) == stride, got, x)
    return x


def to_first(x):
    peers = lax.axis_size("ctx")
    for stride in tree_strides(peers):
        pairs = [(i + stride, i) for i in range(0, peers, 2 * stride) if i + stride < peers]
        x = x + lax.ppermute(x.astype(jnp.bfloat16), "ctx", pairs).astype(x.dtype)
    return x


def turned(x, by, length):
    return lax.ppermute(x, "ctx", [(2 * z + n, 2 * ((z + by) % length) + n) for z in range(length) for n in range(2)])


def swapped(piece, places):
    return lax.ppermute(piece, "ctx", [(2 * z + n, 2 * z + 1 - n) for z in places for n in range(2)])


def tied(x, *others):
    return lax.optimization_barrier((x,) + others)[0]


def start_weights(pieces, held_ref, sems):
    place = lax.div(lax.axis_index("ctx"), 2)
    own, beside, middle, outer, far, farthest = pieces
    low = place < 2
    inner = (place == 1) | (place == 2)

    def send(piece, slot):
        pltpu.make_async_copy(piece, held_ref.at[slot], sems.at[slot]).start()

    send(own, place)
    send(beside, place + 1 - 2 * lax.rem(place, 2))

    @pl.when(inner)
    def _():
        send(middle, 3 - place)
        send(far, jnp.where(low, 3, 0))

    @pl.when(jnp.logical_not(inner))
    def _():
        send(outer, jnp.where(low, 2, 1))
        send(farthest, 3 - place)


def weight_at(held_ref, sems, b):
    pltpu.make_async_copy(held_ref.at[b], held_ref.at[b], sems.at[b]).wait()
    return held_ref[b]


def grads_kernel(length, rows_ref, *rest):
    pieces = rest[:6]
    grad_ref, other_ref, held_ref, sems = rest[6:]
    tokens = grad_ref.shape[0]
    width = rows_ref.shape[1] // length
    start_weights(pieces, held_ref, sems)
    total = None
    for b in range(length):
        part = mm(rows_ref[:, b * width : (b + 1) * width], weight_at(held_ref, sems, b), NN)
        total = part if total is None else total + part
    grad_ref[...] = total[:tokens]
    other_ref[...] = total[tokens:].astype(jnp.bfloat16)


def outs_kernel(length, mixed_ref, other_ref, *rest):
    pieces = rest[:6]
    out_ref, held_ref, sems = rest[6:]
    tokens = mixed_ref.shape[0]
    width = out_ref.shape[1] // length
    start_weights(pieces, held_ref, sems)
    for b in range(length):
        weight = weight_at(held_ref, sems, b)
        columns = slice(b * width, (b + 1) * width)
        out_ref[:tokens, columns] = mm(mixed_ref[...], weight, NT).astype(jnp.bfloat16)
        out_ref[tokens:, columns] = mm(other_ref[...], weight, NT).astype(jnp.bfloat16)


def shuffled(n, length):
    return (n % (length // 2)) * 2 + n // (length // 2)


def weight_kernel(length, rows_ref, *rest):
    pieces = rest[:length]
    own_ref, other_ref, held_ref, sems = rest[length:]
    width = own_ref.shape[0]
    place = lax.div(lax.axis_index("ctx"), 2)
    side = lax.rem(lax.axis_index("ctx"), 2)
    for n, piece in enumerate(pieces):
        origin = lax.rem(place - n + length, length)
        slot = lax.rem(origin, length // 2) * 2 + lax.div(origin, length // 2)
        pltpu.make_async_copy(piece, held_ref.at[slot], sems.at[slot]).start()
    for b in range(length):
        pltpu.make_async_copy(held_ref.at[b], held_ref.at[b], sems.at[b]).wait()
    mixed = held_ref[...].reshape(rows_ref.shape[0], -1)
    other = rows_ref[:, pl.ds(pl.multiple_of((1 - side) * width, 128), width)]
    other_ref[...] = mm(other, mixed, TN).astype(jnp.bfloat16)
    own = rows_ref[:, pl.ds(pl.multiple_of(side * width, 128), width)]
    own_ref[...] = mm(own, mixed, TN)


def finish_kernel(scale, run_ref, own_ref, a_ref, b_ref, c_ref, first_ref, key_ref, value_ref):
    there = jnp.where((run_ref[0] == 0) & (pl.program_id(0) == 0), 1.0, 0.0).astype(jnp.float32)
    for n, out_ref in enumerate((key_ref, value_ref)):
        total = own_ref[n] + a_ref[n].astype(jnp.float32) + b_ref[n].astype(jnp.float32) + c_ref[n].astype(jnp.float32)
        total = total + there * first_ref[n]
        out_ref[...] = (total * (scale if n == 0 else 1.0)).astype(jnp.bfloat16)


def runs_away(offset, run):
    side = lax.rem(run, 2)
    if offset == "pair":
        return 1 - 2 * side
    if offset == "across":
        return 2 * side - 1
    return offset


def block_bias(lists_ref, run, per_dev, total_blocks, offset, i, j):
    row = run * per_dev + i
    key = (run + runs_away(offset, run)) * per_dev + j
    hit = (key - row <= 1) & (row - key <= 1)
    for n in range(lists_ref.shape[1]):
        hit = hit | (lists_ref[row, n] == key)
    hit = hit & (key >= 1) & (key < total_blocks)
    return jnp.where(hit, 0.0, -jnp.inf).astype(jnp.float32)


def fwd_kernel(offsets, per_dev, scale, run_ref, lists_ref, q_ref, k_ref, v_ref, *rest):
    bands = rest[: len(offsets)]
    first_ref, mixed_ref, lse_ref, s_ref = rest[len(offsets) :]
    total_blocks = lists_ref.shape[0]
    run = run_ref[0]
    q = q_ref[...]
    tokens = q.shape[0]

    def key_of(p):
        return k_ref[...] if p == 0 else bands[p - 1][0]

    def value_of(p):
        return v_ref[...] if p == 0 else bands[p - 1][1]

    places = (0,) + offsets
    top = None
    for p, offset in enumerate(places):
        s = mm(key_of(p), q, NT) * scale
        for j in range(per_dev):
            for i in range(per_dev):
                part = s[j * BLK : (j + 1) * BLK, i * BLK : (i + 1) * BLK]
                part = part + block_bias(lists_ref, run, per_dev, total_blocks, offset, i, j)
                s_ref[p * tokens + j * BLK : p * tokens + (j + 1) * BLK, i * BLK : (i + 1) * BLK] = part
    s_ref[len(places) * tokens :, :] = mm(first_ref[0], q, NT) * scale
    s = s_ref[...]
    top = jnp.max(s, axis=0, keepdims=True)
    e = jnp.exp(s - top)
    total = jnp.sum(e, axis=0, keepdims=True)
    inverse = 1.0 / total
    low = (e * inverse).astype(jnp.bfloat16)
    out = mm(first_ref[1], low[len(places) * tokens :], TN)
    for p in range(len(places)):
        out = out + mm(value_of(p), low[p * tokens : (p + 1) * tokens], TN)
    mixed_ref[...] = out.T.astype(jnp.bfloat16)
    lse_ref[0] = top + jnp.log(total)


def probs_of(lists_ref, s_ref, run, per_dev, s, offset, lse):
    if offset is None:
        return jnp.exp(s - lse)
    for j in range(per_dev):
        for i in range(per_dev):
            part = s[j * BLK : (j + 1) * BLK, i * BLK : (i + 1) * BLK]
            part = part + block_bias(lists_ref, run, per_dev, lists_ref.shape[0], offset, i, j)
            s_ref[j * BLK : (j + 1) * BLK, i * BLK : (i + 1) * BLK] = part
    return jnp.exp(s_ref[...] - lse)


def first_kernel(offsets, per_dev, scale, run_ref, lists_ref, q_ref, *rest):
    bands = rest[: len(offsets)]
    first_ref, mixed_ref, grad_ref, lse_ref, out_ref, s_ref = rest[len(offsets) :]
    q = q_ref[...]
    grad = grad_ref[...]
    lse = lse_ref[0]
    product = grad.astype(jnp.float32) * mixed_ref[...].astype(jnp.float32)
    delta = jnp.sum(product.T, axis=0, keepdims=True)
    at = 0
    for n, (offset, pair_ref) in enumerate(zip(tuple(offsets) + (None,), bands + (first_ref,))):
        p = probs_of(lists_ref, s_ref.at[n], run_ref[0], per_dev, mm(pair_ref[0], q, NT) * scale, offset, lse)
        slopes = (p * (mm(pair_ref[1], grad, NT) - delta)).astype(jnp.bfloat16)
        rows = slice(at, at + pair_ref.shape[1])
        at = rows.stop
        out_ref[0, rows, :] = mm(slopes, q, NN).astype(jnp.bfloat16)
        out_ref[1, rows, :] = mm(p.astype(jnp.bfloat16), grad, NN).astype(jnp.bfloat16)


def bwd_kernel(offsets, early, per_dev, scale, run_ref, lists_ref, q_ref, k_ref, v_ref, *rest):
    bands = rest[: len(offsets)]
    first_ref, mixed_ref, grad_ref, lse_ref = rest[len(offsets) : len(offsets) + 4]
    outs = rest[len(offsets) + 4 :]
    dq_ref, own_ref = outs[:2]
    band_outs = list(outs[2:-1])
    s_ref = outs[-1]
    q = q_ref[...]
    grad = grad_ref[...]
    lse = lse_ref[0]
    product = grad.astype(jnp.float32) * mixed_ref[...].astype(jnp.float32)
    delta = jnp.sum(product.T, axis=0, keepdims=True)
    dq = None
    plan = [(None, first_ref[0], first_ref[1], None)]
    for offset, pair_ref in zip(offsets, bands):
        plan.append((offset, pair_ref[0], pair_ref[1], None if offset in early else band_outs.pop(0)))
    plan.append((0, k_ref[...], v_ref[...], own_ref))
    for n, (offset, key, value, out_ref) in enumerate(plan):
        p = probs_of(lists_ref, s_ref.at[n], run_ref[0], per_dev, mm(key, q, NT) * scale, offset, lse)
        slopes = (p * (mm(value, grad, NT) - delta)).astype(jnp.bfloat16)
        more = mm(key, slopes, TN)
        dq = more if dq is None else dq + more
        if out_ref is not None:
            out_ref[0] = mm(slopes, q, NN).astype(out_ref.dtype)
            out_ref[1] = mm(p.astype(jnp.bfloat16), grad, NN).astype(out_ref.dtype)
    dq_ref[...] = (dq * scale).T.astype(jnp.bfloat16)


def local(queries, key_heads, value_heads, out_weight, block_lists, out_grad):
    scale = HD ** (-0.5)
    tokens, features = queries.shape
    groups = features // HD
    per_dev = tokens // BLK
    ctx = lax.axis_size("ctx")
    head = lax.axis_size("head")
    run = lax.axis_index("ctx")
    column = lax.axis_index("head")
    reach = -(-REACH // per_dev)
    length = ctx // 2
    direct = ctx == 8 and head == length and reach == 2 and out_grad.shape[1] == 2 * features
    place = run // 2
    side = run % 2
    if direct:
        offsets, early = (-2, 2, "pair", "across"), ("across",)
    else:
        offsets, early = tuple(o for o in range(-reach, reach + 1) if o != 0), ()
    places = 1 + len(offsets)
    smem = pl.BlockSpec(memory_space=pltpu.SMEM)
    whole = pl.BlockSpec(memory_space=pltpu.VMEM)
    anywhere = pl.BlockSpec(memory_space=pl.ANY)
    width = out_weight.shape[0]

    both = jnp.stack([key_heads, value_heads])
    head_rows = both[:, :BLK]
    if direct:
        half = out_grad.shape[1] // 2
        own_half = lax.dynamic_slice_in_dim(out_grad, side * half, half, 1)
        other_half = lax.dynamic_slice_in_dim(out_grad, (1 - side) * half, half, 1)
        before, after = shifted(both, 2), shifted(both, -2)
        beside = swapped(jnp.concatenate([both, other_half[None]], axis=0), range(length))
        grad_side = lax.all_gather(jnp.concatenate([own_half, tied(beside[2], before, after)], axis=0), "head", axis=1, tiled=True)
        sent = jnp.where(side == 0, after, before)
        hop = [(2 * z, 2 * z + 1) for z in range(length - 1)] + [(2 * z + 1, 2 * z) for z in range(1, length)]
        across = lax.ppermute(sent, "ctx", hop)
        known = jnp.where(run == 2, before[:, :BLK], head_rows)
        known = jnp.where((run == 3) | (run == 4), lax.ppermute(known, "ctx", [(2, 4), (0, 3)]), known)
        late = lax.ppermute(known, "ctx", [(4, 6), (3, 5), (2, 7)])
        first = jnp.where(run == 1, beside[:2, :BLK], jnp.where(run > length, late, known))

        def between(x, places):
            return lax.ppermute(x, "ctx", [(2 * a + n, 2 * b + n) for a, b in places for n in range(2)])

        base = tied(out_weight, before, after)
        near = between(base, ((0, 1), (1, 0), (2, 3), (3, 2)))
        middle = between(base, ((1, 2), (2, 1)))
        near, middle, _ = lax.optimization_barrier((near, middle, known))
        far = between(near, ((1, 2), (2, 1)))
        outer = between(middle, ((1, 0), (2, 3)))
        farthest = between(tied(far, across, first), ((1, 0), (2, 3)))
        pairs = []
        for c in range(ctx):
            for h in range(head):
                pairs.append((c * head + h, (2 * h + c % 2) * head + shuffled(c // 2, length)))
        far_rows = lax.ppermute(tied(out_grad, outer, far), ("ctx", "head"), pairs)
        weight_pieces = [base, near, middle, outer, far, farthest]
        bands = [before, after, beside, across]
    else:
        bands = [shifted(both, -o) for o in offsets]
        first = from_first(head_rows)
        grad_full = lax.all_gather(out_grad, "head", axis=1, tiled=True)
        full_weight = lax.all_gather(out_weight, "ctx", axis=0, tiled=True)
        rounds = ctx // head
        mine = jnp.zeros((rounds * tokens, width), jnp.bfloat16)
        for r in range(rounds):
            pairs = []
            for c in range(ctx):
                for h in range(head):
                    pairs.append((c * head + h, (rounds * h + (c + r) % rounds) * head + c // rounds))
            sent = lax.dynamic_slice_in_dim(out_grad, ((run + r) % rounds) * width, width, 1)
            got = lax.ppermute(sent, ("ctx", "head"), pairs)
            mine = lax.dynamic_update_slice_in_dim(mine, got, ((run - r) % rounds) * tokens, 0)
        grad_rows = lax.all_gather(mine, "head", axis=0, tiled=True)

    run_word = run.astype(jnp.int32).reshape(1)
    flat = pl.BlockSpec((tokens, HD), lambda h: (0, h))
    pair = pl.BlockSpec((2, tokens, HD), lambda h: (0, 0, h))
    head_pair = pl.BlockSpec((2, BLK, HD), lambda h: (0, 0, h))
    row = pl.BlockSpec((1, 1, tokens), lambda h: (h, 0, 0))
    keys = places * tokens + BLK
    mixed, lse = pl.pallas_call(
        functools.partial(fwd_kernel, offsets, per_dev, scale),
        grid=(groups,),
        in_specs=[smem, smem, flat, flat, flat] + [pair] * len(offsets) + [head_pair],
        out_specs=[flat, row],
        out_shape=[
            jax.ShapeDtypeStruct((tokens, features), jnp.bfloat16),
            jax.ShapeDtypeStruct((groups, 1, tokens), jnp.float32),
        ],
        scratch_shapes=[pltpu.VMEM((keys, tokens), jnp.float32)],
        compiler_params=pltpu.CompilerParams(vmem_limit_bytes=40 * 1024 * 1024),
        cost_estimate=CHEAP,
        name="attend",
    )(run_word, block_lists, queries, key_heads, value_heads, *bands, first)

    if direct:
        held = [pltpu.VMEM((length, width, features), jnp.bfloat16), pltpu.SemaphoreType.DMA((length,))]
        own_grad, other_grad = pl.pallas_call(
            functools.partial(grads_kernel, length),
            in_specs=[whole] + [anywhere] * 6,
            out_specs=[whole] * 2,
            out_shape=[
                jax.ShapeDtypeStruct((tokens, features), jnp.float32),
                jax.ShapeDtypeStruct((tokens, features), jnp.bfloat16),
            ],
            scratch_shapes=held,
            compiler_params=pltpu.CompilerParams(vmem_limit_bytes=32 * 1024 * 1024),
            cost_estimate=CHEAP,
            name="project_grad",
        )(tied(grad_side, mixed), *weight_pieces)
        mixed_grad = (own_grad + swapped(other_grad, range(length)).astype(jnp.float32)).astype(jnp.bfloat16)
        grad_rows = lax.all_gather(tied(far_rows, other_grad), "head", axis=0, tiled=True)
        mixed_other = tied(swapped(mixed, range(length)), other_grad)
        partial_out = pl.pallas_call(
            functools.partial(outs_kernel, length),
            in_specs=[whole] * 2 + [anywhere] * 6,
            out_specs=pl.BlockSpec((2 * tokens, length * width), lambda: (0, 0)),
            out_shape=jax.ShapeDtypeStruct((2 * tokens, length * width), jnp.bfloat16),
            scratch_shapes=held,
            compiler_params=pltpu.CompilerParams(vmem_limit_bytes=32 * 1024 * 1024),
            cost_estimate=CHEAP,
            name="project_out",
        )(mixed, mixed_other, *weight_pieces)
        scattered = lax.psum_scatter(partial_out, "head", scatter_dimension=1, tiled=True)
        mine, theirs = scattered[:tokens], swapped(scattered[tokens:], range(length))
        attended = jnp.where(
            side == 0, jnp.concatenate([mine, theirs], axis=1), jnp.concatenate([theirs, mine], axis=1)
        )
        mixed_grad = tied(mixed_grad, partial_out)
        mixed_turns = [turned(mixed, n, length) for n in range(1, length)]
    else:
        partial_out = mm(mixed, full_weight, NT).astype(jnp.bfloat16)
        mixed_grad = mm(grad_full, full_weight, NN).astype(jnp.bfloat16)
        mixed_all = lax.all_gather(mixed, "ctx", axis=0, tiled=True)
        attended = lax.psum_scatter(partial_out, "head", scatter_dimension=1, tiled=True)
    early_bands = [band for o, band in zip(offsets, bands) if o in early]
    early_rows = len(early) * tokens + BLK
    early_grads = pl.pallas_call(
        functools.partial(first_kernel, early, per_dev, scale),
        grid=(groups,),
        in_specs=[smem, smem, flat] + [pair] * len(early) + [head_pair, flat, flat, row],
        out_specs=pl.BlockSpec((2, early_rows, HD), lambda h: (0, 0, h)),
        out_shape=jax.ShapeDtypeStruct((2, early_rows, features), jnp.bfloat16),
        scratch_shapes=[pltpu.VMEM((1 + len(early), tokens, tokens), jnp.float32)],
        compiler_params=pltpu.CompilerParams(vmem_limit_bytes=32 * 1024 * 1024),
        cost_estimate=pl.CostEstimate(flops=10_000_000_000, bytes_accessed=1, transcendentals=0),
        name="first_grad",
    )(run_word, block_lists, queries, *early_bands, first, mixed, mixed_grad, lse)

    lse_later = tied(lse, early_grads, *(mixed_turns if direct else ()))
    results = pl.pallas_call(
        functools.partial(bwd_kernel, offsets, early, per_dev, scale),
        grid=(groups,),
        in_specs=[smem, smem, flat, flat, flat] + [pair] * len(offsets) + [head_pair, flat, flat, row],
        out_specs=[flat, pair] + [pair] * (len(offsets) - len(early)),
        out_shape=[
            jax.ShapeDtypeStruct((tokens, features), jnp.bfloat16),
            jax.ShapeDtypeStruct((2, tokens, features), jnp.float32),
        ]
        + [jax.ShapeDtypeStruct((2, tokens, features), jnp.bfloat16)] * (len(offsets) - len(early)),
        scratch_shapes=[pltpu.VMEM((1 + places, tokens, tokens), jnp.float32)],
        compiler_params=pltpu.CompilerParams(vmem_limit_bytes=40 * 1024 * 1024),
        cost_estimate=pl.CostEstimate(flops=30_000_000_000, bytes_accessed=1, transcendentals=0),
        name="attend_grad",
    )(run_word, block_lists, queries, key_heads, value_heads, *bands, first, mixed, mixed_grad, lse_later)
    query_grad, own = results[:2]
    if direct:
        to_before, to_after, to_beside = results[2:]
        swap = tied(swapped(early_grads, range(length)), query_grad)
        diagonal = swap[:, :tokens].astype(jnp.float32)
        first_sum = early_grads[:, tokens:].astype(jnp.float32) + swap[:, tokens:].astype(jnp.float32)
        folded = jnp.pad(jnp.where(run == 2, first_sum, 0.0), ((0, 0), (0, tokens - BLK), (0, 0)))
        to_before = to_before.astype(jnp.float32) + jnp.where(side == 1, diagonal, 0.0) + folded
        to_after = to_after.astype(jnp.float32) + jnp.where(side == 0, diagonal, 0.0)
        back_pair = swapped(to_beside, range(length))
        to_before, to_after = to_before.astype(jnp.bfloat16), to_after.astype(jnp.bfloat16)
        to_before, to_after, near = lax.optimization_barrier((to_before, to_after, first_sum.astype(jnp.bfloat16)))
        back_down = shifted(to_before, -2)
        back_up = shifted(to_after, 2)
        for c in range(length, ctx, 2):
            got = tied(lax.ppermute(near, "ctx", [(c, 0)]), back_down, back_up)
            first_sum = first_sum + got.astype(jnp.float32)
        own_part, other_part = pl.pallas_call(
            functools.partial(weight_kernel, length),
            in_specs=[whole] + [anywhere] * length,
            out_specs=[whole, whole],
            out_shape=[
                jax.ShapeDtypeStruct((width, features), jnp.float32),
                jax.ShapeDtypeStruct((width, features), jnp.bfloat16),
            ],
            scratch_shapes=[pltpu.VMEM((length, tokens, features), jnp.bfloat16), pltpu.SemaphoreType.DMA((length,))],
            compiler_params=pltpu.CompilerParams(vmem_limit_bytes=32 * 1024 * 1024),
            cost_estimate=CHEAP,
            name="weight_sum",
        )(grad_rows, tied(mixed, to_before, to_after), *mixed_turns)
        weight_grad = own_part + swapped(other_part, range(length)).astype(jnp.float32)
        wide = pl.BlockSpec((2, BLK, features), lambda n: (0, n, 0))
        top = pl.BlockSpec((2, BLK, features), lambda n: (0, 0, 0))
        slab = pl.BlockSpec((BLK, features), lambda n: (n, 0))
        key_grad, value_grad = pl.pallas_call(
            functools.partial(finish_kernel, scale),
            grid=(per_dev,),
            in_specs=[smem] + [wide] * 4 + [top],
            out_specs=[slab, slab],
            out_shape=[jax.ShapeDtypeStruct((tokens, features), jnp.bfloat16)] * 2,
            cost_estimate=CHEAP,
            name="finish",
        )(run_word, own, back_pair, back_down, back_up, first_sum)

    else:
        first_sum = to_first(early_grads.astype(jnp.float32))
        sums = own
        for o, part in zip(offsets, results[2:]):
            sums = sums + shifted(part, o).astype(jnp.float32)
        first_sum = jnp.where(run == 0, first_sum, 0.0)
        sums = sums + jnp.pad(first_sum, ((0, 0), (0, tokens - BLK), (0, 0)))
        key_grad = (sums[0] * scale).astype(jnp.bfloat16)
        value_grad = sums[1].astype(jnp.bfloat16)
    if not direct:
        weight_grad = mm(grad_rows, mixed_all, TN)
    return (attended, query_grad, key_grad, value_grad, weight_grad)


def solution(mesh):
    spec = P("ctx", "head")
    return jax.shard_map(
        local,
        mesh=mesh,
        in_specs=(spec, spec, spec, spec, P(), spec),
        out_specs=(spec,) * 5,
        check_vma=False,
    )
```

```python
import functools

import jax
import jax.numpy as jnp
from jax import lax
from jax.experimental import pallas as pl
from jax.experimental.pallas import tpu as pltpu
from jax.sharding import PartitionSpec as P

HD = 128
BLK = 128
REACH = 4

CHEAP = pl.CostEstimate(flops=1, bytes_accessed=1, transcendentals=0)

NT = (((1,), (1,)), ((), ()))
TN = (((0,), (0,)), ((), ()))
NN = (((1,), (0,)), ((), ()))


def mm(a, b, dims):
    return lax.dot_general(a, b, dims, preferred_element_type=jnp.float32)


def shifted(x, by):
    peers = lax.axis_size("ctx")
    return lax.ppermute(x, "ctx", [(i, i + by) for i in range(peers) if 0 <= i + by < peers])


def tree_strides(peers):
    strides = []
    stride = 1
    while stride < peers:
        strides.append(stride)
        stride *= 2
    return strides


def from_first(x):
    peers = lax.axis_size("ctx")
    me = lax.axis_index("ctx")
    for stride in reversed(tree_strides(peers)):
        pairs = [(i, i + stride) for i in range(0, peers, 2 * stride) if i + stride < peers]
        got = lax.ppermute(x, "ctx", pairs)
        x = jnp.where(me % (2 * stride) == stride, got, x)
    return x


def to_first(x):
    peers = lax.axis_size("ctx")
    for stride in tree_strides(peers):
        pairs = [(i + stride, i) for i in range(0, peers, 2 * stride) if i + stride < peers]
        x = x + lax.ppermute(x.astype(jnp.bfloat16), "ctx", pairs).astype(x.dtype)
    return x


def turned(x, by, length):
    return lax.ppermute(x, "ctx", [(2 * z + n, 2 * ((z + by) % length) + n) for z in range(length) for n in range(2)])


def swapped(piece, places):
    return lax.ppermute(piece, "ctx", [(2 * z + n, 2 * z + 1 - n) for z in places for n in range(2)])


def tied(x, *others):
    return lax.optimization_barrier((x,) + others)[0]


def start_weights(pieces, held_ref, sems):
    place = lax.div(lax.axis_index("ctx"), 2)
    own, beside, middle, outer, far, farthest = pieces
    low = place < 2
    inner = (place == 1) | (place == 2)

    def send(piece, slot):
        pltpu.make_async_copy(piece, held_ref.at[slot], sems.at[slot]).start()

    send(own, place)
    send(beside, place + 1 - 2 * lax.rem(place, 2))

    @pl.when(inner)
    def _():
        send(middle, 3 - place)
        send(far, jnp.where(low, 3, 0))

    @pl.when(jnp.logical_not(inner))
    def _():
        send(outer, jnp.where(low, 2, 1))
        send(farthest, 3 - place)


def weight_at(held_ref, sems, b):
    pltpu.make_async_copy(held_ref.at[b], held_ref.at[b], sems.at[b]).wait()
    return held_ref[b]


def grads_kernel(length, rows_ref, *rest):
    pieces = rest[:6]
    grad_ref, other_ref, held_ref, sems = rest[6:]
    tokens = grad_ref.shape[0]
    width = rows_ref.shape[1] // length
    start_weights(pieces, held_ref, sems)
    total = None
    for b in range(length):
        part = mm(rows_ref[:, b * width : (b + 1) * width], weight_at(held_ref, sems, b), NN)
        total = part if total is None else total + part
    grad_ref[...] = total[:tokens]
    other_ref[...] = total[tokens:].astype(jnp.bfloat16)


def outs_kernel(length, mixed_ref, other_ref, *rest):
    pieces = rest[:6]
    out_ref, held_ref, sems = rest[6:]
    tokens = mixed_ref.shape[0]
    width = out_ref.shape[1] // length
    start_weights(pieces, held_ref, sems)
    for b in range(length):
        weight = weight_at(held_ref, sems, b)
        columns = slice(b * width, (b + 1) * width)
        out_ref[:tokens, columns] = mm(mixed_ref[...], weight, NT).astype(jnp.bfloat16)
        out_ref[tokens:, columns] = mm(other_ref[...], weight, NT).astype(jnp.bfloat16)


def weight_kernel(length, rows_ref, mixed_ref, other_ref, own_ref, *rest):
    sends = rest[: length - 1]
    (both_ref,) = rest[length - 1 :]
    width = own_ref.shape[0]
    tokens = mixed_ref.shape[0]
    place = lax.div(lax.axis_index("ctx"), 2)
    both_ref[:tokens, :] = mixed_ref[...]
    both_ref[tokens:, :] = other_ref[...]
    for n, out_ref in enumerate((own_ref,) + sends):
        column = pl.multiple_of(lax.rem(place + n, length) * width, 128)
        out_ref[...] = mm(rows_ref[:, pl.ds(column, width)], both_ref[...], TN).astype(out_ref.dtype)


def finish_kernel(scale, run_ref, own_ref, a_ref, b_ref, c_ref, first_ref, key_ref, value_ref):
    there = jnp.where((run_ref[0] == 0) & (pl.program_id(0) == 0), 1.0, 0.0).astype(jnp.float32)
    for n, out_ref in enumerate((key_ref, value_ref)):
        total = own_ref[n] + a_ref[n].astype(jnp.float32) + b_ref[n].astype(jnp.float32) + c_ref[n].astype(jnp.float32)
        total = total + there * first_ref[n]
        out_ref[...] = (total * (scale if n == 0 else 1.0)).astype(jnp.bfloat16)


def runs_away(offset, run):
    side = lax.rem(run, 2)
    if offset == "pair":
        return 1 - 2 * side
    if offset == "across":
        return 2 * side - 1
    return offset


def block_bias(lists_ref, run, per_dev, total_blocks, offset, i, j):
    row = run * per_dev + i
    key = (run + runs_away(offset, run)) * per_dev + j
    hit = (key - row <= 1) & (row - key <= 1)
    for n in range(lists_ref.shape[1]):
        hit = hit | (lists_ref[row, n] == key)
    hit = hit & (key >= 1) & (key < total_blocks)
    return jnp.where(hit, 0.0, -jnp.inf).astype(jnp.float32)


def fwd_kernel(offsets, per_dev, scale, run_ref, lists_ref, q_ref, k_ref, v_ref, *rest):
    bands = rest[: len(offsets)]
    first_ref, mixed_ref, lse_ref, s_ref = rest[len(offsets) :]
    total_blocks = lists_ref.shape[0]
    run = run_ref[0]
    q = q_ref[...]
    tokens = q.shape[0]

    def key_of(p):
        return k_ref[...] if p == 0 else bands[p - 1][0]

    def value_of(p):
        return v_ref[...] if p == 0 else bands[p - 1][1]

    places = (0,) + offsets
    top = None
    for p, offset in enumerate(places):
        s = mm(key_of(p), q, NT) * scale
        for j in range(per_dev):
            for i in range(per_dev):
                part = s[j * BLK : (j + 1) * BLK, i * BLK : (i + 1) * BLK]
                part = part + block_bias(lists_ref, run, per_dev, total_blocks, offset, i, j)
                s_ref[p * tokens + j * BLK : p * tokens + (j + 1) * BLK, i * BLK : (i + 1) * BLK] = part
    s_ref[len(places) * tokens :, :] = mm(first_ref[0], q, NT) * scale
    s = s_ref[...]
    top = jnp.max(s, axis=0, keepdims=True)
    e = jnp.exp(s - top)
    total = jnp.sum(e, axis=0, keepdims=True)
    inverse = 1.0 / total
    low = (e * inverse).astype(jnp.bfloat16)
    out = mm(first_ref[1], low[len(places) * tokens :], TN)
    for p in range(len(places)):
        out = out + mm(value_of(p), low[p * tokens : (p + 1) * tokens], TN)
    mixed_ref[...] = out.T.astype(jnp.bfloat16)
    lse_ref[0] = top + jnp.log(total)


def probs_of(lists_ref, s_ref, run, per_dev, s, offset, lse):
    if offset is None:
        return jnp.exp(s - lse)
    for j in range(per_dev):
        for i in range(per_dev):
            part = s[j * BLK : (j + 1) * BLK, i * BLK : (i + 1) * BLK]
            part = part + block_bias(lists_ref, run, per_dev, lists_ref.shape[0], offset, i, j)
            s_ref[j * BLK : (j + 1) * BLK, i * BLK : (i + 1) * BLK] = part
    return jnp.exp(s_ref[...] - lse)


def first_kernel(offsets, per_dev, scale, run_ref, lists_ref, q_ref, *rest):
    bands = rest[: len(offsets)]
    first_ref, mixed_ref, grad_ref, lse_ref, out_ref, s_ref = rest[len(offsets) :]
    q = q_ref[...]
    grad = grad_ref[...]
    lse = lse_ref[0]
    product = grad.astype(jnp.float32) * mixed_ref[...].astype(jnp.float32)
    delta = jnp.sum(product.T, axis=0, keepdims=True)
    at = 0
    for n, (offset, pair_ref) in enumerate(zip(tuple(offsets) + (None,), bands + (first_ref,))):
        p = probs_of(lists_ref, s_ref.at[n], run_ref[0], per_dev, mm(pair_ref[0], q, NT) * scale, offset, lse)
        slopes = (p * (mm(pair_ref[1], grad, NT) - delta)).astype(jnp.bfloat16)
        rows = slice(at, at + pair_ref.shape[1])
        at = rows.stop
        out_ref[0, rows, :] = mm(slopes, q, NN).astype(jnp.bfloat16)
        out_ref[1, rows, :] = mm(p.astype(jnp.bfloat16), grad, NN).astype(jnp.bfloat16)


def bwd_kernel(offsets, early, per_dev, scale, run_ref, lists_ref, q_ref, k_ref, v_ref, *rest):
    bands = rest[: len(offsets)]
    first_ref, mixed_ref, grad_ref, lse_ref = rest[len(offsets) : len(offsets) + 4]
    outs = rest[len(offsets) + 4 :]
    dq_ref, own_ref = outs[:2]
    band_outs = list(outs[2:-1])
    s_ref = outs[-1]
    q = q_ref[...]
    grad = grad_ref[...]
    lse = lse_ref[0]
    product = grad.astype(jnp.float32) * mixed_ref[...].astype(jnp.float32)
    delta = jnp.sum(product.T, axis=0, keepdims=True)
    dq = None
    plan = [(None, first_ref[0], first_ref[1], None)]
    for offset, pair_ref in zip(offsets, bands):
        plan.append((offset, pair_ref[0], pair_ref[1], None if offset in early else band_outs.pop(0)))
    plan.append((0, k_ref[...], v_ref[...], own_ref))
    for n, (offset, key, value, out_ref) in enumerate(plan):
        p = probs_of(lists_ref, s_ref.at[n], run_ref[0], per_dev, mm(key, q, NT) * scale, offset, lse)
        slopes = (p * (mm(value, grad, NT) - delta)).astype(jnp.bfloat16)
        more = mm(key, slopes, TN)
        dq = more if dq is None else dq + more
        if out_ref is not None:
            out_ref[0] = mm(slopes, q, NN).astype(out_ref.dtype)
            out_ref[1] = mm(p.astype(jnp.bfloat16), grad, NN).astype(out_ref.dtype)
    dq_ref[...] = (dq * scale).T.astype(jnp.bfloat16)


def local(queries, key_heads, value_heads, out_weight, block_lists, out_grad):
    scale = HD ** (-0.5)
    tokens, features = queries.shape
    groups = features // HD
    per_dev = tokens // BLK
    ctx = lax.axis_size("ctx")
    head = lax.axis_size("head")
    run = lax.axis_index("ctx")
    column = lax.axis_index("head")
    reach = -(-REACH // per_dev)
    length = ctx // 2
    direct = ctx == 8 and head == length and reach == 2 and out_grad.shape[1] == 2 * features
    place = run // 2
    side = run % 2
    if direct:
        offsets, early = (-2, 2, "pair", "across"), ("across",)
    else:
        offsets, early = tuple(o for o in range(-reach, reach + 1) if o != 0), ()
    places = 1 + len(offsets)
    smem = pl.BlockSpec(memory_space=pltpu.SMEM)
    whole = pl.BlockSpec(memory_space=pltpu.VMEM)
    anywhere = pl.BlockSpec(memory_space=pl.ANY)
    width = out_weight.shape[0]

    both = jnp.stack([key_heads, value_heads])
    head_rows = both[:, :BLK]
    if direct:
        half = out_grad.shape[1] // 2
        own_half = lax.dynamic_slice_in_dim(out_grad, side * half, half, 1)
        other_half = lax.dynamic_slice_in_dim(out_grad, (1 - side) * half, half, 1)
        before, after = shifted(both, 2), shifted(both, -2)
        beside = swapped(jnp.concatenate([both, other_half[None]], axis=0), range(length))
        grad_side = lax.all_gather(jnp.concatenate([own_half, tied(beside[2], before, after)], axis=0), "head", axis=1, tiled=True)
        sent = jnp.where(side == 0, after, before)
        hop = [(2 * z, 2 * z + 1) for z in range(length - 1)] + [(2 * z + 1, 2 * z) for z in range(1, length)]
        across = lax.ppermute(sent, "ctx", hop)
        known = jnp.where(run == 1, beside[:2, :BLK], head_rows)
        known = jnp.where(run == 2, before[:, :BLK], known)
        middle_rows = lax.ppermute(head_rows, "ctx", [(0, length)])
        known = jnp.where(run == length, middle_rows, known)
        late = lax.ppermute(known, "ctx", [(1, 7), (0, 3), (4, 5), (2, 6)])
        first = jnp.where((run == 3) | (run > length), late, known)

        def between(x, places):
            return lax.ppermute(x, "ctx", [(2 * a + n, 2 * b + n) for a, b in places for n in range(2)])

        base = tied(out_weight, before, after, middle_rows)
        near = between(base, ((0, 1), (1, 0), (2, 3), (3, 2)))
        middle = between(base, ((1, 2), (2, 1)))
        far = between(near, ((1, 2), (2, 1)))
        outer = between(middle, ((1, 0), (2, 3)))
        farthest = between(far, ((1, 0), (2, 3)))
        weight_pieces = [base, near, middle, outer, far, farthest]
        bands = [before, after, beside, across]
    else:
        bands = [shifted(both, -o) for o in offsets]
        first = from_first(head_rows)
        grad_full = lax.all_gather(out_grad, "head", axis=1, tiled=True)
        full_weight = lax.all_gather(out_weight, "ctx", axis=0, tiled=True)
        rounds = ctx // head
        mine = jnp.zeros((rounds * tokens, width), jnp.bfloat16)
        for r in range(rounds):
            pairs = []
            for c in range(ctx):
                for h in range(head):
                    pairs.append((c * head + h, (rounds * h + (c + r) % rounds) * head + c // rounds))
            sent = lax.dynamic_slice_in_dim(out_grad, ((run + r) % rounds) * width, width, 1)
            got = lax.ppermute(sent, ("ctx", "head"), pairs)
            mine = lax.dynamic_update_slice_in_dim(mine, got, ((run - r) % rounds) * tokens, 0)
        grad_rows = lax.all_gather(mine, "head", axis=0, tiled=True)

    run_word = run.astype(jnp.int32).reshape(1)
    flat = pl.BlockSpec((tokens, HD), lambda h: (0, h))
    pair = pl.BlockSpec((2, tokens, HD), lambda h: (0, 0, h))
    head_pair = pl.BlockSpec((2, BLK, HD), lambda h: (0, 0, h))
    row = pl.BlockSpec((1, 1, tokens), lambda h: (h, 0, 0))
    keys = places * tokens + BLK
    mixed, lse = pl.pallas_call(
        functools.partial(fwd_kernel, offsets, per_dev, scale),
        grid=(groups,),
        in_specs=[smem, smem, flat, flat, flat] + [pair] * len(offsets) + [head_pair],
        out_specs=[flat, row],
        out_shape=[
            jax.ShapeDtypeStruct((tokens, features), jnp.bfloat16),
            jax.ShapeDtypeStruct((groups, 1, tokens), jnp.float32),
        ],
        scratch_shapes=[pltpu.VMEM((keys, tokens), jnp.float32)],
        compiler_params=pltpu.CompilerParams(vmem_limit_bytes=40 * 1024 * 1024),
        cost_estimate=CHEAP,
        name="attend",
    )(run_word, block_lists, queries, key_heads, value_heads, *bands, first)

    if direct:
        held = [pltpu.VMEM((length, width, features), jnp.bfloat16), pltpu.SemaphoreType.DMA((length,))]
        own_grad, other_grad = pl.pallas_call(
            functools.partial(grads_kernel, length),
            in_specs=[whole] + [anywhere] * 6,
            out_specs=[whole] * 2,
            out_shape=[
                jax.ShapeDtypeStruct((tokens, features), jnp.float32),
                jax.ShapeDtypeStruct((tokens, features), jnp.bfloat16),
            ],
            scratch_shapes=held,
            compiler_params=pltpu.CompilerParams(vmem_limit_bytes=32 * 1024 * 1024),
            cost_estimate=CHEAP,
            name="project_grad",
        )(grad_side, *weight_pieces)
        mixed_grad = (own_grad + swapped(other_grad, range(length)).astype(jnp.float32)).astype(jnp.bfloat16)
        mixed_other = tied(swapped(mixed, range(length)), other_grad)
        own_part, *weight_parts = pl.pallas_call(
            functools.partial(weight_kernel, length),
            in_specs=[whole] + [whole] * 2,
            out_specs=[whole] * length,
            out_shape=[jax.ShapeDtypeStruct((width, features), jnp.float32)]
            + [jax.ShapeDtypeStruct((width, features), jnp.bfloat16)] * (length - 1),
            scratch_shapes=[pltpu.VMEM((2 * tokens, features), jnp.bfloat16)],
            compiler_params=pltpu.CompilerParams(vmem_limit_bytes=32 * 1024 * 1024),
            cost_estimate=CHEAP,
            name="weight_part",
        )(grad_side, mixed, mixed_other)
        partial_out = pl.pallas_call(
            functools.partial(outs_kernel, length),
            in_specs=[whole] * 2 + [anywhere] * 6,
            out_specs=pl.BlockSpec((2 * tokens, length * width), lambda: (0, 0)),
            out_shape=jax.ShapeDtypeStruct((2 * tokens, length * width), jnp.bfloat16),
            scratch_shapes=held,
            compiler_params=pltpu.CompilerParams(vmem_limit_bytes=32 * 1024 * 1024),
            cost_estimate=CHEAP,
            name="project_out",
        )(mixed, tied(mixed_other, own_part), *weight_pieces)
        scattered = lax.psum_scatter(partial_out, "head", scatter_dimension=1, tiled=True)
        mixed_grad = tied(mixed_grad, own_part)
        weight_turns = [turned(weight_parts[n - 1], n, length) for n in (1, 3)]
    else:
        partial_out = mm(mixed, full_weight, NT).astype(jnp.bfloat16)
        mixed_grad = mm(grad_full, full_weight, NN).astype(jnp.bfloat16)
        mixed_all = lax.all_gather(mixed, "ctx", axis=0, tiled=True)
        attended = lax.psum_scatter(partial_out, "head", scatter_dimension=1, tiled=True)
    early_bands = [band for o, band in zip(offsets, bands) if o in early]
    early_rows = len(early) * tokens + BLK
    early_grads = pl.pallas_call(
        functools.partial(first_kernel, early, per_dev, scale),
        grid=(groups,),
        in_specs=[smem, smem, flat] + [pair] * len(early) + [head_pair, flat, flat, row],
        out_specs=pl.BlockSpec((2, early_rows, HD), lambda h: (0, 0, h)),
        out_shape=jax.ShapeDtypeStruct((2, early_rows, features), jnp.bfloat16),
        scratch_shapes=[pltpu.VMEM((1 + len(early), tokens, tokens), jnp.float32)],
        compiler_params=pltpu.CompilerParams(vmem_limit_bytes=32 * 1024 * 1024),
        cost_estimate=pl.CostEstimate(flops=10_000_000_000, bytes_accessed=1, transcendentals=0),
        name="first_grad",
    )(run_word, block_lists, queries, *early_bands, first, mixed, mixed_grad, lse)

    lse_later = tied(lse, early_grads, partial_out)
    results = pl.pallas_call(
        functools.partial(bwd_kernel, offsets, early, per_dev, scale),
        grid=(groups,),
        in_specs=[smem, smem, flat, flat, flat] + [pair] * len(offsets) + [head_pair, flat, flat, row],
        out_specs=[flat, pair] + [pair] * (len(offsets) - len(early)),
        out_shape=[
            jax.ShapeDtypeStruct((tokens, features), jnp.bfloat16),
            jax.ShapeDtypeStruct((2, tokens, features), jnp.float32),
        ]
        + [jax.ShapeDtypeStruct((2, tokens, features), jnp.bfloat16)] * (len(offsets) - len(early)),
        scratch_shapes=[pltpu.VMEM((1 + places, tokens, tokens), jnp.float32)],
        compiler_params=pltpu.CompilerParams(vmem_limit_bytes=40 * 1024 * 1024),
        cost_estimate=pl.CostEstimate(flops=30_000_000_000, bytes_accessed=1, transcendentals=0),
        name="attend_grad",
    )(run_word, block_lists, queries, key_heads, value_heads, *bands, first, mixed, mixed_grad, lse_later)
    query_grad, own = results[:2]
    if direct:
        to_before, to_after, to_beside = results[2:]
        swap = tied(swapped(early_grads, range(length)), query_grad)
        diagonal = swap[:, :tokens].astype(jnp.float32)
        first_sum = early_grads[:, tokens:].astype(jnp.float32) + swap[:, tokens:].astype(jnp.float32)
        folded = jnp.pad(jnp.where(run == 2, first_sum, 0.0), ((0, 0), (0, tokens - BLK), (0, 0)))
        to_before, to_after, _ = lax.optimization_barrier((to_before, to_after, weight_turns))
        to_before = to_before.astype(jnp.float32) + jnp.where(side == 1, diagonal, 0.0) + folded
        to_after = to_after.astype(jnp.float32) + jnp.where(side == 0, diagonal, 0.0)
        back_pair = swapped(to_beside, range(length))
        to_before, to_after = to_before.astype(jnp.bfloat16), to_after.astype(jnp.bfloat16)
        to_before, to_after, near, last_part = lax.optimization_barrier(
            (to_before, to_after, first_sum.astype(jnp.bfloat16), weight_parts[1])
        )
        back_down = shifted(to_before, -2)
        back_up = shifted(to_after, 2)
        scattered = tied(scattered, back_pair)
        mine, theirs = scattered[:tokens], swapped(scattered[tokens:], range(length))
        attended = jnp.where(
            side == 0, jnp.concatenate([mine, theirs], axis=1), jnp.concatenate([theirs, mine], axis=1)
        )
        weight_grad = own_part
        for part in weight_turns + [turned(last_part, 2, length)]:
            weight_grad = weight_grad + part.astype(jnp.float32)
        for c in range(length, ctx, 2):
            got = tied(lax.ppermute(near, "ctx", [(c, 0)]), back_down, back_up, attended)
            first_sum = first_sum + got.astype(jnp.float32)
        wide = pl.BlockSpec((2, BLK, features), lambda n: (0, n, 0))
        top = pl.BlockSpec((2, BLK, features), lambda n: (0, 0, 0))
        slab = pl.BlockSpec((BLK, features), lambda n: (n, 0))
        key_grad, value_grad = pl.pallas_call(
            functools.partial(finish_kernel, scale),
            grid=(per_dev,),
            in_specs=[smem] + [wide] * 4 + [top],
            out_specs=[slab, slab],
            out_shape=[jax.ShapeDtypeStruct((tokens, features), jnp.bfloat16)] * 2,
            cost_estimate=CHEAP,
            name="finish",
        )(run_word, own, back_pair, back_down, back_up, first_sum)

    else:
        first_sum = to_first(early_grads.astype(jnp.float32))
        sums = own
        for o, part in zip(offsets, results[2:]):
            sums = sums + shifted(part, o).astype(jnp.float32)
        first_sum = jnp.where(run == 0, first_sum, 0.0)
        sums = sums + jnp.pad(first_sum, ((0, 0), (0, tokens - BLK), (0, 0)))
        key_grad = (sums[0] * scale).astype(jnp.bfloat16)
        value_grad = sums[1].astype(jnp.bfloat16)
    if not direct:
        weight_grad = mm(grad_rows, mixed_all, TN)
    return (attended, query_grad, key_grad, value_grad, weight_grad)


def solution(mesh):
    spec = P("ctx", "head")
    return jax.shard_map(
        local,
        mesh=mesh,
        in_specs=(spec, spec, spec, spec, P(), spec),
        out_specs=(spec,) * 5,
        check_vma=False,
    )
```

```python
import functools

import jax
import jax.numpy as jnp
from jax import lax
from jax.experimental import pallas as pl
from jax.experimental.pallas import tpu as pltpu
from jax.sharding import PartitionSpec as P

HD = 128
BLK = 128
REACH = 4

CHEAP = pl.CostEstimate(flops=1, bytes_accessed=1, transcendentals=0)

NT = (((1,), (1,)), ((), ()))
TN = (((0,), (0,)), ((), ()))
NN = (((1,), (0,)), ((), ()))


def mm(a, b, dims):
    return lax.dot_general(a, b, dims, preferred_element_type=jnp.float32)


def shifted(x, by):
    peers = lax.axis_size("ctx")
    return lax.ppermute(x, "ctx", [(i, i + by) for i in range(peers) if 0 <= i + by < peers])


def tree_strides(peers):
    strides = []
    stride = 1
    while stride < peers:
        strides.append(stride)
        stride *= 2
    return strides


def from_first(x):
    peers = lax.axis_size("ctx")
    me = lax.axis_index("ctx")
    for stride in reversed(tree_strides(peers)):
        pairs = [(i, i + stride) for i in range(0, peers, 2 * stride) if i + stride < peers]
        got = lax.ppermute(x, "ctx", pairs)
        x = jnp.where(me % (2 * stride) == stride, got, x)
    return x


def to_first(x):
    peers = lax.axis_size("ctx")
    for stride in tree_strides(peers):
        pairs = [(i + stride, i) for i in range(0, peers, 2 * stride) if i + stride < peers]
        x = x + lax.ppermute(x.astype(jnp.bfloat16), "ctx", pairs).astype(x.dtype)
    return x


def turned(x, by, length):
    return lax.ppermute(x, "ctx", [(2 * z + n, 2 * ((z + by) % length) + n) for z in range(length) for n in range(2)])


def swapped(piece, places):
    return lax.ppermute(piece, "ctx", [(2 * z + n, 2 * z + 1 - n) for z in places for n in range(2)])


def tied(x, *others):
    return lax.optimization_barrier((x,) + others)[0]


def start_weights(pieces, held_ref, sems):
    place = lax.div(lax.axis_index("ctx"), 2)
    own, beside, middle, outer, far, farthest = pieces
    low = place < 2
    inner = (place == 1) | (place == 2)

    def send(piece, slot):
        pltpu.make_async_copy(piece, held_ref.at[slot], sems.at[slot]).start()

    send(own, place)
    send(beside, place + 1 - 2 * lax.rem(place, 2))

    @pl.when(inner)
    def _():
        send(middle, 3 - place)
        send(far, jnp.where(low, 3, 0))

    @pl.when(jnp.logical_not(inner))
    def _():
        send(outer, jnp.where(low, 2, 1))
        send(farthest, 3 - place)


def weight_at(held_ref, sems, b):
    pltpu.make_async_copy(held_ref.at[b], held_ref.at[b], sems.at[b]).wait()
    return held_ref[b]


def grads_kernel(length, rows_ref, *rest):
    pieces = rest[:6]
    grad_ref, other_ref, held_ref, sems = rest[6:]
    tokens = grad_ref.shape[0]
    width = rows_ref.shape[1] // length
    start_weights(pieces, held_ref, sems)
    total = None
    for b in range(length):
        part = mm(rows_ref[:, b * width : (b + 1) * width], weight_at(held_ref, sems, b), NN)
        total = part if total is None else total + part
    grad_ref[...] = total[:tokens]
    other_ref[...] = total[tokens:].astype(jnp.bfloat16)


def outs_kernel(length, mixed_ref, other_ref, *rest):
    pieces = rest[:6]
    out_ref, held_ref, sems = rest[6:]
    tokens = mixed_ref.shape[0]
    width = out_ref.shape[1] // length
    start_weights(pieces, held_ref, sems)
    for b in range(length):
        weight = weight_at(held_ref, sems, b)
        columns = slice(b * width, (b + 1) * width)
        out_ref[:tokens, columns] = mm(mixed_ref[...], weight, NT).astype(jnp.bfloat16)
        out_ref[tokens:, columns] = mm(other_ref[...], weight, NT).astype(jnp.bfloat16)


def weight_kernel(length, rows_ref, mixed_ref, other_ref, own_ref, *rest):
    sends = rest[: length - 1]
    (both_ref,) = rest[length - 1 :]
    width = own_ref.shape[0]
    tokens = mixed_ref.shape[0]
    place = lax.div(lax.axis_index("ctx"), 2)
    both_ref[:tokens, :] = mixed_ref[...]
    both_ref[tokens:, :] = other_ref[...]
    for n, out_ref in enumerate((own_ref,) + sends):
        column = pl.multiple_of(lax.rem(place + n, length) * width, 128)
        out_ref[...] = mm(rows_ref[:, pl.ds(column, width)], both_ref[...], TN).astype(out_ref.dtype)


def finish_kernel(scale, run_ref, own_ref, a_ref, b_ref, c_ref, first_ref, key_ref, value_ref):
    there = jnp.where((run_ref[0] == 0) & (pl.program_id(0) == 0), 1.0, 0.0).astype(jnp.float32)
    for n, out_ref in enumerate((key_ref, value_ref)):
        total = own_ref[n] + a_ref[n].astype(jnp.float32) + b_ref[n].astype(jnp.float32) + c_ref[n].astype(jnp.float32)
        total = total + there * first_ref[n]
        out_ref[...] = (total * (scale if n == 0 else 1.0)).astype(jnp.bfloat16)


def runs_away(offset, run):
    side = lax.rem(run, 2)
    if offset == "pair":
        return 1 - 2 * side
    if offset == "across":
        return 2 * side - 1
    return offset


def block_bias(lists_ref, run, per_dev, total_blocks, offset, i, j):
    row = run * per_dev + i
    key = (run + runs_away(offset, run)) * per_dev + j
    hit = (key - row <= 1) & (row - key <= 1)
    for n in range(lists_ref.shape[1]):
        hit = hit | (lists_ref[row, n] == key)
    hit = hit & (key >= 1) & (key < total_blocks)
    return jnp.where(hit, 0.0, -jnp.inf).astype(jnp.float32)


def fwd_kernel(offsets, per_dev, scale, run_ref, lists_ref, q_ref, k_ref, v_ref, *rest):
    bands = rest[: len(offsets)]
    first_ref, mixed_ref, lse_ref, s_ref = rest[len(offsets) :]
    total_blocks = lists_ref.shape[0]
    run = run_ref[0]
    q = q_ref[...]
    tokens = q.shape[0]

    def key_of(p):
        return k_ref[...] if p == 0 else bands[p - 1][0]

    def value_of(p):
        return v_ref[...] if p == 0 else bands[p - 1][1]

    places = (0,) + offsets
    top = None
    for p, offset in enumerate(places):
        s = mm(key_of(p), q, NT) * scale
        for j in range(per_dev):
            for i in range(per_dev):
                part = s[j * BLK : (j + 1) * BLK, i * BLK : (i + 1) * BLK]
                part = part + block_bias(lists_ref, run, per_dev, total_blocks, offset, i, j)
                s_ref[p * tokens + j * BLK : p * tokens + (j + 1) * BLK, i * BLK : (i + 1) * BLK] = part
    s_ref[len(places) * tokens :, :] = mm(first_ref[0], q, NT) * scale
    s = s_ref[...]
    top = jnp.max(s, axis=0, keepdims=True)
    e = jnp.exp(s - top)
    total = jnp.sum(e, axis=0, keepdims=True)
    inverse = 1.0 / total
    low = (e * inverse).astype(jnp.bfloat16)
    out = mm(first_ref[1], low[len(places) * tokens :], TN)
    for p in range(len(places)):
        out = out + mm(value_of(p), low[p * tokens : (p + 1) * tokens], TN)
    mixed_ref[...] = out.T.astype(jnp.bfloat16)
    lse_ref[0] = top + jnp.log(total)


def probs_of(lists_ref, s_ref, run, per_dev, s, offset, lse):
    if offset is None:
        return jnp.exp(s - lse)
    for j in range(per_dev):
        for i in range(per_dev):
            part = s[j * BLK : (j + 1) * BLK, i * BLK : (i + 1) * BLK]
            part = part + block_bias(lists_ref, run, per_dev, lists_ref.shape[0], offset, i, j)
            s_ref[j * BLK : (j + 1) * BLK, i * BLK : (i + 1) * BLK] = part
    return jnp.exp(s_ref[...] - lse)


def first_kernel(offsets, per_dev, scale, run_ref, lists_ref, q_ref, *rest):
    bands = rest[: len(offsets)]
    first_ref, mixed_ref, grad_ref, lse_ref, out_ref, s_ref = rest[len(offsets) :]
    q = q_ref[...]
    grad = grad_ref[...]
    lse = lse_ref[0]
    product = grad.astype(jnp.float32) * mixed_ref[...].astype(jnp.float32)
    delta = jnp.sum(product.T, axis=0, keepdims=True)
    at = 0
    for n, (offset, pair_ref) in enumerate(zip(tuple(offsets) + (None,), bands + (first_ref,))):
        p = probs_of(lists_ref, s_ref.at[n], run_ref[0], per_dev, mm(pair_ref[0], q, NT) * scale, offset, lse)
        slopes = (p * (mm(pair_ref[1], grad, NT) - delta)).astype(jnp.bfloat16)
        rows = slice(at, at + pair_ref.shape[1])
        at = rows.stop
        out_ref[0, rows, :] = mm(slopes, q, NN).astype(jnp.bfloat16)
        out_ref[1, rows, :] = mm(p.astype(jnp.bfloat16), grad, NN).astype(jnp.bfloat16)


def bwd_kernel(offsets, early, per_dev, scale, run_ref, lists_ref, q_ref, k_ref, v_ref, *rest):
    bands = rest[: len(offsets)]
    first_ref, mixed_ref, grad_ref, lse_ref = rest[len(offsets) : len(offsets) + 4]
    outs = rest[len(offsets) + 4 :]
    dq_ref, own_ref = outs[:2]
    band_outs = list(outs[2:-1])
    s_ref = outs[-1]
    q = q_ref[...]
    grad = grad_ref[...]
    lse = lse_ref[0]
    product = grad.astype(jnp.float32) * mixed_ref[...].astype(jnp.float32)
    delta = jnp.sum(product.T, axis=0, keepdims=True)
    dq = None
    plan = [(None, first_ref[0], first_ref[1], None)]
    for offset, pair_ref in zip(offsets, bands):
        plan.append((offset, pair_ref[0], pair_ref[1], None if offset in early else band_outs.pop(0)))
    plan.append((0, k_ref[...], v_ref[...], own_ref))
    for n, (offset, key, value, out_ref) in enumerate(plan):
        p = probs_of(lists_ref, s_ref.at[n], run_ref[0], per_dev, mm(key, q, NT) * scale, offset, lse)
        slopes = (p * (mm(value, grad, NT) - delta)).astype(jnp.bfloat16)
        more = mm(key, slopes, TN)
        dq = more if dq is None else dq + more
        if out_ref is not None:
            out_ref[0] = mm(slopes, q, NN).astype(out_ref.dtype)
            out_ref[1] = mm(p.astype(jnp.bfloat16), grad, NN).astype(out_ref.dtype)
    dq_ref[...] = (dq * scale).T.astype(jnp.bfloat16)


def local(queries, key_heads, value_heads, out_weight, block_lists, out_grad):
    scale = HD ** (-0.5)
    tokens, features = queries.shape
    groups = features // HD
    per_dev = tokens // BLK
    ctx = lax.axis_size("ctx")
    head = lax.axis_size("head")
    run = lax.axis_index("ctx")
    column = lax.axis_index("head")
    reach = -(-REACH // per_dev)
    length = ctx // 2
    direct = ctx == 8 and head == length and reach == 2 and out_grad.shape[1] == 2 * features
    place = run // 2
    side = run % 2
    if direct:
        offsets, early = (-2, 2, "pair", "across"), ("across",)
    else:
        offsets, early = tuple(o for o in range(-reach, reach + 1) if o != 0), ()
    places = 1 + len(offsets)
    smem = pl.BlockSpec(memory_space=pltpu.SMEM)
    whole = pl.BlockSpec(memory_space=pltpu.VMEM)
    anywhere = pl.BlockSpec(memory_space=pl.ANY)
    width = out_weight.shape[0]

    both = jnp.stack([key_heads, value_heads])
    head_rows = both[:, :BLK]
    if direct:
        half = out_grad.shape[1] // 2
        own_half = lax.dynamic_slice_in_dim(out_grad, side * half, half, 1)
        other_half = lax.dynamic_slice_in_dim(out_grad, (1 - side) * half, half, 1)
        before, after = shifted(both, 2), shifted(both, -2)
        beside = swapped(jnp.concatenate([both, other_half[None]], axis=0), range(length))
        grad_side = lax.all_gather(jnp.concatenate([own_half, tied(beside[2], before, after)], axis=0), "head", axis=1, tiled=True)
        sent = jnp.where(side == 0, after, before)
        hop = [(2 * z, 2 * z + 1) for z in range(length - 1)] + [(2 * z + 1, 2 * z) for z in range(1, length)]
        across = lax.ppermute(sent, "ctx", hop)
        known = jnp.where(run == 1, beside[:2, :BLK], head_rows)
        known = jnp.where(run == 2, before[:, :BLK], known)
        middle_rows = lax.ppermute(head_rows, "ctx", [(0, length)])
        known = jnp.where(run == length, middle_rows, known)
        late = lax.ppermute(known, "ctx", [(1, 7), (0, 3), (4, 5), (2, 6)])
        first = jnp.where((run == 3) | (run > length), late, known)

        def between(x, places):
            return lax.ppermute(x, "ctx", [(2 * a + n, 2 * b + n) for a, b in places for n in range(2)])

        base = tied(out_weight, before, after, middle_rows)
        near = between(base, ((0, 1), (1, 0), (2, 3), (3, 2)))
        middle = between(base, ((1, 2), (2, 1)))
        far = between(near, ((1, 2), (2, 1)))
        outer = between(middle, ((1, 0), (2, 3)))
        farthest = between(far, ((1, 0), (2, 3)))
        weight_pieces = [base, near, middle, outer, far, farthest]
        bands = [before, after, beside, across]
    else:
        bands = [shifted(both, -o) for o in offsets]
        first = from_first(head_rows)
        grad_full = lax.all_gather(out_grad, "head", axis=1, tiled=True)
        full_weight = lax.all_gather(out_weight, "ctx", axis=0, tiled=True)
        rounds = ctx // head
        mine = jnp.zeros((rounds * tokens, width), jnp.bfloat16)
        for r in range(rounds):
            pairs = []
            for c in range(ctx):
                for h in range(head):
                    pairs.append((c * head + h, (rounds * h + (c + r) % rounds) * head + c // rounds))
            sent = lax.dynamic_slice_in_dim(out_grad, ((run + r) % rounds) * width, width, 1)
            got = lax.ppermute(sent, ("ctx", "head"), pairs)
            mine = lax.dynamic_update_slice_in_dim(mine, got, ((run - r) % rounds) * tokens, 0)
        grad_rows = lax.all_gather(mine, "head", axis=0, tiled=True)

    run_word = run.astype(jnp.int32).reshape(1)
    flat = pl.BlockSpec((tokens, HD), lambda h: (0, h))
    pair = pl.BlockSpec((2, tokens, HD), lambda h: (0, 0, h))
    head_pair = pl.BlockSpec((2, BLK, HD), lambda h: (0, 0, h))
    row = pl.BlockSpec((1, 1, tokens), lambda h: (h, 0, 0))
    keys = places * tokens + BLK
    mixed, lse = pl.pallas_call(
        functools.partial(fwd_kernel, offsets, per_dev, scale),
        grid=(groups,),
        in_specs=[smem, smem, flat, flat, flat] + [pair] * len(offsets) + [head_pair],
        out_specs=[flat, row],
        out_shape=[
            jax.ShapeDtypeStruct((tokens, features), jnp.bfloat16),
            jax.ShapeDtypeStruct((groups, 1, tokens), jnp.float32),
        ],
        scratch_shapes=[pltpu.VMEM((keys, tokens), jnp.float32)],
        compiler_params=pltpu.CompilerParams(vmem_limit_bytes=40 * 1024 * 1024),
        cost_estimate=CHEAP,
        name="attend",
    )(run_word, block_lists, queries, key_heads, value_heads, *bands, first)

    if direct:
        held = [pltpu.VMEM((length, width, features), jnp.bfloat16), pltpu.SemaphoreType.DMA((length,))]
        own_grad, other_grad = pl.pallas_call(
            functools.partial(grads_kernel, length),
            in_specs=[whole] + [anywhere] * 6,
            out_specs=[whole] * 2,
            out_shape=[
                jax.ShapeDtypeStruct((tokens, features), jnp.float32),
                jax.ShapeDtypeStruct((tokens, features), jnp.bfloat16),
            ],
            scratch_shapes=held,
            compiler_params=pltpu.CompilerParams(vmem_limit_bytes=32 * 1024 * 1024),
            cost_estimate=CHEAP,
            name="project_grad",
        )(grad_side, *weight_pieces)
        mixed_grad = (own_grad + swapped(other_grad, range(length)).astype(jnp.float32)).astype(jnp.bfloat16)
        mixed_other = tied(swapped(mixed, range(length)), other_grad)
        own_part, *weight_parts = pl.pallas_call(
            functools.partial(weight_kernel, length),
            in_specs=[whole] + [whole] * 2,
            out_specs=[whole] * length,
            out_shape=[jax.ShapeDtypeStruct((width, features), jnp.float32)]
            + [jax.ShapeDtypeStruct((width, features), jnp.bfloat16)] * (length - 1),
            scratch_shapes=[pltpu.VMEM((2 * tokens, features), jnp.bfloat16)],
            compiler_params=pltpu.CompilerParams(vmem_limit_bytes=32 * 1024 * 1024),
            cost_estimate=CHEAP,
            name="weight_part",
        )(grad_side, mixed, mixed_other)
        mixed_grad = tied(mixed_grad, own_part)
        weight_turns = [turned(weight_parts[n - 1], n, length) for n in range(1, length)]
    else:
        partial_out = mm(mixed, full_weight, NT).astype(jnp.bfloat16)
        mixed_grad = mm(grad_full, full_weight, NN).astype(jnp.bfloat16)
        mixed_all = lax.all_gather(mixed, "ctx", axis=0, tiled=True)
        attended = lax.psum_scatter(partial_out, "head", scatter_dimension=1, tiled=True)
    early_bands = [band for o, band in zip(offsets, bands) if o in early]
    early_rows = len(early) * tokens + BLK
    early_grads = pl.pallas_call(
        functools.partial(first_kernel, early, per_dev, scale),
        grid=(groups,),
        in_specs=[smem, smem, flat] + [pair] * len(early) + [head_pair, flat, flat, row],
        out_specs=pl.BlockSpec((2, early_rows, HD), lambda h: (0, 0, h)),
        out_shape=jax.ShapeDtypeStruct((2, early_rows, features), jnp.bfloat16),
        scratch_shapes=[pltpu.VMEM((1 + len(early), tokens, tokens), jnp.float32)],
        compiler_params=pltpu.CompilerParams(vmem_limit_bytes=32 * 1024 * 1024),
        cost_estimate=pl.CostEstimate(flops=10_000_000_000, bytes_accessed=1, transcendentals=0),
        name="first_grad",
    )(run_word, block_lists, queries, *early_bands, first, mixed, mixed_grad, lse)

    if direct:
        partial_out = pl.pallas_call(
            functools.partial(outs_kernel, length),
            in_specs=[whole] * 2 + [anywhere] * 6,
            out_specs=pl.BlockSpec((2 * tokens, length * width), lambda: (0, 0)),
            out_shape=jax.ShapeDtypeStruct((2 * tokens, length * width), jnp.bfloat16),
            scratch_shapes=held,
            compiler_params=pltpu.CompilerParams(vmem_limit_bytes=32 * 1024 * 1024),
            cost_estimate=CHEAP,
            name="project_out",
        )(mixed, tied(mixed_other, early_grads), *weight_pieces)
        scattered = lax.psum_scatter(partial_out, "head", scatter_dimension=1, tiled=True)
        lse_later = tied(lse, early_grads, partial_out)
    else:
        lse_later = tied(lse, early_grads)
    results = pl.pallas_call(
        functools.partial(bwd_kernel, offsets, early, per_dev, scale),
        grid=(groups,),
        in_specs=[smem, smem, flat, flat, flat] + [pair] * len(offsets) + [head_pair, flat, flat, row],
        out_specs=[flat, pair] + [pair] * (len(offsets) - len(early)),
        out_shape=[
            jax.ShapeDtypeStruct((tokens, features), jnp.bfloat16),
            jax.ShapeDtypeStruct((2, tokens, features), jnp.float32),
        ]
        + [jax.ShapeDtypeStruct((2, tokens, features), jnp.bfloat16)] * (len(offsets) - len(early)),
        scratch_shapes=[pltpu.VMEM((1 + places, tokens, tokens), jnp.float32)],
        compiler_params=pltpu.CompilerParams(vmem_limit_bytes=40 * 1024 * 1024),
        cost_estimate=pl.CostEstimate(flops=30_000_000_000, bytes_accessed=1, transcendentals=0),
        name="attend_grad",
    )(run_word, block_lists, queries, key_heads, value_heads, *bands, first, mixed, mixed_grad, lse_later)
    query_grad, own = results[:2]
    if direct:
        to_before, to_after, to_beside = results[2:]
        swap = tied(swapped(early_grads, range(length)), query_grad)
        diagonal = swap[:, :tokens].astype(jnp.float32)
        first_sum = early_grads[:, tokens:].astype(jnp.float32) + swap[:, tokens:].astype(jnp.float32)
        folded = jnp.pad(jnp.where(run == 2, first_sum, 0.0), ((0, 0), (0, tokens - BLK), (0, 0)))
        to_before, to_after, _ = lax.optimization_barrier((to_before, to_after, weight_turns))
        to_before = to_before.astype(jnp.float32) + jnp.where(side == 1, diagonal, 0.0) + folded
        to_after = to_after.astype(jnp.float32) + jnp.where(side == 0, diagonal, 0.0)
        back_pair = swapped(to_beside, range(length))
        to_before, to_after = to_before.astype(jnp.bfloat16), to_after.astype(jnp.bfloat16)
        to_before, to_after, near = lax.optimization_barrier((to_before, to_after, first_sum.astype(jnp.bfloat16)))
        back_down = shifted(to_before, -2)
        back_up = shifted(to_after, 2)
        scattered = tied(scattered, back_pair)
        mine, theirs = scattered[:tokens], swapped(scattered[tokens:], range(length))
        attended = jnp.where(
            side == 0, jnp.concatenate([mine, theirs], axis=1), jnp.concatenate([theirs, mine], axis=1)
        )
        weight_grad = own_part
        for part in weight_turns:
            weight_grad = weight_grad + part.astype(jnp.float32)
        for c in range(length, ctx, 2):
            got = tied(lax.ppermute(near, "ctx", [(c, 0)]), back_down, back_up, attended)
            first_sum = first_sum + got.astype(jnp.float32)
        wide = pl.BlockSpec((2, BLK, features), lambda n: (0, n, 0))
        top = pl.BlockSpec((2, BLK, features), lambda n: (0, 0, 0))
        slab = pl.BlockSpec((BLK, features), lambda n: (n, 0))
        key_grad, value_grad = pl.pallas_call(
            functools.partial(finish_kernel, scale),
            grid=(per_dev,),
            in_specs=[smem] + [wide] * 4 + [top],
            out_specs=[slab, slab],
            out_shape=[jax.ShapeDtypeStruct((tokens, features), jnp.bfloat16)] * 2,
            cost_estimate=CHEAP,
            name="finish",
        )(run_word, own, back_pair, back_down, back_up, first_sum)

    else:
        first_sum = to_first(early_grads.astype(jnp.float32))
        sums = own
        for o, part in zip(offsets, results[2:]):
            sums = sums + shifted(part, o).astype(jnp.float32)
        first_sum = jnp.where(run == 0, first_sum, 0.0)
        sums = sums + jnp.pad(first_sum, ((0, 0), (0, tokens - BLK), (0, 0)))
        key_grad = (sums[0] * scale).astype(jnp.bfloat16)
        value_grad = sums[1].astype(jnp.bfloat16)
    if not direct:
        weight_grad = mm(grad_rows, mixed_all, TN)
    return (attended, query_grad, key_grad, value_grad, weight_grad)


def solution(mesh):
    spec = P("ctx", "head")
    return jax.shard_map(
        local,
        mesh=mesh,
        in_specs=(spec, spec, spec, spec, P(), spec),
        out_specs=(spec,) * 5,
        check_vma=False,
    )
```

```python
import functools

import jax
import jax.numpy as jnp
from jax import lax
from jax.experimental import pallas as pl
from jax.experimental.pallas import tpu as pltpu
from jax.sharding import PartitionSpec as P

HD = 128
BLK = 128
REACH = 4

CHEAP = pl.CostEstimate(flops=1, bytes_accessed=1, transcendentals=0)

NT = (((1,), (1,)), ((), ()))
TN = (((0,), (0,)), ((), ()))
NN = (((1,), (0,)), ((), ()))


def mm(a, b, dims):
    return lax.dot_general(a, b, dims, preferred_element_type=jnp.float32)


def shifted(x, by):
    peers = lax.axis_size("ctx")
    return lax.ppermute(x, "ctx", [(i, i + by) for i in range(peers) if 0 <= i + by < peers])


def tree_strides(peers):
    strides = []
    stride = 1
    while stride < peers:
        strides.append(stride)
        stride *= 2
    return strides


def from_first(x):
    peers = lax.axis_size("ctx")
    me = lax.axis_index("ctx")
    for stride in reversed(tree_strides(peers)):
        pairs = [(i, i + stride) for i in range(0, peers, 2 * stride) if i + stride < peers]
        got = lax.ppermute(x, "ctx", pairs)
        x = jnp.where(me % (2 * stride) == stride, got, x)
    return x


def to_first(x):
    peers = lax.axis_size("ctx")
    for stride in tree_strides(peers):
        pairs = [(i + stride, i) for i in range(0, peers, 2 * stride) if i + stride < peers]
        x = x + lax.ppermute(x.astype(jnp.bfloat16), "ctx", pairs).astype(x.dtype)
    return x


def turned(x, by, length):
    return lax.ppermute(x, "ctx", [(2 * z + n, 2 * ((z + by) % length) + n) for z in range(length) for n in range(2)])


def swapped(piece, places):
    return lax.ppermute(piece, "ctx", [(2 * z + n, 2 * z + 1 - n) for z in places for n in range(2)])


def tied(x, *others):
    return lax.optimization_barrier((x,) + others)[0]


def start_weights(pieces, held_ref, sems):
    place = lax.div(lax.axis_index("ctx"), 2)
    own, beside, middle, outer, far, farthest = pieces
    low = place < 2
    inner = (place == 1) | (place == 2)

    def send(piece, slot):
        pltpu.make_async_copy(piece, held_ref.at[slot], sems.at[slot]).start()

    send(own, place)
    send(beside, place + 1 - 2 * lax.rem(place, 2))

    @pl.when(inner)
    def _():
        send(middle, 3 - place)
        send(far, jnp.where(low, 3, 0))

    @pl.when(jnp.logical_not(inner))
    def _():
        send(outer, jnp.where(low, 2, 1))
        send(farthest, 3 - place)


def weight_at(held_ref, sems, b):
    pltpu.make_async_copy(held_ref.at[b], held_ref.at[b], sems.at[b]).wait()
    return held_ref[b]


def grads_kernel(length, rows_ref, *rest):
    pieces = rest[:6]
    grad_ref, other_ref, held_ref, sems = rest[6:]
    tokens = grad_ref.shape[0]
    width = rows_ref.shape[1] // length
    start_weights(pieces, held_ref, sems)
    total = None
    for b in range(length):
        part = mm(rows_ref[:, b * width : (b + 1) * width], weight_at(held_ref, sems, b), NN)
        total = part if total is None else total + part
    grad_ref[...] = total[:tokens]
    other_ref[...] = total[tokens:].astype(jnp.bfloat16)


def outs_kernel(length, mixed_ref, other_ref, *rest):
    pieces = rest[:6]
    out_ref, held_ref, sems = rest[6:]
    tokens = mixed_ref.shape[0]
    width = out_ref.shape[1] // length
    start_weights(pieces, held_ref, sems)
    for b in range(length):
        weight = weight_at(held_ref, sems, b)
        columns = slice(b * width, (b + 1) * width)
        out_ref[:tokens, columns] = mm(mixed_ref[...], weight, NT).astype(jnp.bfloat16)
        out_ref[tokens:, columns] = mm(other_ref[...], weight, NT).astype(jnp.bfloat16)


def weight_kernel(length, rows_ref, mixed_ref, other_ref, own_ref, *rest):
    sends = rest[: length - 1]
    (both_ref,) = rest[length - 1 :]
    width = own_ref.shape[0]
    tokens = mixed_ref.shape[0]
    place = lax.div(lax.axis_index("ctx"), 2)
    both_ref[:tokens, :] = mixed_ref[...]
    both_ref[tokens:, :] = other_ref[...]
    for n, out_ref in enumerate((own_ref,) + sends):
        column = pl.multiple_of(lax.rem(place + n, length) * width, 128)
        out_ref[...] = mm(rows_ref[:, pl.ds(column, width)], both_ref[...], TN).astype(out_ref.dtype)


def finish_kernel(scale, run_ref, own_ref, a_ref, b_ref, c_ref, first_ref, key_ref, value_ref):
    there = jnp.where((run_ref[0] == 0) & (pl.program_id(0) == 0), 1.0, 0.0).astype(jnp.float32)
    for n, out_ref in enumerate((key_ref, value_ref)):
        total = own_ref[n] + a_ref[n].astype(jnp.float32) + b_ref[n].astype(jnp.float32) + c_ref[n].astype(jnp.float32)
        total = total + there * first_ref[n]
        out_ref[...] = (total * (scale if n == 0 else 1.0)).astype(jnp.bfloat16)


def runs_away(offset, run):
    side = lax.rem(run, 2)
    if offset == "pair":
        return 1 - 2 * side
    if offset == "across":
        return 2 * side - 1
    return offset


def block_bias(lists_ref, run, per_dev, total_blocks, offset, i, j):
    row = run * per_dev + i
    key = (run + runs_away(offset, run)) * per_dev + j
    hit = (key - row <= 1) & (row - key <= 1)
    for n in range(lists_ref.shape[1]):
        hit = hit | (lists_ref[row, n] == key)
    hit = hit & (key >= 1) & (key < total_blocks)
    return jnp.where(hit, 0.0, -jnp.inf).astype(jnp.float32)


def fwd_kernel(offsets, per_dev, scale, run_ref, lists_ref, q_ref, k_ref, v_ref, *rest):
    bands = rest[: len(offsets)]
    first_ref, mixed_ref, lse_ref, s_ref = rest[len(offsets) :]
    total_blocks = lists_ref.shape[0]
    run = run_ref[0]
    q = q_ref[...]
    tokens = q.shape[0]

    def key_of(p):
        return k_ref[...] if p == 0 else bands[p - 1][0]

    def value_of(p):
        return v_ref[...] if p == 0 else bands[p - 1][1]

    places = (0,) + offsets
    top = None
    for p, offset in enumerate(places):
        s = mm(key_of(p), q, NT) * scale
        for j in range(per_dev):
            for i in range(per_dev):
                part = s[j * BLK : (j + 1) * BLK, i * BLK : (i + 1) * BLK]
                part = part + block_bias(lists_ref, run, per_dev, total_blocks, offset, i, j)
                s_ref[p * tokens + j * BLK : p * tokens + (j + 1) * BLK, i * BLK : (i + 1) * BLK] = part
    s_ref[len(places) * tokens :, :] = mm(first_ref[0], q, NT) * scale
    s = s_ref[...]
    top = jnp.max(s, axis=0, keepdims=True)
    e = jnp.exp(s - top)
    total = jnp.sum(e, axis=0, keepdims=True)
    inverse = 1.0 / total
    low = (e * inverse).astype(jnp.bfloat16)
    out = mm(first_ref[1], low[len(places) * tokens :], TN)
    for p in range(len(places)):
        out = out + mm(value_of(p), low[p * tokens : (p + 1) * tokens], TN)
    mixed_ref[...] = out.T.astype(jnp.bfloat16)
    lse_ref[0] = top + jnp.log(total)


def probs_of(lists_ref, s_ref, run, per_dev, s, offset, lse):
    if offset is None:
        return jnp.exp(s - lse)
    for j in range(per_dev):
        for i in range(per_dev):
            part = s[j * BLK : (j + 1) * BLK, i * BLK : (i + 1) * BLK]
            part = part + block_bias(lists_ref, run, per_dev, lists_ref.shape[0], offset, i, j)
            s_ref[j * BLK : (j + 1) * BLK, i * BLK : (i + 1) * BLK] = part
    return jnp.exp(s_ref[...] - lse)


def first_kernel(offsets, per_dev, scale, run_ref, lists_ref, q_ref, *rest):
    bands = rest[: len(offsets)]
    first_ref, mixed_ref, grad_ref, lse_ref, out_ref, s_ref = rest[len(offsets) :]
    q = q_ref[...]
    grad = grad_ref[...]
    lse = lse_ref[0]
    product = grad.astype(jnp.float32) * mixed_ref[...].astype(jnp.float32)
    delta = jnp.sum(product.T, axis=0, keepdims=True)
    at = 0
    for n, (offset, pair_ref) in enumerate(zip(tuple(offsets) + (None,), bands + (first_ref,))):
        p = probs_of(lists_ref, s_ref.at[n], run_ref[0], per_dev, mm(pair_ref[0], q, NT) * scale, offset, lse)
        slopes = (p * (mm(pair_ref[1], grad, NT) - delta)).astype(jnp.bfloat16)
        rows = slice(at, at + pair_ref.shape[1])
        at = rows.stop
        out_ref[0, rows, :] = mm(slopes, q, NN).astype(jnp.bfloat16)
        out_ref[1, rows, :] = mm(p.astype(jnp.bfloat16), grad, NN).astype(jnp.bfloat16)


def bwd_kernel(offsets, early, per_dev, scale, run_ref, lists_ref, q_ref, k_ref, v_ref, *rest):
    bands = rest[: len(offsets)]
    first_ref, mixed_ref, grad_ref, lse_ref = rest[len(offsets) : len(offsets) + 4]
    outs = rest[len(offsets) + 4 :]
    dq_ref, own_ref = outs[:2]
    band_outs = list(outs[2:-1])
    s_ref = outs[-1]
    q = q_ref[...]
    grad = grad_ref[...]
    lse = lse_ref[0]
    product = grad.astype(jnp.float32) * mixed_ref[...].astype(jnp.float32)
    delta = jnp.sum(product.T, axis=0, keepdims=True)
    dq = None
    plan = [(None, first_ref[0], first_ref[1], None)]
    for offset, pair_ref in zip(offsets, bands):
        plan.append((offset, pair_ref[0], pair_ref[1], None if offset in early else band_outs.pop(0)))
    plan.append((0, k_ref[...], v_ref[...], own_ref))
    for n, (offset, key, value, out_ref) in enumerate(plan):
        p = probs_of(lists_ref, s_ref.at[n], run_ref[0], per_dev, mm(key, q, NT) * scale, offset, lse)
        slopes = (p * (mm(value, grad, NT) - delta)).astype(jnp.bfloat16)
        more = mm(key, slopes, TN)
        dq = more if dq is None else dq + more
        if out_ref is not None:
            out_ref[0] = mm(slopes, q, NN).astype(out_ref.dtype)
            out_ref[1] = mm(p.astype(jnp.bfloat16), grad, NN).astype(out_ref.dtype)
    dq_ref[...] = (dq * scale).T.astype(jnp.bfloat16)


def local(queries, key_heads, value_heads, out_weight, block_lists, out_grad):
    scale = HD ** (-0.5)
    tokens, features = queries.shape
    groups = features // HD
    per_dev = tokens // BLK
    ctx = lax.axis_size("ctx")
    head = lax.axis_size("head")
    run = lax.axis_index("ctx")
    column = lax.axis_index("head")
    reach = -(-REACH // per_dev)
    length = ctx // 2
    direct = ctx == 8 and head == length and reach == 2 and out_grad.shape[1] == 2 * features
    place = run // 2
    side = run % 2
    if direct:
        offsets, early = (-2, 2, "pair", "across"), ("across",)
    else:
        offsets, early = tuple(o for o in range(-reach, reach + 1) if o != 0), ()
    places = 1 + len(offsets)
    smem = pl.BlockSpec(memory_space=pltpu.SMEM)
    whole = pl.BlockSpec(memory_space=pltpu.VMEM)
    anywhere = pl.BlockSpec(memory_space=pl.ANY)
    width = out_weight.shape[0]

    both = jnp.stack([key_heads, value_heads])
    head_rows = both[:, :BLK]
    if direct:
        half = out_grad.shape[1] // 2
        own_half = lax.dynamic_slice_in_dim(out_grad, side * half, half, 1)
        other_half = lax.dynamic_slice_in_dim(out_grad, (1 - side) * half, half, 1)
        before, after = shifted(both, 2), shifted(both, -2)
        beside = swapped(jnp.concatenate([both, other_half[None]], axis=0), range(length))
        grad_side = lax.all_gather(jnp.concatenate([own_half, tied(beside[2], before, after)], axis=0), "head", axis=1, tiled=True)
        sent = jnp.where(side == 0, after, before)
        hop = [(2 * z, 2 * z + 1) for z in range(length - 1)] + [(2 * z + 1, 2 * z) for z in range(1, length)]
        across = lax.ppermute(sent, "ctx", hop)
        known = jnp.where(run == 1, beside[:2, :BLK], head_rows)
        known = jnp.where(run == 2, before[:, :BLK], known)
        middle_rows = lax.ppermute(head_rows, "ctx", [(0, length)])
        known = jnp.where(run == length, middle_rows, known)
        late = lax.ppermute(known, "ctx", [(1, 7), (0, 3), (4, 5), (2, 6)])
        first = jnp.where((run == 3) | (run > length), late, known)

        def between(x, places):
            return lax.ppermute(x, "ctx", [(2 * a + n, 2 * b + n) for a, b in places for n in range(2)])

        base = tied(out_weight, before, after, middle_rows)
        near = between(base, ((0, 1), (1, 0), (2, 3), (3, 2)))
        middle = between(base, ((1, 2), (2, 1)))
        far = between(near, ((1, 2), (2, 1)))
        outer = between(middle, ((1, 0), (2, 3)))
        farthest = between(far, ((1, 0), (2, 3)))
        weight_pieces = [base, near, middle, outer, far, farthest]
        bands = [before, after, beside, across]
    else:
        bands = [shifted(both, -o) for o in offsets]
        first = from_first(head_rows)
        grad_full = lax.all_gather(out_grad, "head", axis=1, tiled=True)
        full_weight = lax.all_gather(out_weight, "ctx", axis=0, tiled=True)
        rounds = ctx // head
        mine = jnp.zeros((rounds * tokens, width), jnp.bfloat16)
        for r in range(rounds):
            pairs = []
            for c in range(ctx):
                for h in range(head):
                    pairs.append((c * head + h, (rounds * h + (c + r) % rounds) * head + c // rounds))
            sent = lax.dynamic_slice_in_dim(out_grad, ((run + r) % rounds) * width, width, 1)
            got = lax.ppermute(sent, ("ctx", "head"), pairs)
            mine = lax.dynamic_update_slice_in_dim(mine, got, ((run - r) % rounds) * tokens, 0)
        grad_rows = lax.all_gather(mine, "head", axis=0, tiled=True)

    run_word = run.astype(jnp.int32).reshape(1)
    flat = pl.BlockSpec((tokens, HD), lambda h: (0, h))
    pair = pl.BlockSpec((2, tokens, HD), lambda h: (0, 0, h))
    head_pair = pl.BlockSpec((2, BLK, HD), lambda h: (0, 0, h))
    row = pl.BlockSpec((1, 1, tokens), lambda h: (h, 0, 0))
    keys = places * tokens + BLK
    mixed, lse = pl.pallas_call(
        functools.partial(fwd_kernel, offsets, per_dev, scale),
        grid=(groups,),
        in_specs=[smem, smem, flat, flat, flat] + [pair] * len(offsets) + [head_pair],
        out_specs=[flat, row],
        out_shape=[
            jax.ShapeDtypeStruct((tokens, features), jnp.bfloat16),
            jax.ShapeDtypeStruct((groups, 1, tokens), jnp.float32),
        ],
        scratch_shapes=[pltpu.VMEM((keys, tokens), jnp.float32)],
        compiler_params=pltpu.CompilerParams(vmem_limit_bytes=40 * 1024 * 1024),
        cost_estimate=CHEAP,
        name="attend",
    )(run_word, block_lists, queries, key_heads, value_heads, *bands, first)

    if direct:
        held = [pltpu.VMEM((length, width, features), jnp.bfloat16), pltpu.SemaphoreType.DMA((length,))]
        own_grad, other_grad = pl.pallas_call(
            functools.partial(grads_kernel, length),
            in_specs=[whole] + [anywhere] * 6,
            out_specs=[whole] * 2,
            out_shape=[
                jax.ShapeDtypeStruct((tokens, features), jnp.float32),
                jax.ShapeDtypeStruct((tokens, features), jnp.bfloat16),
            ],
            scratch_shapes=held,
            compiler_params=pltpu.CompilerParams(vmem_limit_bytes=32 * 1024 * 1024),
            cost_estimate=CHEAP,
            name="project_grad",
        )(grad_side, *weight_pieces)
        mixed_grad = (own_grad + swapped(other_grad, range(length)).astype(jnp.float32)).astype(jnp.bfloat16)
        mixed_other = tied(swapped(mixed, range(length)), other_grad)
        own_part, *weight_parts = pl.pallas_call(
            functools.partial(weight_kernel, length),
            in_specs=[whole] + [whole] * 2,
            out_specs=[whole] * length,
            out_shape=[jax.ShapeDtypeStruct((width, features), jnp.float32)]
            + [jax.ShapeDtypeStruct((width, features), jnp.bfloat16)] * (length - 1),
            scratch_shapes=[pltpu.VMEM((2 * tokens, features), jnp.bfloat16)],
            compiler_params=pltpu.CompilerParams(vmem_limit_bytes=32 * 1024 * 1024),
            cost_estimate=CHEAP,
            name="weight_part",
        )(grad_side, mixed, mixed_other)
        partial_out = pl.pallas_call(
            functools.partial(outs_kernel, length),
            in_specs=[whole] * 2 + [anywhere] * 6,
            out_specs=pl.BlockSpec((2 * tokens, length * width), lambda: (0, 0)),
            out_shape=jax.ShapeDtypeStruct((2 * tokens, length * width), jnp.bfloat16),
            scratch_shapes=held,
            compiler_params=pltpu.CompilerParams(vmem_limit_bytes=32 * 1024 * 1024),
            cost_estimate=CHEAP,
            name="project_out",
        )(mixed, tied(mixed_other, own_part), *weight_pieces)
        scattered = lax.psum_scatter(partial_out, "head", scatter_dimension=1, tiled=True)
        mixed_grad = tied(mixed_grad, own_part)
        weight_turns = [turned(weight_parts[n - 1], n, length) for n in (1, 3)]
    else:
        partial_out = mm(mixed, full_weight, NT).astype(jnp.bfloat16)
        mixed_grad = mm(grad_full, full_weight, NN).astype(jnp.bfloat16)
        mixed_all = lax.all_gather(mixed, "ctx", axis=0, tiled=True)
        attended = lax.psum_scatter(partial_out, "head", scatter_dimension=1, tiled=True)
    early_bands = [band for o, band in zip(offsets, bands) if o in early]
    early_rows = len(early) * tokens + BLK
    early_grads = pl.pallas_call(
        functools.partial(first_kernel, early, per_dev, scale),
        grid=(groups,),
        in_specs=[smem, smem, flat] + [pair] * len(early) + [head_pair, flat, flat, row],
        out_specs=pl.BlockSpec((2, early_rows, HD), lambda h: (0, 0, h)),
        out_shape=jax.ShapeDtypeStruct((2, early_rows, features), jnp.bfloat16),
        scratch_shapes=[pltpu.VMEM((1 + len(early), tokens, tokens), jnp.float32)],
        compiler_params=pltpu.CompilerParams(vmem_limit_bytes=32 * 1024 * 1024),
        cost_estimate=pl.CostEstimate(flops=10_000_000_000, bytes_accessed=1, transcendentals=0),
        name="first_grad",
    )(run_word, block_lists, queries, *early_bands, first, mixed, mixed_grad, lse)

    lse_later = tied(lse, early_grads, partial_out)
    results = pl.pallas_call(
        functools.partial(bwd_kernel, offsets, early, per_dev, scale),
        grid=(groups,),
        in_specs=[smem, smem, flat, flat, flat] + [pair] * len(offsets) + [head_pair, flat, flat, row],
        out_specs=[flat, pair] + [pair] * (len(offsets) - len(early)),
        out_shape=[
            jax.ShapeDtypeStruct((tokens, features), jnp.bfloat16),
            jax.ShapeDtypeStruct((2, tokens, features), jnp.float32),
        ]
        + [jax.ShapeDtypeStruct((2, tokens, features), jnp.bfloat16)] * (len(offsets) - len(early)),
        scratch_shapes=[pltpu.VMEM((1 + places, tokens, tokens), jnp.float32)],
        compiler_params=pltpu.CompilerParams(vmem_limit_bytes=40 * 1024 * 1024),
        cost_estimate=pl.CostEstimate(flops=30_000_000_000, bytes_accessed=1, transcendentals=0),
        name="attend_grad",
    )(run_word, block_lists, queries, key_heads, value_heads, *bands, first, mixed, mixed_grad, lse_later)
    query_grad, own = results[:2]
    if direct:
        to_before, to_after, to_beside = results[2:]
        swap = tied(swapped(early_grads, range(length)), query_grad)
        diagonal = swap[:, :tokens].astype(jnp.float32)
        first_sum = early_grads[:, tokens:].astype(jnp.float32) + swap[:, tokens:].astype(jnp.float32)
        folded = jnp.pad(jnp.where(run == 2, first_sum, 0.0), ((0, 0), (0, tokens - BLK), (0, 0)))
        to_before, to_after, _ = lax.optimization_barrier((to_before, to_after, weight_turns))
        to_before = to_before.astype(jnp.float32) + jnp.where(side == 1, diagonal, 0.0) + folded
        to_after = to_after.astype(jnp.float32) + jnp.where(side == 0, diagonal, 0.0)
        to_before, to_after = to_before.astype(jnp.bfloat16), to_after.astype(jnp.bfloat16)
        to_before, to_after, to_beside, near, last_part = lax.optimization_barrier(
            (to_before, to_after, to_beside, first_sum.astype(jnp.bfloat16), weight_parts[1])
        )
        back_pair = swapped(to_beside, range(length))
        back_down = shifted(to_before, -2)
        back_up = shifted(to_after, 2)
        scattered = tied(scattered, back_pair)
        mine, theirs = scattered[:tokens], swapped(scattered[tokens:], range(length))
        attended = jnp.where(
            side == 0, jnp.concatenate([mine, theirs], axis=1), jnp.concatenate([theirs, mine], axis=1)
        )
        weight_grad = own_part
        for part in weight_turns + [turned(last_part, 2, length)]:
            weight_grad = weight_grad + part.astype(jnp.float32)
        for c in range(length, ctx, 2):
            got = tied(lax.ppermute(near, "ctx", [(c, 0)]), back_down, back_up, attended)
            first_sum = first_sum + got.astype(jnp.float32)
        wide = pl.BlockSpec((2, BLK, features), lambda n: (0, n, 0))
        top = pl.BlockSpec((2, BLK, features), lambda n: (0, 0, 0))
        slab = pl.BlockSpec((BLK, features), lambda n: (n, 0))
        key_grad, value_grad = pl.pallas_call(
            functools.partial(finish_kernel, scale),
            grid=(per_dev,),
            in_specs=[smem] + [wide] * 4 + [top],
            out_specs=[slab, slab],
            out_shape=[jax.ShapeDtypeStruct((tokens, features), jnp.bfloat16)] * 2,
            cost_estimate=CHEAP,
            name="finish",
        )(run_word, own, back_pair, back_down, back_up, first_sum)

    else:
        first_sum = to_first(early_grads.astype(jnp.float32))
        sums = own
        for o, part in zip(offsets, results[2:]):
            sums = sums + shifted(part, o).astype(jnp.float32)
        first_sum = jnp.where(run == 0, first_sum, 0.0)
        sums = sums + jnp.pad(first_sum, ((0, 0), (0, tokens - BLK), (0, 0)))
        key_grad = (sums[0] * scale).astype(jnp.bfloat16)
        value_grad = sums[1].astype(jnp.bfloat16)
    if not direct:
        weight_grad = mm(grad_rows, mixed_all, TN)
    return (attended, query_grad, key_grad, value_grad, weight_grad)


def solution(mesh):
    spec = P("ctx", "head")
    return jax.shard_map(
        local,
        mesh=mesh,
        in_specs=(spec, spec, spec, spec, P(), spec),
        out_specs=(spec,) * 5,
        check_vma=False,
    )
```

```python
import functools

import jax
import jax.numpy as jnp
from jax import lax
from jax.experimental import pallas as pl
from jax.experimental.pallas import tpu as pltpu
from jax.sharding import PartitionSpec as P

HD = 128
BLK = 128
REACH = 4

CHEAP = pl.CostEstimate(flops=1, bytes_accessed=1, transcendentals=0)

NT = (((1,), (1,)), ((), ()))
TN = (((0,), (0,)), ((), ()))
NN = (((1,), (0,)), ((), ()))


def mm(a, b, dims):
    return lax.dot_general(a, b, dims, preferred_element_type=jnp.float32)


def shifted(x, by):
    peers = lax.axis_size("ctx")
    return lax.ppermute(x, "ctx", [(i, i + by) for i in range(peers) if 0 <= i + by < peers])


def tree_strides(peers):
    strides = []
    stride = 1
    while stride < peers:
        strides.append(stride)
        stride *= 2
    return strides


def from_first(x):
    peers = lax.axis_size("ctx")
    me = lax.axis_index("ctx")
    for stride in reversed(tree_strides(peers)):
        pairs = [(i, i + stride) for i in range(0, peers, 2 * stride) if i + stride < peers]
        got = lax.ppermute(x, "ctx", pairs)
        x = jnp.where(me % (2 * stride) == stride, got, x)
    return x


def to_first(x):
    peers = lax.axis_size("ctx")
    for stride in tree_strides(peers):
        pairs = [(i + stride, i) for i in range(0, peers, 2 * stride) if i + stride < peers]
        x = x + lax.ppermute(x.astype(jnp.bfloat16), "ctx", pairs).astype(x.dtype)
    return x


def turned(x, by, length):
    return lax.ppermute(x, "ctx", [(2 * z + n, 2 * ((z + by) % length) + n) for z in range(length) for n in range(2)])


def swapped(piece, places):
    return lax.ppermute(piece, "ctx", [(2 * z + n, 2 * z + 1 - n) for z in places for n in range(2)])


def tied(x, *others):
    return lax.optimization_barrier((x,) + others)[0]


def start_weights(pieces, held_ref, sems):
    place = lax.div(lax.axis_index("ctx"), 2)
    own, beside, middle, outer, far, farthest = pieces
    low = place < 2
    inner = (place == 1) | (place == 2)

    def send(piece, slot):
        pltpu.make_async_copy(piece, held_ref.at[slot], sems.at[slot]).start()

    send(own, place)
    send(beside, place + 1 - 2 * lax.rem(place, 2))

    @pl.when(inner)
    def _():
        send(middle, 3 - place)
        send(far, jnp.where(low, 3, 0))

    @pl.when(jnp.logical_not(inner))
    def _():
        send(outer, jnp.where(low, 2, 1))
        send(farthest, 3 - place)


def weight_at(held_ref, sems, b):
    pltpu.make_async_copy(held_ref.at[b], held_ref.at[b], sems.at[b]).wait()
    return held_ref[b]


def grads_kernel(length, rows_ref, *rest):
    pieces = rest[:6]
    grad_ref, other_ref, held_ref, sems = rest[6:]
    tokens = grad_ref.shape[0]
    width = rows_ref.shape[1] // length
    start_weights(pieces, held_ref, sems)
    total = None
    for b in range(length):
        part = mm(rows_ref[:, b * width : (b + 1) * width], weight_at(held_ref, sems, b), NN)
        total = part if total is None else total + part
    grad_ref[...] = total[:tokens]
    other_ref[...] = total[tokens:].astype(jnp.bfloat16)


def outs_kernel(length, mixed_ref, other_ref, *rest):
    pieces = rest[:6]
    out_ref, held_ref, sems = rest[6:]
    tokens = mixed_ref.shape[0]
    width = out_ref.shape[1] // length
    start_weights(pieces, held_ref, sems)
    for b in range(length):
        weight = weight_at(held_ref, sems, b)
        columns = slice(b * width, (b + 1) * width)
        out_ref[:tokens, columns] = mm(mixed_ref[...], weight, NT).astype(jnp.bfloat16)
        out_ref[tokens:, columns] = mm(other_ref[...], weight, NT).astype(jnp.bfloat16)


def weight_kernel(length, rows_ref, mixed_ref, other_ref, own_ref, *rest):
    sends = rest[: length - 1]
    (both_ref,) = rest[length - 1 :]
    width = own_ref.shape[0]
    tokens = mixed_ref.shape[0]
    place = lax.div(lax.axis_index("ctx"), 2)
    both_ref[:tokens, :] = mixed_ref[...]
    both_ref[tokens:, :] = other_ref[...]
    for n, out_ref in enumerate((own_ref,) + sends):
        column = pl.multiple_of(lax.rem(place + n, length) * width, 128)
        out_ref[...] = mm(rows_ref[:, pl.ds(column, width)], both_ref[...], TN).astype(out_ref.dtype)


def finish_kernel(scale, run_ref, own_ref, a_ref, b_ref, c_ref, first_ref, key_ref, value_ref):
    there = jnp.where((run_ref[0] == 0) & (pl.program_id(0) == 0), 1.0, 0.0).astype(jnp.float32)
    for n, out_ref in enumerate((key_ref, value_ref)):
        total = own_ref[n] + a_ref[n].astype(jnp.float32) + b_ref[n].astype(jnp.float32) + c_ref[n].astype(jnp.float32)
        total = total + there * first_ref[n]
        out_ref[...] = (total * (scale if n == 0 else 1.0)).astype(jnp.bfloat16)


def runs_away(offset, run):
    side = lax.rem(run, 2)
    if offset == "pair":
        return 1 - 2 * side
    if offset == "across":
        return 2 * side - 1
    return offset


def block_bias(lists_ref, run, per_dev, total_blocks, offset, i, j):
    row = run * per_dev + i
    key = (run + runs_away(offset, run)) * per_dev + j
    hit = (key - row <= 1) & (row - key <= 1)
    for n in range(lists_ref.shape[1]):
        hit = hit | (lists_ref[row, n] == key)
    hit = hit & (key >= 1) & (key < total_blocks)
    return jnp.where(hit, 0.0, -jnp.inf).astype(jnp.float32)


def fwd_kernel(offsets, per_dev, scale, run_ref, lists_ref, q_ref, k_ref, v_ref, *rest):
    bands = rest[: len(offsets)]
    first_ref, mixed_ref, lse_ref, s_ref = rest[len(offsets) :]
    total_blocks = lists_ref.shape[0]
    run = run_ref[0]
    q = q_ref[...]
    tokens = q.shape[0]

    def key_of(p):
        return k_ref[...] if p == 0 else bands[p - 1][0]

    def value_of(p):
        return v_ref[...] if p == 0 else bands[p - 1][1]

    places = (0,) + offsets
    top = None
    for p, offset in enumerate(places):
        s = mm(key_of(p), q, NT) * scale
        for j in range(per_dev):
            for i in range(per_dev):
                part = s[j * BLK : (j + 1) * BLK, i * BLK : (i + 1) * BLK]
                part = part + block_bias(lists_ref, run, per_dev, total_blocks, offset, i, j)
                s_ref[p * tokens + j * BLK : p * tokens + (j + 1) * BLK, i * BLK : (i + 1) * BLK] = part
    s_ref[len(places) * tokens :, :] = mm(first_ref[0], q, NT) * scale
    s = s_ref[...]
    top = jnp.max(s, axis=0, keepdims=True)
    e = jnp.exp(s - top)
    total = jnp.sum(e, axis=0, keepdims=True)
    inverse = 1.0 / total
    low = (e * inverse).astype(jnp.bfloat16)
    out = mm(first_ref[1], low[len(places) * tokens :], TN)
    for p in range(len(places)):
        out = out + mm(value_of(p), low[p * tokens : (p + 1) * tokens], TN)
    mixed_ref[...] = out.T.astype(jnp.bfloat16)
    lse_ref[0] = top + jnp.log(total)


def probs_of(lists_ref, s_ref, run, per_dev, s, offset, lse):
    if offset is None:
        return jnp.exp(s - lse)
    for j in range(per_dev):
        for i in range(per_dev):
            part = s[j * BLK : (j + 1) * BLK, i * BLK : (i + 1) * BLK]
            part = part + block_bias(lists_ref, run, per_dev, lists_ref.shape[0], offset, i, j)
            s_ref[j * BLK : (j + 1) * BLK, i * BLK : (i + 1) * BLK] = part
    return jnp.exp(s_ref[...] - lse)


def first_kernel(offsets, per_dev, scale, run_ref, lists_ref, q_ref, *rest):
    bands = rest[: len(offsets)]
    first_ref, mixed_ref, grad_ref, lse_ref, out_ref, s_ref = rest[len(offsets) :]
    q = q_ref[...]
    grad = grad_ref[...]
    lse = lse_ref[0]
    product = grad.astype(jnp.float32) * mixed_ref[...].astype(jnp.float32)
    delta = jnp.sum(product.T, axis=0, keepdims=True)
    at = 0
    for n, (offset, pair_ref) in enumerate(zip(tuple(offsets) + (None,), bands + (first_ref,))):
        p = probs_of(lists_ref, s_ref.at[n], run_ref[0], per_dev, mm(pair_ref[0], q, NT) * scale, offset, lse)
        slopes = (p * (mm(pair_ref[1], grad, NT) - delta)).astype(jnp.bfloat16)
        rows = slice(at, at + pair_ref.shape[1])
        at = rows.stop
        out_ref[0, rows, :] = mm(slopes, q, NN).astype(jnp.bfloat16)
        out_ref[1, rows, :] = mm(p.astype(jnp.bfloat16), grad, NN).astype(jnp.bfloat16)


def bwd_kernel(offsets, early, per_dev, scale, run_ref, lists_ref, q_ref, k_ref, v_ref, *rest):
    bands = rest[: len(offsets)]
    first_ref, mixed_ref, grad_ref, lse_ref = rest[len(offsets) : len(offsets) + 4]
    outs = rest[len(offsets) + 4 :]
    dq_ref, own_ref = outs[:2]
    band_outs = list(outs[2:-1])
    s_ref = outs[-1]
    q = q_ref[...]
    grad = grad_ref[...]
    lse = lse_ref[0]
    product = grad.astype(jnp.float32) * mixed_ref[...].astype(jnp.float32)
    delta = jnp.sum(product.T, axis=0, keepdims=True)
    dq = None
    plan = [(None, first_ref[0], first_ref[1], None)]
    for offset, pair_ref in zip(offsets, bands):
        plan.append((offset, pair_ref[0], pair_ref[1], None if offset in early else band_outs.pop(0)))
    plan.append((0, k_ref[...], v_ref[...], own_ref))
    for n, (offset, key, value, out_ref) in enumerate(plan):
        p = probs_of(lists_ref, s_ref.at[n], run_ref[0], per_dev, mm(key, q, NT) * scale, offset, lse)
        slopes = (p * (mm(value, grad, NT) - delta)).astype(jnp.bfloat16)
        more = mm(key, slopes, TN)
        dq = more if dq is None else dq + more
        if out_ref is not None:
            out_ref[0] = mm(slopes, q, NN).astype(out_ref.dtype)
            out_ref[1] = mm(p.astype(jnp.bfloat16), grad, NN).astype(out_ref.dtype)
    dq_ref[...] = (dq * scale).T.astype(jnp.bfloat16)


def local(queries, key_heads, value_heads, out_weight, block_lists, out_grad):
    scale = HD ** (-0.5)
    tokens, features = queries.shape
    groups = features // HD
    per_dev = tokens // BLK
    ctx = lax.axis_size("ctx")
    head = lax.axis_size("head")
    run = lax.axis_index("ctx")
    column = lax.axis_index("head")
    reach = -(-REACH // per_dev)
    length = ctx // 2
    direct = ctx == 8 and head == length and reach == 2 and out_grad.shape[1] == 2 * features
    place = run // 2
    side = run % 2
    if direct:
        offsets, early = (-2, 2, "pair", "across"), ("across",)
    else:
        offsets, early = tuple(o for o in range(-reach, reach + 1) if o != 0), ()
    places = 1 + len(offsets)
    smem = pl.BlockSpec(memory_space=pltpu.SMEM)
    whole = pl.BlockSpec(memory_space=pltpu.VMEM)
    anywhere = pl.BlockSpec(memory_space=pl.ANY)
    width = out_weight.shape[0]

    both = jnp.stack([key_heads, value_heads])
    head_rows = both[:, :BLK]
    if direct:
        half = out_grad.shape[1] // 2
        own_half = lax.dynamic_slice_in_dim(out_grad, side * half, half, 1)
        other_half = lax.dynamic_slice_in_dim(out_grad, (1 - side) * half, half, 1)
        before, after = shifted(both, 2), shifted(both, -2)
        beside = swapped(jnp.concatenate([both, other_half[None]], axis=0), range(length))
        grad_side = lax.all_gather(jnp.concatenate([own_half, tied(beside[2], before, after)], axis=0), "head", axis=1, tiled=True)
        sent = jnp.where(side == 0, after, before)
        hop = [(2 * z, 2 * z + 1) for z in range(length - 1)] + [(2 * z + 1, 2 * z) for z in range(1, length)]
        across = lax.ppermute(sent, "ctx", hop)
        known = jnp.where(run == 1, beside[:2, :BLK], head_rows)
        known = jnp.where(run == 2, before[:, :BLK], known)
        middle_rows = lax.ppermute(head_rows, "ctx", [(0, length)])
        known = jnp.where(run == length, middle_rows, known)
        late = lax.ppermute(known, "ctx", [(1, 7), (0, 3), (4, 5), (2, 6)])
        first = jnp.where((run == 3) | (run > length), late, known)

        def between(x, places):
            return lax.ppermute(x, "ctx", [(2 * a + n, 2 * b + n) for a, b in places for n in range(2)])

        base = tied(out_weight, before, after)
        near = between(base, ((0, 1), (1, 0), (2, 3), (3, 2)))
        middle = between(base, ((1, 2), (2, 1)))
        near, middle, _ = lax.optimization_barrier((near, middle, middle_rows))
        far = between(near, ((1, 2), (2, 1)))
        outer = between(middle, ((1, 0), (2, 3)))
        farthest = between(far, ((1, 0), (2, 3)))
        weight_pieces = [base, near, middle, outer, far, farthest]
        bands = [before, after, beside, across]
    else:
        bands = [shifted(both, -o) for o in offsets]
        first = from_first(head_rows)
        grad_full = lax.all_gather(out_grad, "head", axis=1, tiled=True)
        full_weight = lax.all_gather(out_weight, "ctx", axis=0, tiled=True)
        rounds = ctx // head
        mine = jnp.zeros((rounds * tokens, width), jnp.bfloat16)
        for r in range(rounds):
            pairs = []
            for c in range(ctx):
                for h in range(head):
                    pairs.append((c * head + h, (rounds * h + (c + r) % rounds) * head + c // rounds))
            sent = lax.dynamic_slice_in_dim(out_grad, ((run + r) % rounds) * width, width, 1)
            got = lax.ppermute(sent, ("ctx", "head"), pairs)
            mine = lax.dynamic_update_slice_in_dim(mine, got, ((run - r) % rounds) * tokens, 0)
        grad_rows = lax.all_gather(mine, "head", axis=0, tiled=True)

    run_word = run.astype(jnp.int32).reshape(1)
    flat = pl.BlockSpec((tokens, HD), lambda h: (0, h))
    pair = pl.BlockSpec((2, tokens, HD), lambda h: (0, 0, h))
    head_pair = pl.BlockSpec((2, BLK, HD), lambda h: (0, 0, h))
    row = pl.BlockSpec((1, 1, tokens), lambda h: (h, 0, 0))
    keys = places * tokens + BLK
    mixed, lse = pl.pallas_call(
        functools.partial(fwd_kernel, offsets, per_dev, scale),
        grid=(groups,),
        in_specs=[smem, smem, flat, flat, flat] + [pair] * len(offsets) + [head_pair],
        out_specs=[flat, row],
        out_shape=[
            jax.ShapeDtypeStruct((tokens, features), jnp.bfloat16),
            jax.ShapeDtypeStruct((groups, 1, tokens), jnp.float32),
        ],
        scratch_shapes=[pltpu.VMEM((keys, tokens), jnp.float32)],
        compiler_params=pltpu.CompilerParams(vmem_limit_bytes=40 * 1024 * 1024),
        cost_estimate=CHEAP,
        name="attend",
    )(run_word, block_lists, queries, key_heads, value_heads, *bands, first)

    if direct:
        held = [pltpu.VMEM((length, width, features), jnp.bfloat16), pltpu.SemaphoreType.DMA((length,))]
        own_grad, other_grad = pl.pallas_call(
            functools.partial(grads_kernel, length),
            in_specs=[whole] + [anywhere] * 6,
            out_specs=[whole] * 2,
            out_shape=[
                jax.ShapeDtypeStruct((tokens, features), jnp.float32),
                jax.ShapeDtypeStruct((tokens, features), jnp.bfloat16),
            ],
            scratch_shapes=held,
            compiler_params=pltpu.CompilerParams(vmem_limit_bytes=32 * 1024 * 1024),
            cost_estimate=CHEAP,
            name="project_grad",
        )(grad_side, *weight_pieces)
        mixed_grad = (own_grad + swapped(other_grad, range(length)).astype(jnp.float32)).astype(jnp.bfloat16)
        mixed_other = tied(swapped(mixed, range(length)), other_grad)
        own_part, *weight_parts = pl.pallas_call(
            functools.partial(weight_kernel, length),
            in_specs=[whole] + [whole] * 2,
            out_specs=[whole] * length,
            out_shape=[jax.ShapeDtypeStruct((width, features), jnp.float32)]
            + [jax.ShapeDtypeStruct((width, features), jnp.bfloat16)] * (length - 1),
            scratch_shapes=[pltpu.VMEM((2 * tokens, features), jnp.bfloat16)],
            compiler_params=pltpu.CompilerParams(vmem_limit_bytes=32 * 1024 * 1024),
            cost_estimate=CHEAP,
            name="weight_part",
        )(grad_side, mixed, mixed_other)
        partial_out = pl.pallas_call(
            functools.partial(outs_kernel, length),
            in_specs=[whole] * 2 + [anywhere] * 6,
            out_specs=pl.BlockSpec((2 * tokens, length * width), lambda: (0, 0)),
            out_shape=jax.ShapeDtypeStruct((2 * tokens, length * width), jnp.bfloat16),
            scratch_shapes=held,
            compiler_params=pltpu.CompilerParams(vmem_limit_bytes=32 * 1024 * 1024),
            cost_estimate=CHEAP,
            name="project_out",
        )(mixed, tied(mixed_other, own_part), *weight_pieces)
        scattered = lax.psum_scatter(partial_out, "head", scatter_dimension=1, tiled=True)
        mixed_grad = tied(mixed_grad, own_part)
        weight_turns = [turned(weight_parts[n - 1], n, length) for n in (1, 3)]
    else:
        partial_out = mm(mixed, full_weight, NT).astype(jnp.bfloat16)
        mixed_grad = mm(grad_full, full_weight, NN).astype(jnp.bfloat16)
        mixed_all = lax.all_gather(mixed, "ctx", axis=0, tiled=True)
        attended = lax.psum_scatter(partial_out, "head", scatter_dimension=1, tiled=True)
    early_bands = [band for o, band in zip(offsets, bands) if o in early]
    early_rows = len(early) * tokens + BLK
    early_grads = pl.pallas_call(
        functools.partial(first_kernel, early, per_dev, scale),
        grid=(groups,),
        in_specs=[smem, smem, flat] + [pair] * len(early) + [head_pair, flat, flat, row],
        out_specs=pl.BlockSpec((2, early_rows, HD), lambda h: (0, 0, h)),
        out_shape=jax.ShapeDtypeStruct((2, early_rows, features), jnp.bfloat16),
        scratch_shapes=[pltpu.VMEM((1 + len(early), tokens, tokens), jnp.float32)],
        compiler_params=pltpu.CompilerParams(vmem_limit_bytes=32 * 1024 * 1024),
        cost_estimate=pl.CostEstimate(flops=10_000_000_000, bytes_accessed=1, transcendentals=0),
        name="first_grad",
    )(run_word, block_lists, queries, *early_bands, first, mixed, mixed_grad, lse)

    lse_later = tied(lse, early_grads, partial_out)
    results = pl.pallas_call(
        functools.partial(bwd_kernel, offsets, early, per_dev, scale),
        grid=(groups,),
        in_specs=[smem, smem, flat, flat, flat] + [pair] * len(offsets) + [head_pair, flat, flat, row],
        out_specs=[flat, pair] + [pair] * (len(offsets) - len(early)),
        out_shape=[
            jax.ShapeDtypeStruct((tokens, features), jnp.bfloat16),
            jax.ShapeDtypeStruct((2, tokens, features), jnp.float32),
        ]
        + [jax.ShapeDtypeStruct((2, tokens, features), jnp.bfloat16)] * (len(offsets) - len(early)),
        scratch_shapes=[pltpu.VMEM((1 + places, tokens, tokens), jnp.float32)],
        compiler_params=pltpu.CompilerParams(vmem_limit_bytes=40 * 1024 * 1024),
        cost_estimate=pl.CostEstimate(flops=30_000_000_000, bytes_accessed=1, transcendentals=0),
        name="attend_grad",
    )(run_word, block_lists, queries, key_heads, value_heads, *bands, first, mixed, mixed_grad, lse_later)
    query_grad, own = results[:2]
    if direct:
        to_before, to_after, to_beside = results[2:]
        swap = tied(swapped(early_grads, range(length)), query_grad)
        diagonal = swap[:, :tokens].astype(jnp.float32)
        first_sum = early_grads[:, tokens:].astype(jnp.float32) + swap[:, tokens:].astype(jnp.float32)
        folded = jnp.pad(jnp.where(run == 2, first_sum, 0.0), ((0, 0), (0, tokens - BLK), (0, 0)))
        to_before, to_after, _ = lax.optimization_barrier((to_before, to_after, weight_turns))
        to_before = to_before.astype(jnp.float32) + jnp.where(side == 1, diagonal, 0.0) + folded
        to_after = to_after.astype(jnp.float32) + jnp.where(side == 0, diagonal, 0.0)
        back_pair = swapped(to_beside, range(length))
        to_before, to_after = to_before.astype(jnp.bfloat16), to_after.astype(jnp.bfloat16)
        to_before, to_after, near, last_part = lax.optimization_barrier(
            (to_before, to_after, first_sum.astype(jnp.bfloat16), weight_parts[1])
        )
        back_down = shifted(to_before, -2)
        back_up = shifted(to_after, 2)
        scattered = tied(scattered, back_pair)
        mine, theirs = scattered[:tokens], swapped(scattered[tokens:], range(length))
        attended = jnp.where(
            side == 0, jnp.concatenate([mine, theirs], axis=1), jnp.concatenate([theirs, mine], axis=1)
        )
        weight_grad = own_part
        for part in weight_turns + [turned(last_part, 2, length)]:
            weight_grad = weight_grad + part.astype(jnp.float32)
        for c in range(length, ctx, 2):
            got = tied(lax.ppermute(near, "ctx", [(c, 0)]), back_down, back_up, attended)
            first_sum = first_sum + got.astype(jnp.float32)
        wide = pl.BlockSpec((2, BLK, features), lambda n: (0, n, 0))
        top = pl.BlockSpec((2, BLK, features), lambda n: (0, 0, 0))
        slab = pl.BlockSpec((BLK, features), lambda n: (n, 0))
        key_grad, value_grad = pl.pallas_call(
            functools.partial(finish_kernel, scale),
            grid=(per_dev,),
            in_specs=[smem] + [wide] * 4 + [top],
            out_specs=[slab, slab],
            out_shape=[jax.ShapeDtypeStruct((tokens, features), jnp.bfloat16)] * 2,
            cost_estimate=CHEAP,
            name="finish",
        )(run_word, own, back_pair, back_down, back_up, first_sum)

    else:
        first_sum = to_first(early_grads.astype(jnp.float32))
        sums = own
        for o, part in zip(offsets, results[2:]):
            sums = sums + shifted(part, o).astype(jnp.float32)
        first_sum = jnp.where(run == 0, first_sum, 0.0)
        sums = sums + jnp.pad(first_sum, ((0, 0), (0, tokens - BLK), (0, 0)))
        key_grad = (sums[0] * scale).astype(jnp.bfloat16)
        value_grad = sums[1].astype(jnp.bfloat16)
    if not direct:
        weight_grad = mm(grad_rows, mixed_all, TN)
    return (attended, query_grad, key_grad, value_grad, weight_grad)


def solution(mesh):
    spec = P("ctx", "head")
    return jax.shard_map(
        local,
        mesh=mesh,
        in_specs=(spec, spec, spec, spec, P(), spec),
        out_specs=(spec,) * 5,
        check_vma=False,
    )
```

```python
import functools

import jax
import jax.numpy as jnp
from jax import lax
from jax.experimental import pallas as pl
from jax.experimental.pallas import tpu as pltpu
from jax.sharding import PartitionSpec as P

HD = 128
BLK = 128
REACH = 4

CHEAP = pl.CostEstimate(flops=1, bytes_accessed=1, transcendentals=0)

NT = (((1,), (1,)), ((), ()))
TN = (((0,), (0,)), ((), ()))
NN = (((1,), (0,)), ((), ()))


def mm(a, b, dims):
    return lax.dot_general(a, b, dims, preferred_element_type=jnp.float32)


def shifted(x, by):
    peers = lax.axis_size("ctx")
    return lax.ppermute(x, "ctx", [(i, i + by) for i in range(peers) if 0 <= i + by < peers])


def tree_strides(peers):
    strides = []
    stride = 1
    while stride < peers:
        strides.append(stride)
        stride *= 2
    return strides


def from_first(x):
    peers = lax.axis_size("ctx")
    me = lax.axis_index("ctx")
    for stride in reversed(tree_strides(peers)):
        pairs = [(i, i + stride) for i in range(0, peers, 2 * stride) if i + stride < peers]
        got = lax.ppermute(x, "ctx", pairs)
        x = jnp.where(me % (2 * stride) == stride, got, x)
    return x


def to_first(x):
    peers = lax.axis_size("ctx")
    for stride in tree_strides(peers):
        pairs = [(i + stride, i) for i in range(0, peers, 2 * stride) if i + stride < peers]
        x = x + lax.ppermute(x.astype(jnp.bfloat16), "ctx", pairs).astype(x.dtype)
    return x


def turned(x, by, length):
    return lax.ppermute(x, "ctx", [(2 * z + n, 2 * ((z + by) % length) + n) for z in range(length) for n in range(2)])


def swapped(piece, places):
    return lax.ppermute(piece, "ctx", [(2 * z + n, 2 * z + 1 - n) for z in places for n in range(2)])


def tied(x, *others):
    return lax.optimization_barrier((x,) + others)[0]


def start_weights(pieces, held_ref, sems):
    place = lax.div(lax.axis_index("ctx"), 2)
    own, beside, middle, outer, far, farthest = pieces
    low = place < 2
    inner = (place == 1) | (place == 2)

    def send(piece, slot):
        pltpu.make_async_copy(piece, held_ref.at[slot], sems.at[slot]).start()

    send(own, place)
    send(beside, place + 1 - 2 * lax.rem(place, 2))

    @pl.when(inner)
    def _():
        send(middle, 3 - place)
        send(far, jnp.where(low, 3, 0))

    @pl.when(jnp.logical_not(inner))
    def _():
        send(outer, jnp.where(low, 2, 1))
        send(farthest, 3 - place)


def weight_at(held_ref, sems, b):
    pltpu.make_async_copy(held_ref.at[b], held_ref.at[b], sems.at[b]).wait()
    return held_ref[b]


def grads_kernel(length, rows_ref, *rest):
    pieces = rest[:6]
    grad_ref, other_ref, held_ref, sems = rest[6:]
    tokens = grad_ref.shape[0]
    width = rows_ref.shape[1] // length
    start_weights(pieces, held_ref, sems)
    total = None
    for b in range(length):
        part = mm(rows_ref[:, b * width : (b + 1) * width], weight_at(held_ref, sems, b), NN)
        total = part if total is None else total + part
    grad_ref[...] = total[:tokens]
    other_ref[...] = total[tokens:].astype(jnp.bfloat16)


def outs_kernel(length, mixed_ref, other_ref, *rest):
    pieces = rest[:6]
    out_ref, held_ref, sems = rest[6:]
    tokens = mixed_ref.shape[0]
    width = out_ref.shape[1] // length
    start_weights(pieces, held_ref, sems)
    for b in range(length):
        weight = weight_at(held_ref, sems, b)
        columns = slice(b * width, (b + 1) * width)
        out_ref[:tokens, columns] = mm(mixed_ref[...], weight, NT).astype(jnp.bfloat16)
        out_ref[tokens:, columns] = mm(other_ref[...], weight, NT).astype(jnp.bfloat16)


def weight_kernel(length, rows_ref, mixed_ref, other_ref, own_ref, *rest):
    sends = rest[: length - 1]
    (both_ref,) = rest[length - 1 :]
    width = own_ref.shape[0]
    tokens = mixed_ref.shape[0]
    place = lax.div(lax.axis_index("ctx"), 2)
    both_ref[:tokens, :] = mixed_ref[...]
    both_ref[tokens:, :] = other_ref[...]
    for n, out_ref in enumerate((own_ref,) + sends):
        column = pl.multiple_of(lax.rem(place + n, length) * width, 128)
        out_ref[...] = mm(rows_ref[:, pl.ds(column, width)], both_ref[...], TN).astype(out_ref.dtype)


def finish_kernel(scale, run_ref, own_ref, a_ref, b_ref, c_ref, first_ref, *rest):
    key_ref, value_ref = rest[-2:]
    there = jnp.where((run_ref[0] == 0) & (pl.program_id(0) == 0), 1.0, 0.0).astype(jnp.float32)
    for n, out_ref in enumerate((key_ref, value_ref)):
        total = own_ref[n] + a_ref[n].astype(jnp.float32) + b_ref[n].astype(jnp.float32) + c_ref[n].astype(jnp.float32)
        head = first_ref[n]
        for ref in rest[:-2]:
            head = head + ref[n].astype(jnp.float32)
        total = total + there * head
        out_ref[...] = (total * (scale if n == 0 else 1.0)).astype(jnp.bfloat16)


def runs_away(offset, run):
    side = lax.rem(run, 2)
    if offset == "pair":
        return 1 - 2 * side
    if offset == "across":
        return 2 * side - 1
    return offset


def block_bias(lists_ref, run, per_dev, total_blocks, offset, i, j):
    row = run * per_dev + i
    key = (run + runs_away(offset, run)) * per_dev + j
    hit = (key - row <= 1) & (row - key <= 1)
    for n in range(lists_ref.shape[1]):
        hit = hit | (lists_ref[row, n] == key)
    hit = hit & (key >= 1) & (key < total_blocks)
    return jnp.where(hit, 0.0, -jnp.inf).astype(jnp.float32)


def fwd_kernel(offsets, per_dev, scale, run_ref, lists_ref, q_ref, k_ref, v_ref, *rest):
    bands = rest[: len(offsets)]
    first_ref, mixed_ref, lse_ref, s_ref = rest[len(offsets) :]
    total_blocks = lists_ref.shape[0]
    run = run_ref[0]
    q = q_ref[...]
    tokens = q.shape[0]

    def key_of(p):
        return k_ref[...] if p == 0 else bands[p - 1][0]

    def value_of(p):
        return v_ref[...] if p == 0 else bands[p - 1][1]

    places = (0,) + offsets
    top = None
    for p, offset in enumerate(places):
        s = mm(key_of(p), q, NT) * scale
        for j in range(per_dev):
            for i in range(per_dev):
                part = s[j * BLK : (j + 1) * BLK, i * BLK : (i + 1) * BLK]
                part = part + block_bias(lists_ref, run, per_dev, total_blocks, offset, i, j)
                s_ref[p * tokens + j * BLK : p * tokens + (j + 1) * BLK, i * BLK : (i + 1) * BLK] = part
    s_ref[len(places) * tokens :, :] = mm(first_ref[0], q, NT) * scale
    s = s_ref[...]
    top = jnp.max(s, axis=0, keepdims=True)
    e = jnp.exp(s - top)
    total = jnp.sum(e, axis=0, keepdims=True)
    inverse = 1.0 / total
    low = (e * inverse).astype(jnp.bfloat16)
    out = mm(first_ref[1], low[len(places) * tokens :], TN)
    for p in range(len(places)):
        out = out + mm(value_of(p), low[p * tokens : (p + 1) * tokens], TN)
    mixed_ref[...] = out.T.astype(jnp.bfloat16)
    lse_ref[0] = top + jnp.log(total)


def probs_of(lists_ref, s_ref, run, per_dev, s, offset, lse):
    if offset is None:
        return jnp.exp(s - lse)
    for j in range(per_dev):
        for i in range(per_dev):
            part = s[j * BLK : (j + 1) * BLK, i * BLK : (i + 1) * BLK]
            part = part + block_bias(lists_ref, run, per_dev, lists_ref.shape[0], offset, i, j)
            s_ref[j * BLK : (j + 1) * BLK, i * BLK : (i + 1) * BLK] = part
    return jnp.exp(s_ref[...] - lse)


def first_kernel(offsets, per_dev, scale, run_ref, lists_ref, q_ref, *rest):
    bands = rest[: len(offsets)]
    first_ref, mixed_ref, grad_ref, lse_ref, out_ref, s_ref = rest[len(offsets) :]
    q = q_ref[...]
    grad = grad_ref[...]
    lse = lse_ref[0]
    product = grad.astype(jnp.float32) * mixed_ref[...].astype(jnp.float32)
    delta = jnp.sum(product.T, axis=0, keepdims=True)
    at = 0
    for n, (offset, pair_ref) in enumerate(zip(tuple(offsets) + (None,), bands + (first_ref,))):
        p = probs_of(lists_ref, s_ref.at[n], run_ref[0], per_dev, mm(pair_ref[0], q, NT) * scale, offset, lse)
        slopes = (p * (mm(pair_ref[1], grad, NT) - delta)).astype(jnp.bfloat16)
        rows = slice(at, at + pair_ref.shape[1])
        at = rows.stop
        out_ref[0, rows, :] = mm(slopes, q, NN).astype(jnp.bfloat16)
        out_ref[1, rows, :] = mm(p.astype(jnp.bfloat16), grad, NN).astype(jnp.bfloat16)


def bwd_kernel(offsets, early, per_dev, scale, run_ref, lists_ref, q_ref, k_ref, v_ref, *rest):
    bands = rest[: len(offsets)]
    first_ref, mixed_ref, grad_ref, lse_ref = rest[len(offsets) : len(offsets) + 4]
    outs = rest[len(offsets) + 4 :]
    dq_ref, own_ref = outs[:2]
    band_outs = list(outs[2:-1])
    s_ref = outs[-1]
    q = q_ref[...]
    grad = grad_ref[...]
    lse = lse_ref[0]
    product = grad.astype(jnp.float32) * mixed_ref[...].astype(jnp.float32)
    delta = jnp.sum(product.T, axis=0, keepdims=True)
    dq = None
    plan = [(None, first_ref[0], first_ref[1], None)]
    for offset, pair_ref in zip(offsets, bands):
        plan.append((offset, pair_ref[0], pair_ref[1], None if offset in early else band_outs.pop(0)))
    plan.append((0, k_ref[...], v_ref[...], own_ref))
    for n, (offset, key, value, out_ref) in enumerate(plan):
        p = probs_of(lists_ref, s_ref.at[n], run_ref[0], per_dev, mm(key, q, NT) * scale, offset, lse)
        slopes = (p * (mm(value, grad, NT) - delta)).astype(jnp.bfloat16)
        more = mm(key, slopes, TN)
        dq = more if dq is None else dq + more
        if out_ref is not None:
            out_ref[0] = mm(slopes, q, NN).astype(out_ref.dtype)
            out_ref[1] = mm(p.astype(jnp.bfloat16), grad, NN).astype(out_ref.dtype)
    dq_ref[...] = (dq * scale).T.astype(jnp.bfloat16)


def local(queries, key_heads, value_heads, out_weight, block_lists, out_grad):
    scale = HD ** (-0.5)
    tokens, features = queries.shape
    groups = features // HD
    per_dev = tokens // BLK
    ctx = lax.axis_size("ctx")
    head = lax.axis_size("head")
    run = lax.axis_index("ctx")
    column = lax.axis_index("head")
    reach = -(-REACH // per_dev)
    length = ctx // 2
    direct = ctx == 8 and head == length and reach == 2 and out_grad.shape[1] == 2 * features
    place = run // 2
    side = run % 2
    if direct:
        offsets, early = (-2, 2, "pair", "across"), ("across",)
    else:
        offsets, early = tuple(o for o in range(-reach, reach + 1) if o != 0), ()
    places = 1 + len(offsets)
    smem = pl.BlockSpec(memory_space=pltpu.SMEM)
    whole = pl.BlockSpec(memory_space=pltpu.VMEM)
    anywhere = pl.BlockSpec(memory_space=pl.ANY)
    width = out_weight.shape[0]

    both = jnp.stack([key_heads, value_heads])
    head_rows = both[:, :BLK]
    if direct:
        half = out_grad.shape[1] // 2
        own_half = lax.dynamic_slice_in_dim(out_grad, side * half, half, 1)
        other_half = lax.dynamic_slice_in_dim(out_grad, (1 - side) * half, half, 1)
        before, after = shifted(both, 2), shifted(both, -2)
        beside = swapped(jnp.concatenate([both, other_half[None]], axis=0), range(length))
        grad_side = lax.all_gather(jnp.concatenate([own_half, tied(beside[2], before, after)], axis=0), "head", axis=1, tiled=True)
        sent = jnp.where(side == 0, after, before)
        hop = [(2 * z, 2 * z + 1) for z in range(length - 1)] + [(2 * z + 1, 2 * z) for z in range(1, length)]
        across = lax.ppermute(sent, "ctx", hop)
        known = jnp.where(run == 1, beside[:2, :BLK], head_rows)
        known = jnp.where(run == 2, before[:, :BLK], known)
        middle_rows = lax.ppermute(head_rows, "ctx", [(0, length)])
        known = jnp.where(run == length, middle_rows, known)
        late = lax.ppermute(known, "ctx", [(1, 7), (0, 3), (4, 5), (2, 6)])
        first = jnp.where((run == 3) | (run > length), late, known)

        def between(x, places):
            return lax.ppermute(x, "ctx", [(2 * a + n, 2 * b + n) for a, b in places for n in range(2)])

        base = tied(out_weight, before, after, middle_rows)
        near = between(base, ((0, 1), (1, 0), (2, 3), (3, 2)))
        middle = between(base, ((1, 2), (2, 1)))
        far = between(near, ((1, 2), (2, 1)))
        outer = between(middle, ((1, 0), (2, 3)))
        farthest = between(far, ((1, 0), (2, 3)))
        weight_pieces = [base, near, middle, outer, far, farthest]
        bands = [before, after, beside, across]
    else:
        bands = [shifted(both, -o) for o in offsets]
        first = from_first(head_rows)
        grad_full = lax.all_gather(out_grad, "head", axis=1, tiled=True)
        full_weight = lax.all_gather(out_weight, "ctx", axis=0, tiled=True)
        rounds = ctx // head
        mine = jnp.zeros((rounds * tokens, width), jnp.bfloat16)
        for r in range(rounds):
            pairs = []
            for c in range(ctx):
                for h in range(head):
                    pairs.append((c * head + h, (rounds * h + (c + r) % rounds) * head + c // rounds))
            sent = lax.dynamic_slice_in_dim(out_grad, ((run + r) % rounds) * width, width, 1)
            got = lax.ppermute(sent, ("ctx", "head"), pairs)
            mine = lax.dynamic_update_slice_in_dim(mine, got, ((run - r) % rounds) * tokens, 0)
        grad_rows = lax.all_gather(mine, "head", axis=0, tiled=True)

    run_word = run.astype(jnp.int32).reshape(1)
    flat = pl.BlockSpec((tokens, HD), lambda h: (0, h))
    pair = pl.BlockSpec((2, tokens, HD), lambda h: (0, 0, h))
    head_pair = pl.BlockSpec((2, BLK, HD), lambda h: (0, 0, h))
    row = pl.BlockSpec((1, 1, tokens), lambda h: (h, 0, 0))
    keys = places * tokens + BLK
    mixed, lse = pl.pallas_call(
        functools.partial(fwd_kernel, offsets, per_dev, scale),
        grid=(groups,),
        in_specs=[smem, smem, flat, flat, flat] + [pair] * len(offsets) + [head_pair],
        out_specs=[flat, row],
        out_shape=[
            jax.ShapeDtypeStruct((tokens, features), jnp.bfloat16),
            jax.ShapeDtypeStruct((groups, 1, tokens), jnp.float32),
        ],
        scratch_shapes=[pltpu.VMEM((keys, tokens), jnp.float32)],
        compiler_params=pltpu.CompilerParams(vmem_limit_bytes=40 * 1024 * 1024),
        cost_estimate=CHEAP,
        name="attend",
    )(run_word, block_lists, queries, key_heads, value_heads, *bands, first)

    if direct:
        held = [pltpu.VMEM((length, width, features), jnp.bfloat16), pltpu.SemaphoreType.DMA((length,))]
        own_grad, other_grad = pl.pallas_call(
            functools.partial(grads_kernel, length),
            in_specs=[whole] + [anywhere] * 6,
            out_specs=[whole] * 2,
            out_shape=[
                jax.ShapeDtypeStruct((tokens, features), jnp.float32),
                jax.ShapeDtypeStruct((tokens, features), jnp.bfloat16),
            ],
            scratch_shapes=held,
            compiler_params=pltpu.CompilerParams(vmem_limit_bytes=32 * 1024 * 1024),
            cost_estimate=CHEAP,
            name="project_grad",
        )(grad_side, *weight_pieces)
        mixed_grad = (own_grad + swapped(other_grad, range(length)).astype(jnp.float32)).astype(jnp.bfloat16)
        mixed_other = tied(swapped(mixed, range(length)), other_grad)
        own_part, *weight_parts = pl.pallas_call(
            functools.partial(weight_kernel, length),
            in_specs=[whole] + [whole] * 2,
            out_specs=[whole] * length,
            out_shape=[jax.ShapeDtypeStruct((width, features), jnp.float32)]
            + [jax.ShapeDtypeStruct((width, features), jnp.bfloat16)] * (length - 1),
            scratch_shapes=[pltpu.VMEM((2 * tokens, features), jnp.bfloat16)],
            compiler_params=pltpu.CompilerParams(vmem_limit_bytes=32 * 1024 * 1024),
            cost_estimate=CHEAP,
            name="weight_part",
        )(grad_side, mixed, mixed_other)
        partial_out = pl.pallas_call(
            functools.partial(outs_kernel, length),
            in_specs=[whole] * 2 + [anywhere] * 6,
            out_specs=pl.BlockSpec((2 * tokens, length * width), lambda: (0, 0)),
            out_shape=jax.ShapeDtypeStruct((2 * tokens, length * width), jnp.bfloat16),
            scratch_shapes=held,
            compiler_params=pltpu.CompilerParams(vmem_limit_bytes=32 * 1024 * 1024),
            cost_estimate=CHEAP,
            name="project_out",
        )(mixed, tied(mixed_other, own_part), *weight_pieces)
        scattered = lax.psum_scatter(partial_out, "head", scatter_dimension=1, tiled=True)
        mixed_grad = tied(mixed_grad, own_part)
        weight_turns = [turned(weight_parts[n - 1], n, length) for n in (1, 3)]
    else:
        partial_out = mm(mixed, full_weight, NT).astype(jnp.bfloat16)
        mixed_grad = mm(grad_full, full_weight, NN).astype(jnp.bfloat16)
        mixed_all = lax.all_gather(mixed, "ctx", axis=0, tiled=True)
        attended = lax.psum_scatter(partial_out, "head", scatter_dimension=1, tiled=True)
    early_bands = [band for o, band in zip(offsets, bands) if o in early]
    early_rows = len(early) * tokens + BLK
    early_grads = pl.pallas_call(
        functools.partial(first_kernel, early, per_dev, scale),
        grid=(groups,),
        in_specs=[smem, smem, flat] + [pair] * len(early) + [head_pair, flat, flat, row],
        out_specs=pl.BlockSpec((2, early_rows, HD), lambda h: (0, 0, h)),
        out_shape=jax.ShapeDtypeStruct((2, early_rows, features), jnp.bfloat16),
        scratch_shapes=[pltpu.VMEM((1 + len(early), tokens, tokens), jnp.float32)],
        compiler_params=pltpu.CompilerParams(vmem_limit_bytes=32 * 1024 * 1024),
        cost_estimate=pl.CostEstimate(flops=10_000_000_000, bytes_accessed=1, transcendentals=0),
        name="first_grad",
    )(run_word, block_lists, queries, *early_bands, first, mixed, mixed_grad, lse)

    lse_later = tied(lse, early_grads, partial_out)
    results = pl.pallas_call(
        functools.partial(bwd_kernel, offsets, early, per_dev, scale),
        grid=(groups,),
        in_specs=[smem, smem, flat, flat, flat] + [pair] * len(offsets) + [head_pair, flat, flat, row],
        out_specs=[flat, pair] + [pair] * (len(offsets) - len(early)),
        out_shape=[
            jax.ShapeDtypeStruct((tokens, features), jnp.bfloat16),
            jax.ShapeDtypeStruct((2, tokens, features), jnp.float32),
        ]
        + [jax.ShapeDtypeStruct((2, tokens, features), jnp.bfloat16)] * (len(offsets) - len(early)),
        scratch_shapes=[pltpu.VMEM((1 + places, tokens, tokens), jnp.float32)],
        compiler_params=pltpu.CompilerParams(vmem_limit_bytes=40 * 1024 * 1024),
        cost_estimate=pl.CostEstimate(flops=30_000_000_000, bytes_accessed=1, transcendentals=0),
        name="attend_grad",
    )(run_word, block_lists, queries, key_heads, value_heads, *bands, first, mixed, mixed_grad, lse_later)
    query_grad, own = results[:2]
    if direct:
        to_before, to_after, to_beside = results[2:]
        swap = tied(swapped(early_grads, range(length)), query_grad)
        diagonal = swap[:, :tokens].astype(jnp.float32)
        first_sum = early_grads[:, tokens:].astype(jnp.float32) + swap[:, tokens:].astype(jnp.float32)
        folded = jnp.pad(jnp.where(run == 2, first_sum, 0.0), ((0, 0), (0, tokens - BLK), (0, 0)))
        to_before, to_after, _ = lax.optimization_barrier((to_before, to_after, weight_turns))
        to_before = to_before.astype(jnp.float32) + jnp.where(side == 1, diagonal, 0.0) + folded
        to_after = to_after.astype(jnp.float32) + jnp.where(side == 0, diagonal, 0.0)
        back_pair = swapped(to_beside, range(length))
        to_before, to_after = to_before.astype(jnp.bfloat16), to_after.astype(jnp.bfloat16)
        to_before, to_after, near, last_part = lax.optimization_barrier(
            (to_before, to_after, first_sum.astype(jnp.bfloat16), weight_parts[1])
        )
        back_down = shifted(to_before, -2)
        back_up = shifted(to_after, 2)
        scattered = tied(scattered, back_pair)
        mine, theirs = scattered[:tokens], swapped(scattered[tokens:], range(length))
        attended = jnp.where(
            side == 0, jnp.concatenate([mine, theirs], axis=1), jnp.concatenate([theirs, mine], axis=1)
        )
        weight_grad = own_part
        for part in weight_turns + [turned(last_part, 2, length)]:
            weight_grad = weight_grad + part.astype(jnp.float32)
        near_sums = []
        for c in range(length, ctx, 2):
            got = tied(lax.ppermute(near, "ctx", [(c, 0)]), back_down, back_up, attended)
            near_sums.append(got)
        wide = pl.BlockSpec((2, BLK, features), lambda n: (0, n, 0))
        top = pl.BlockSpec((2, BLK, features), lambda n: (0, 0, 0))
        slab = pl.BlockSpec((BLK, features), lambda n: (n, 0))
        key_grad, value_grad = pl.pallas_call(
            functools.partial(finish_kernel, scale),
            grid=(per_dev,),
            in_specs=[smem] + [wide] * 4 + [top] * (1 + len(near_sums)),
            out_specs=[slab, slab],
            out_shape=[jax.ShapeDtypeStruct((tokens, features), jnp.bfloat16)] * 2,
            cost_estimate=CHEAP,
            name="finish",
        )(run_word, own, back_pair, back_down, back_up, first_sum, *near_sums)

    else:
        first_sum = to_first(early_grads.astype(jnp.float32))
        sums = own
        for o, part in zip(offsets, results[2:]):
            sums = sums + shifted(part, o).astype(jnp.float32)
        first_sum = jnp.where(run == 0, first_sum, 0.0)
        sums = sums + jnp.pad(first_sum, ((0, 0), (0, tokens - BLK), (0, 0)))
        key_grad = (sums[0] * scale).astype(jnp.bfloat16)
        value_grad = sums[1].astype(jnp.bfloat16)
    if not direct:
        weight_grad = mm(grad_rows, mixed_all, TN)
    return (attended, query_grad, key_grad, value_grad, weight_grad)


def solution(mesh):
    spec = P("ctx", "head")
    return jax.shard_map(
        local,
        mesh=mesh,
        in_specs=(spec, spec, spec, spec, P(), spec),
        out_specs=(spec,) * 5,
        check_vma=False,
    )
```

```python
import functools

import jax
import jax.numpy as jnp
from jax import lax
from jax.experimental import pallas as pl
from jax.experimental.pallas import tpu as pltpu
from jax.sharding import PartitionSpec as P

HD = 128
BLK = 128
REACH = 4

CHEAP = pl.CostEstimate(flops=1, bytes_accessed=1, transcendentals=0)

NT = (((1,), (1,)), ((), ()))
TN = (((0,), (0,)), ((), ()))
NN = (((1,), (0,)), ((), ()))


def mm(a, b, dims):
    return lax.dot_general(a, b, dims, preferred_element_type=jnp.float32)


def shifted(x, by):
    peers = lax.axis_size("ctx")
    return lax.ppermute(x, "ctx", [(i, i + by) for i in range(peers) if 0 <= i + by < peers])


def tree_strides(peers):
    strides = []
    stride = 1
    while stride < peers:
        strides.append(stride)
        stride *= 2
    return strides


def from_first(x):
    peers = lax.axis_size("ctx")
    me = lax.axis_index("ctx")
    for stride in reversed(tree_strides(peers)):
        pairs = [(i, i + stride) for i in range(0, peers, 2 * stride) if i + stride < peers]
        got = lax.ppermute(x, "ctx", pairs)
        x = jnp.where(me % (2 * stride) == stride, got, x)
    return x


def to_first(x):
    peers = lax.axis_size("ctx")
    for stride in tree_strides(peers):
        pairs = [(i + stride, i) for i in range(0, peers, 2 * stride) if i + stride < peers]
        x = x + lax.ppermute(x.astype(jnp.bfloat16), "ctx", pairs).astype(x.dtype)
    return x


def turned(x, by, length):
    return lax.ppermute(x, "ctx", [(2 * z + n, 2 * ((z + by) % length) + n) for z in range(length) for n in range(2)])


def swapped(piece, places):
    return lax.ppermute(piece, "ctx", [(2 * z + n, 2 * z + 1 - n) for z in places for n in range(2)])


def tied(x, *others):
    return lax.optimization_barrier((x,) + others)[0]


def start_weights(pieces, held_ref, sems):
    place = lax.div(lax.axis_index("ctx"), 2)
    own, beside, middle, outer, far, farthest = pieces
    low = place < 2
    inner = (place == 1) | (place == 2)

    def send(piece, slot):
        pltpu.make_async_copy(piece, held_ref.at[slot], sems.at[slot]).start()

    send(own, place)
    send(beside, place + 1 - 2 * lax.rem(place, 2))

    @pl.when(inner)
    def _():
        send(middle, 3 - place)
        send(far, jnp.where(low, 3, 0))

    @pl.when(jnp.logical_not(inner))
    def _():
        send(outer, jnp.where(low, 2, 1))
        send(farthest, 3 - place)


def weight_at(held_ref, sems, b):
    pltpu.make_async_copy(held_ref.at[b], held_ref.at[b], sems.at[b]).wait()
    return held_ref[b]


def grads_kernel(length, rows_ref, *rest):
    pieces = rest[:6]
    grad_ref, other_ref, held_ref, sems = rest[6:]
    tokens = grad_ref.shape[0]
    width = rows_ref.shape[1] // length
    start_weights(pieces, held_ref, sems)
    total = None
    for b in range(length):
        part = mm(rows_ref[:, b * width : (b + 1) * width], weight_at(held_ref, sems, b), NN)
        total = part if total is None else total + part
    grad_ref[...] = total[:tokens]
    other_ref[...] = total[tokens:].astype(jnp.bfloat16)


def outs_kernel(length, mixed_ref, other_ref, *rest):
    pieces = rest[:6]
    out_ref, held_ref, sems = rest[6:]
    tokens = mixed_ref.shape[0]
    width = out_ref.shape[1] // length
    start_weights(pieces, held_ref, sems)
    for b in range(length):
        weight = weight_at(held_ref, sems, b)
        columns = slice(b * width, (b + 1) * width)
        out_ref[:tokens, columns] = mm(mixed_ref[...], weight, NT).astype(jnp.bfloat16)
        out_ref[tokens:, columns] = mm(other_ref[...], weight, NT).astype(jnp.bfloat16)


def weight_kernel(length, rows_ref, mixed_ref, other_ref, own_ref, *rest):
    sends = rest[: length - 1]
    (both_ref,) = rest[length - 1 :]
    width = own_ref.shape[0]
    tokens = mixed_ref.shape[0]
    place = lax.div(lax.axis_index("ctx"), 2)
    both_ref[:tokens, :] = mixed_ref[...]
    both_ref[tokens:, :] = other_ref[...]
    for n, out_ref in enumerate((own_ref,) + sends):
        column = pl.multiple_of(lax.rem(place + n, length) * width, 128)
        out_ref[...] = mm(rows_ref[:, pl.ds(column, width)], both_ref[...], TN).astype(out_ref.dtype)


def finish_kernel(scale, run_ref, own_ref, a_ref, b_ref, c_ref, first_ref, *rest):
    key_ref, value_ref = rest[-2:]
    there = jnp.where((run_ref[0] == 0) & (pl.program_id(0) == 0), 1.0, 0.0).astype(jnp.float32)
    for n, out_ref in enumerate((key_ref, value_ref)):
        total = own_ref[n] + a_ref[n].astype(jnp.float32) + b_ref[n].astype(jnp.float32) + c_ref[n].astype(jnp.float32)
        head = first_ref[n]
        for ref in rest[:-2]:
            head = head + ref[n].astype(jnp.float32)
        total = total + there * head
        out_ref[...] = (total * (scale if n == 0 else 1.0)).astype(jnp.bfloat16)


def runs_away(offset, run):
    side = lax.rem(run, 2)
    if offset == "pair":
        return 1 - 2 * side
    if offset == "across":
        return 2 * side - 1
    return offset


def block_bias(lists_ref, run, per_dev, total_blocks, offset, i, j):
    row = run * per_dev + i
    key = (run + runs_away(offset, run)) * per_dev + j
    hit = (key - row <= 1) & (row - key <= 1)
    for n in range(lists_ref.shape[1]):
        hit = hit | (lists_ref[row, n] == key)
    hit = hit & (key >= 1) & (key < total_blocks)
    return jnp.where(hit, 0.0, -jnp.inf).astype(jnp.float32)


def fwd_kernel(offsets, per_dev, scale, run_ref, lists_ref, q_ref, k_ref, v_ref, *rest):
    bands = rest[: len(offsets)]
    first_ref, mixed_ref, lse_ref, s_ref = rest[len(offsets) :]
    total_blocks = lists_ref.shape[0]
    run = run_ref[0]
    q = q_ref[...]
    tokens = q.shape[0]

    def key_of(p):
        return k_ref[...] if p == 0 else bands[p - 1][0]

    def value_of(p):
        return v_ref[...] if p == 0 else bands[p - 1][1]

    places = (0,) + offsets
    top = None
    for p, offset in enumerate(places):
        s = mm(key_of(p), q, NT) * scale
        for j in range(per_dev):
            for i in range(per_dev):
                part = s[j * BLK : (j + 1) * BLK, i * BLK : (i + 1) * BLK]
                part = part + block_bias(lists_ref, run, per_dev, total_blocks, offset, i, j)
                s_ref[p * tokens + j * BLK : p * tokens + (j + 1) * BLK, i * BLK : (i + 1) * BLK] = part
    s_ref[len(places) * tokens :, :] = mm(first_ref[0], q, NT) * scale
    s = s_ref[...]
    top = jnp.max(s, axis=0, keepdims=True)
    e = jnp.exp(s - top)
    total = jnp.sum(e, axis=0, keepdims=True)
    inverse = 1.0 / total
    low = (e * inverse).astype(jnp.bfloat16)
    out = mm(first_ref[1], low[len(places) * tokens :], TN)
    for p in range(len(places)):
        out = out + mm(value_of(p), low[p * tokens : (p + 1) * tokens], TN)
    mixed_ref[...] = out.T.astype(jnp.bfloat16)
    lse_ref[0] = top + jnp.log(total)


def probs_of(lists_ref, s_ref, run, per_dev, s, offset, lse):
    if offset is None:
        return jnp.exp(s - lse)
    for j in range(per_dev):
        for i in range(per_dev):
            part = s[j * BLK : (j + 1) * BLK, i * BLK : (i + 1) * BLK]
            part = part + block_bias(lists_ref, run, per_dev, lists_ref.shape[0], offset, i, j)
            s_ref[j * BLK : (j + 1) * BLK, i * BLK : (i + 1) * BLK] = part
    return jnp.exp(s_ref[...] - lse)


def first_kernel(offsets, per_dev, scale, run_ref, lists_ref, q_ref, *rest):
    bands = rest[: len(offsets)]
    first_ref, mixed_ref, grad_ref, lse_ref, out_ref, s_ref = rest[len(offsets) :]
    q = q_ref[...]
    grad = grad_ref[...]
    lse = lse_ref[0]
    product = grad.astype(jnp.float32) * mixed_ref[...].astype(jnp.float32)
    delta = jnp.sum(product.T, axis=0, keepdims=True)
    at = 0
    for n, (offset, pair_ref) in enumerate(zip(tuple(offsets) + (None,), bands + (first_ref,))):
        p = probs_of(lists_ref, s_ref.at[n], run_ref[0], per_dev, mm(pair_ref[0], q, NT) * scale, offset, lse)
        slopes = (p * (mm(pair_ref[1], grad, NT) - delta)).astype(jnp.bfloat16)
        rows = slice(at, at + pair_ref.shape[1])
        at = rows.stop
        out_ref[0, rows, :] = mm(slopes, q, NN).astype(jnp.bfloat16)
        out_ref[1, rows, :] = mm(p.astype(jnp.bfloat16), grad, NN).astype(jnp.bfloat16)


def bwd_kernel(offsets, early, per_dev, scale, run_ref, lists_ref, q_ref, k_ref, v_ref, *rest):
    bands = rest[: len(offsets)]
    first_ref, mixed_ref, grad_ref, lse_ref = rest[len(offsets) : len(offsets) + 4]
    outs = rest[len(offsets) + 4 :]
    dq_ref, own_ref = outs[:2]
    band_outs = list(outs[2:-1])
    s_ref = outs[-1]
    q = q_ref[...]
    grad = grad_ref[...]
    lse = lse_ref[0]
    product = grad.astype(jnp.float32) * mixed_ref[...].astype(jnp.float32)
    delta = jnp.sum(product.T, axis=0, keepdims=True)
    dq = None
    plan = [(None, first_ref[0], first_ref[1], None)]
    for offset, pair_ref in zip(offsets, bands):
        plan.append((offset, pair_ref[0], pair_ref[1], None if offset in early else band_outs.pop(0)))
    plan.append((0, k_ref[...], v_ref[...], own_ref))
    for n, (offset, key, value, out_ref) in enumerate(plan):
        p = probs_of(lists_ref, s_ref.at[n], run_ref[0], per_dev, mm(key, q, NT) * scale, offset, lse)
        slopes = (p * (mm(value, grad, NT) - delta)).astype(jnp.bfloat16)
        more = mm(key, slopes, TN)
        dq = more if dq is None else dq + more
        if out_ref is not None:
            out_ref[0] = mm(slopes, q, NN).astype(out_ref.dtype)
            out_ref[1] = mm(p.astype(jnp.bfloat16), grad, NN).astype(out_ref.dtype)
    dq_ref[...] = (dq * scale).T.astype(jnp.bfloat16)


def local(queries, key_heads, value_heads, out_weight, block_lists, out_grad):
    scale = HD ** (-0.5)
    tokens, features = queries.shape
    groups = features // HD
    per_dev = tokens // BLK
    ctx = lax.axis_size("ctx")
    head = lax.axis_size("head")
    run = lax.axis_index("ctx")
    column = lax.axis_index("head")
    reach = -(-REACH // per_dev)
    length = ctx // 2
    direct = ctx == 8 and head == length and reach == 2 and out_grad.shape[1] == 2 * features
    place = run // 2
    side = run % 2
    if direct:
        offsets, early = (-2, 2, "pair", "across"), ("across",)
    else:
        offsets, early = tuple(o for o in range(-reach, reach + 1) if o != 0), ()
    places = 1 + len(offsets)
    smem = pl.BlockSpec(memory_space=pltpu.SMEM)
    whole = pl.BlockSpec(memory_space=pltpu.VMEM)
    anywhere = pl.BlockSpec(memory_space=pl.ANY)
    width = out_weight.shape[0]

    both = jnp.stack([key_heads, value_heads])
    head_rows = both[:, :BLK]
    if direct:
        half = out_grad.shape[1] // 2
        own_half = lax.dynamic_slice_in_dim(out_grad, side * half, half, 1)
        other_half = lax.dynamic_slice_in_dim(out_grad, (1 - side) * half, half, 1)
        before, after = shifted(both, 2), shifted(both, -2)
        beside = swapped(jnp.concatenate([both, other_half[None]], axis=0), range(length))
        grad_side = lax.all_gather(jnp.concatenate([own_half, tied(beside[2], before, after)], axis=0), "head", axis=1, tiled=True)
        sent = jnp.where(side == 0, after, before)
        hop = [(2 * z, 2 * z + 1) for z in range(length - 1)] + [(2 * z + 1, 2 * z) for z in range(1, length)]
        across = lax.ppermute(sent, "ctx", hop)
        known = jnp.where(run == 1, beside[:2, :BLK], head_rows)
        known = jnp.where(run == 2, before[:, :BLK], known)
        middle_rows = lax.ppermute(head_rows, "ctx", [(0, length)])
        known = jnp.where(run == length, middle_rows, known)
        late = lax.ppermute(known, "ctx", [(1, 7), (0, 3), (4, 5), (2, 6)])
        first = jnp.where((run == 3) | (run > length), late, known)

        def between(x, places):
            return lax.ppermute(x, "ctx", [(2 * a + n, 2 * b + n) for a, b in places for n in range(2)])

        base = tied(out_weight, before, after, middle_rows)
        near = between(base, ((0, 1), (1, 0), (2, 3), (3, 2)))
        middle = between(base, ((1, 2), (2, 1)))
        far = between(near, ((1, 2), (2, 1)))
        outer = between(middle, ((1, 0), (2, 3)))
        farthest = between(far, ((1, 0), (2, 3)))
        weight_pieces = [base, near, middle, outer, far, farthest]
        bands = [before, after, beside, across]
    else:
        bands = [shifted(both, -o) for o in offsets]
        first = from_first(head_rows)
        grad_full = lax.all_gather(out_grad, "head", axis=1, tiled=True)
        full_weight = lax.all_gather(out_weight, "ctx", axis=0, tiled=True)
        rounds = ctx // head
        mine = jnp.zeros((rounds * tokens, width), jnp.bfloat16)
        for r in range(rounds):
            pairs = []
            for c in range(ctx):
                for h in range(head):
                    pairs.append((c * head + h, (rounds * h + (c + r) % rounds) * head + c // rounds))
            sent = lax.dynamic_slice_in_dim(out_grad, ((run + r) % rounds) * width, width, 1)
            got = lax.ppermute(sent, ("ctx", "head"), pairs)
            mine = lax.dynamic_update_slice_in_dim(mine, got, ((run - r) % rounds) * tokens, 0)
        grad_rows = lax.all_gather(mine, "head", axis=0, tiled=True)

    run_word = run.astype(jnp.int32).reshape(1)
    flat = pl.BlockSpec((tokens, HD), lambda h: (0, h))
    pair = pl.BlockSpec((2, tokens, HD), lambda h: (0, 0, h))
    head_pair = pl.BlockSpec((2, BLK, HD), lambda h: (0, 0, h))
    row = pl.BlockSpec((1, 1, tokens), lambda h: (h, 0, 0))
    keys = places * tokens + BLK
    mixed, lse = pl.pallas_call(
        functools.partial(fwd_kernel, offsets, per_dev, scale),
        grid=(groups,),
        in_specs=[smem, smem, flat, flat, flat] + [pair] * len(offsets) + [head_pair],
        out_specs=[flat, row],
        out_shape=[
            jax.ShapeDtypeStruct((tokens, features), jnp.bfloat16),
            jax.ShapeDtypeStruct((groups, 1, tokens), jnp.float32),
        ],
        scratch_shapes=[pltpu.VMEM((keys, tokens), jnp.float32)],
        compiler_params=pltpu.CompilerParams(vmem_limit_bytes=40 * 1024 * 1024),
        cost_estimate=CHEAP,
        name="attend",
    )(run_word, block_lists, queries, key_heads, value_heads, *bands, first)

    if direct:
        held = [pltpu.VMEM((length, width, features), jnp.bfloat16), pltpu.SemaphoreType.DMA((length,))]
        own_grad, other_grad = pl.pallas_call(
            functools.partial(grads_kernel, length),
            in_specs=[whole] + [anywhere] * 6,
            out_specs=[whole] * 2,
            out_shape=[
                jax.ShapeDtypeStruct((tokens, features), jnp.float32),
                jax.ShapeDtypeStruct((tokens, features), jnp.bfloat16),
            ],
            scratch_shapes=held,
            compiler_params=pltpu.CompilerParams(vmem_limit_bytes=32 * 1024 * 1024),
            cost_estimate=CHEAP,
            name="project_grad",
        )(grad_side, *weight_pieces)
        mixed_grad = (own_grad + swapped(other_grad, range(length)).astype(jnp.float32)).astype(jnp.bfloat16)
        mixed_other = tied(swapped(mixed, range(length)), other_grad)
        own_part, *weight_parts = pl.pallas_call(
            functools.partial(weight_kernel, length),
            in_specs=[whole] + [whole] * 2,
            out_specs=[whole] * length,
            out_shape=[jax.ShapeDtypeStruct((width, features), jnp.float32)]
            + [jax.ShapeDtypeStruct((width, features), jnp.bfloat16)] * (length - 1),
            scratch_shapes=[pltpu.VMEM((2 * tokens, features), jnp.bfloat16)],
            compiler_params=pltpu.CompilerParams(vmem_limit_bytes=32 * 1024 * 1024),
            cost_estimate=CHEAP,
            name="weight_part",
        )(grad_side, mixed, mixed_other)
        partial_out = pl.pallas_call(
            functools.partial(outs_kernel, length),
            in_specs=[whole] * 2 + [anywhere] * 6,
            out_specs=pl.BlockSpec((2 * tokens, length * width), lambda: (0, 0)),
            out_shape=jax.ShapeDtypeStruct((2 * tokens, length * width), jnp.bfloat16),
            scratch_shapes=held,
            compiler_params=pltpu.CompilerParams(vmem_limit_bytes=32 * 1024 * 1024),
            cost_estimate=CHEAP,
            name="project_out",
        )(mixed, tied(mixed_other, own_part), *weight_pieces)
        scattered = lax.psum_scatter(partial_out, "head", scatter_dimension=1, tiled=True)
        mixed_grad = tied(mixed_grad, own_part)
        weight_turns = [turned(weight_parts[n - 1], n, length) for n in (1, 3)]
    else:
        partial_out = mm(mixed, full_weight, NT).astype(jnp.bfloat16)
        mixed_grad = mm(grad_full, full_weight, NN).astype(jnp.bfloat16)
        mixed_all = lax.all_gather(mixed, "ctx", axis=0, tiled=True)
        attended = lax.psum_scatter(partial_out, "head", scatter_dimension=1, tiled=True)
    early_bands = [band for o, band in zip(offsets, bands) if o in early]
    early_rows = len(early) * tokens + BLK
    early_grads = pl.pallas_call(
        functools.partial(first_kernel, early, per_dev, scale),
        grid=(groups,),
        in_specs=[smem, smem, flat] + [pair] * len(early) + [head_pair, flat, flat, row],
        out_specs=pl.BlockSpec((2, early_rows, HD), lambda h: (0, 0, h)),
        out_shape=jax.ShapeDtypeStruct((2, early_rows, features), jnp.bfloat16),
        scratch_shapes=[pltpu.VMEM((1 + len(early), tokens, tokens), jnp.float32)],
        compiler_params=pltpu.CompilerParams(vmem_limit_bytes=32 * 1024 * 1024),
        cost_estimate=pl.CostEstimate(flops=10_000_000_000, bytes_accessed=1, transcendentals=0),
        name="first_grad",
    )(run_word, block_lists, queries, *early_bands, first, mixed, mixed_grad, lse)

    lse_later = tied(lse, early_grads, partial_out)
    results = pl.pallas_call(
        functools.partial(bwd_kernel, offsets, early, per_dev, scale),
        grid=(groups,),
        in_specs=[smem, smem, flat, flat, flat] + [pair] * len(offsets) + [head_pair, flat, flat, row],
        out_specs=[flat, pair] + [pair] * (len(offsets) - len(early)),
        out_shape=[
            jax.ShapeDtypeStruct((tokens, features), jnp.bfloat16),
            jax.ShapeDtypeStruct((2, tokens, features), jnp.float32),
        ]
        + [jax.ShapeDtypeStruct((2, tokens, features), jnp.bfloat16)] * (len(offsets) - len(early)),
        scratch_shapes=[pltpu.VMEM((1 + places, tokens, tokens), jnp.float32)],
        compiler_params=pltpu.CompilerParams(vmem_limit_bytes=40 * 1024 * 1024),
        cost_estimate=pl.CostEstimate(flops=30_000_000_000, bytes_accessed=1, transcendentals=0),
        name="attend_grad",
    )(run_word, block_lists, queries, key_heads, value_heads, *bands, first, mixed, mixed_grad, lse_later)
    query_grad, own = results[:2]
    if direct:
        to_before, to_after, to_beside = results[2:]
        swap = tied(swapped(early_grads, range(length)), query_grad)
        diagonal = swap[:, :tokens].astype(jnp.float32)
        first_sum = early_grads[:, tokens:].astype(jnp.float32) + swap[:, tokens:].astype(jnp.float32)
        folded = jnp.pad(jnp.where(run == 2, first_sum, 0.0), ((0, 0), (0, tokens - BLK), (0, 0)))
        to_before, to_after, _ = lax.optimization_barrier((to_before, to_after, weight_turns))
        to_before = to_before.astype(jnp.float32) + jnp.where(side == 1, diagonal, 0.0) + folded
        to_after = to_after.astype(jnp.float32) + jnp.where(side == 0, diagonal, 0.0)
        to_before, to_after = to_before.astype(jnp.bfloat16), to_after.astype(jnp.bfloat16)
        to_before, to_after, to_beside, near, last_part = lax.optimization_barrier(
            (to_before, to_after, to_beside, first_sum.astype(jnp.bfloat16), weight_parts[1])
        )
        back_pair = swapped(to_beside, range(length))
        back_down = shifted(to_before, -2)
        back_up = shifted(to_after, 2)
        scattered = tied(scattered, back_up)
        mine, theirs = scattered[:tokens], swapped(scattered[tokens:], range(length))
        attended = jnp.where(
            side == 0, jnp.concatenate([mine, theirs], axis=1), jnp.concatenate([theirs, mine], axis=1)
        )
        weight_grad = own_part
        for part in weight_turns + [turned(last_part, 2, length)]:
            weight_grad = weight_grad + part.astype(jnp.float32)
        near_sums = []
        for c in range(length, ctx, 2):
            got = tied(lax.ppermute(near, "ctx", [(c, 0)]), back_down, back_up, attended)
            near_sums.append(got)
        wide = pl.BlockSpec((2, BLK, features), lambda n: (0, n, 0))
        top = pl.BlockSpec((2, BLK, features), lambda n: (0, 0, 0))
        slab = pl.BlockSpec((BLK, features), lambda n: (n, 0))
        key_grad, value_grad = pl.pallas_call(
            functools.partial(finish_kernel, scale),
            grid=(per_dev,),
            in_specs=[smem] + [wide] * 4 + [top] * (1 + len(near_sums)),
            out_specs=[slab, slab],
            out_shape=[jax.ShapeDtypeStruct((tokens, features), jnp.bfloat16)] * 2,
            cost_estimate=CHEAP,
            name="finish",
        )(run_word, own, back_pair, back_down, back_up, first_sum, *near_sums)

    else:
        first_sum = to_first(early_grads.astype(jnp.float32))
        sums = own
        for o, part in zip(offsets, results[2:]):
            sums = sums + shifted(part, o).astype(jnp.float32)
        first_sum = jnp.where(run == 0, first_sum, 0.0)
        sums = sums + jnp.pad(first_sum, ((0, 0), (0, tokens - BLK), (0, 0)))
        key_grad = (sums[0] * scale).astype(jnp.bfloat16)
        value_grad = sums[1].astype(jnp.bfloat16)
    if not direct:
        weight_grad = mm(grad_rows, mixed_all, TN)
    return (attended, query_grad, key_grad, value_grad, weight_grad)


def solution(mesh):
    spec = P("ctx", "head")
    return jax.shard_map(
        local,
        mesh=mesh,
        in_specs=(spec, spec, spec, spec, P(), spec),
        out_specs=(spec,) * 5,
        check_vma=False,
    )
```
